32 devices in a mesh: seq: 16 (over z, y, x), head: 2 (over core).
Axes of the slice: x: 2, y: 2, z: 4, core: 2. Of those that a mesh axis runs over, the one named last changes fastest.
Arguments:
- block_input: bfloat16 [4, 2048, 2560], P(None, 'seq'), may hold values from -6 to 6
- norm_gain: float32 [2560], replicated, may hold values from 0.1 to 1.9
- conv_weight: float32 [4, 2560], P(None, 'head'), may hold values from -3 to 3
- conv_bias: float32 [2560], P('head'), may hold values from -3 to 3
- recur_weight: bfloat16 [10, 256, 256], P('head'), may hold values from -0.375 to 0.375
- recur_bias: float32 [2560], P('head'), may hold values from -4 to 4
- input_weight: bfloat16 [10, 256, 256], P('head'), may hold values from -0.375 to 0.375
- input_bias: float32 [2560], P('head'), may hold values from -4 to 4
- decay_param: float32 [2560], P('head'), may hold values from 5 to 12, as said below
- mlp_gain: float32 [2560], replicated, may hold values from 0.1 to 1.9
- w_gate: bfloat16 [2560, 7680], P('seq', 'head'), may hold values from -0.125 to 0.125
- w_up: bfloat16 [2560, 7680], P('seq', 'head'), may hold values from -0.125 to 0.125
- w_down: bfloat16 [2560, 7680], P('seq', 'head'), may hold values from -0.0625 to 0.0625
- out_grad: bfloat16 [4, 2048, 2560], P(None, 'seq'), may hold values from -6 to 6
Outputs:
- block_output: bfloat16 [4, 2048, 2560], P(None, 'seq')
- input_grad: float32 [4, 2048, 2560], P(None, 'seq')
- norm_gain_grad: float32 [2560], replicated
- conv_weight_grad: float32 [4, 2560], P(None, 'head')
- conv_bias_grad: float32 [2560], P('head')
- recur_weight_grad: float32 [10, 256, 256], P('head')
- recur_bias_grad: float32 [2560], P('head')
- input_weight_grad: float32 [10, 256, 256], P('head')
- input_bias_grad: float32 [2560], P('head')
- decay_param_grad: float32 [2560], P('head')
- mlp_gain_grad: float32 [2560], replicated
- w_gate_grad: float32 [2560, 7680], P('seq', 'head')
- w_up_grad: float32 [2560, 7680], P('seq', 'head')
- w_down_grad: float32 [2560, 7680], P('seq', 'head')
The draws below stay inside these ranges and needn't reach their ends.
Inputs may be any that keep to these rules, and one draw needn't show every extreme that they name: softplus(-decay_param) lies between 0.1 / 2048 and 0.006 for every channel.
All inputs are finite; a program needn't handle non-finite values.
Results may differ from the reference program's by a relative error of at most 0.0081.
Values may be sent and summed in bfloat16 or wider, within the bound.
A program may use at most 256 MiB of HBM per device.

```python
import math
import jax
import jax.numpy as jnp
from jax import lax

D = 2560
HEADS = 10
HEAD_W = 256
FF = 7680
SEQS = 4
LENGTH = 2048


def draw_decay_param(key, part):
    key = jax.random.fold_in(key, 11)
    pick_key, slow_key, fast_key = jax.random.split(key, 3)
    share = 0.5
    chooser = jax.random.uniform(pick_key, (D,), jnp.float32)
    slow_rate = jnp.exp(jax.random.uniform(slow_key, (D,), jnp.float32, math.log(0.1 / LENGTH), math.log(0.3 / LENGTH)))
    fast_rate = jnp.exp(jax.random.uniform(fast_key, (D,), jnp.float32, math.log(0.0025), math.log(0.006)))
    rate = jnp.where(chooser < share, slow_rate, fast_rate)
    return -jnp.log(jnp.expm1(rate))


def block_scale(rng, shape, cuts, least, high):
    def one(position, blocks):
        heights = jax.random.uniform(jax.random.fold_in(jax.random.fold_in(rng, 6), position), (blocks,), jnp.float32, least / len(cuts), high / len(cuts))
        return jnp.repeat(jnp.exp(heights), shape[position] // blocks).reshape((-1,) + (1,) * (len(shape) - position - 1))

    factor_of = one(*cuts[0])
    for cut in cuts[1:]:
        factor_of = factor_of * one(*cut)
    return factor_of


def centred(own_key, dims, scale, bound, pieces=(), kind=jnp.bfloat16):
    drawn = jax.random.normal(own_key, dims, jnp.float32) * scale
    if len(pieces) > 0:
        drawn = block_scale(own_key, dims, pieces, -0.22, 0.18) * drawn
    return jnp.clip(drawn, min=-bound, max=bound).astype(kind)


def setup_inputs(seed: int = 0) -> dict:
    splits = jax.random.split(jax.random.key(seed), 15)
    return {
        "block_input": centred(splits[0], (SEQS, LENGTH, D), 1.0, 6.0, ((1, 16),)),
        "norm_gain": jnp.clip(1.0 + 0.18 * jax.random.normal(splits[1], (D,), jnp.float32), 0.1, 1.9),
        "conv_weight": centred(splits[2], (4, D), 0.5, 3.0, ((1, 2),), jnp.float32),
        "conv_bias": centred(splits[3], (D,), 0.5, 3.0, ((0, 2),), jnp.float32),
        "recur_weight": centred(splits[4], (HEADS, HEAD_W, HEAD_W), HEAD_W ** -0.5, 0.375, ((0, 2),)),
        "recur_bias": centred(splits[5], (D,), 1.0, 4.0, ((0, 2),), jnp.float32),
        "input_weight": centred(splits[6], (HEADS, HEAD_W, HEAD_W), HEAD_W ** -0.5, 0.375, ((0, 2),)),
        "input_bias": centred(splits[7], (D,), 1.0, 4.0, ((0, 2),), jnp.float32),
        "decay_param": draw_decay_param(jax.random.fold_in(splits[14], 71), 0),
        "mlp_gain": jnp.clip(1.0 + 0.18 * jax.random.normal(splits[9], (D,), jnp.float32), 0.1, 1.9),
        "w_gate": centred(splits[10], (D, FF), D ** -0.5, 0.125, ((0, 16), (1, 2))),
        "w_up": centred(splits[11], (D, FF), D ** -0.5, 0.125, ((0, 16), (1, 2))),
        "w_down": centred(splits[12], (D, FF), FF ** -0.5, 0.0625, ((0, 16), (1, 2))),
        "out_grad": centred(splits[13], (SEQS, LENGTH, D), 1.0, 6.0, ((1, 16),)),
    }


EPS = 1e-06

@jax.custom_vjp
def low(v):
    return lax.optimization_barrier(v.astype(jnp.bfloat16)).astype(jnp.float32)

@jax.custom_vjp
def low_back(v):
    return v

def low_keep(v):
    return (low(v), None)

def low_pass(kept, grad):
    return (grad,)

def back_keep(v):
    return (v, None)

def back_low(kept, grad):
    return (low(grad),)
low.defvjp(low_keep, low_pass)
low_back.defvjp(back_keep, back_low)

def forward(stream, norm_gain, conv_weight, conv_bias, recur_weight, recur_bias, input_weight, input_bias, decay_param, mlp_gain, w_gate, w_up, w_down):
    group, length, width = stream.shape
    high = lax.Precision.HIGHEST
    first_hat = stream * lax.rsqrt(lax.optimization_barrier(jnp.mean(stream * stream, axis=-1, keepdims=True)) + EPS)
    xn_first = low(first_hat * norm_gain)
    padded = jnp.pad(xn_first, ((0, 0), (3, 0), (0, 0)))
    conv_sum = conv_bias + conv_weight[0] * padded[:, 3:3 + length]
    for offset in range(1, 4):
        conv_sum = conv_sum + conv_weight[offset] * padded[:, 3 - offset:3 - offset + length]
    conv_out = low_back(low(conv_sum))
    blocks = conv_out.reshape(group, length, HEADS, width // HEADS)
    recur_pre = low_back(jnp.einsum('slnh,nhk->slnk', blocks, recur_weight, precision=high).reshape(group, length, width) + recur_bias)
    input_pre = low_back(jnp.einsum('slnh,nhk->slnk', blocks, input_weight, precision=high).reshape(group, length, width) + input_bias)
    recur_gate = jax.nn.sigmoid(recur_pre)
    input_gate = jax.nn.sigmoid(input_pre)
    rate = jax.nn.softplus(-decay_param)
    log_decay = -8.0 * rate * recur_gate
    decay = jnp.exp(log_decay)
    multiplier = jnp.sqrt(-jnp.expm1(2.0 * log_decay))
    pushed = multiplier * input_gate * conv_out

    def advance(state, inputs):
        decay_step, push_step = inputs
        state = decay_step * state + push_step
        return (state, state)
    start_state = jnp.zeros((group, width), jnp.float32)
    _, states = lax.scan(advance, start_state, (jnp.swapaxes(decay, 0, 1), jnp.swapaxes(pushed, 0, 1)))
    state = jnp.swapaxes(states, 0, 1)
    residual = stream + low(state)
    second_hat = residual * lax.rsqrt(lax.optimization_barrier(jnp.mean(residual * residual, axis=-1, keepdims=True)) + EPS)
    xn_second = low(second_hat * mlp_gain).reshape(group * length, width)
    gate = low_back(jnp.dot(xn_second, w_gate, precision=high, preferred_element_type=jnp.float32))
    up_value = low_back(jnp.dot(xn_second, w_up, precision=high, preferred_element_type=jnp.float32))
    hidden = low(jax.nn.gelu(gate) * up_value)
    mixed = jnp.dot(hidden, w_down.T, precision=high, preferred_element_type=jnp.float32)
    return residual + mixed.reshape(group, length, width)

def reference(block_input, norm_gain, conv_weight, conv_bias, recur_weight, recur_bias, input_weight, input_bias, decay_param, mlp_gain, w_gate, w_up, w_down, out_grad):
    group = math.gcd(SEQS, max(1, 4096 // LENGTH))
    params = (norm_gain.astype(jnp.float32), conv_weight.astype(jnp.float32), conv_bias.astype(jnp.float32), recur_weight.astype(jnp.float32), recur_bias.astype(jnp.float32), input_weight.astype(jnp.float32), input_bias.astype(jnp.float32), decay_param.astype(jnp.float32), mlp_gain.astype(jnp.float32), w_gate.astype(jnp.float32), w_up.astype(jnp.float32), w_down.astype(jnp.float32))
    streams = block_input.astype(jnp.float32).reshape(SEQS // group, group, LENGTH, D)
    cotangents = out_grad.astype(jnp.float32).reshape(SEQS // group, group, LENGTH, D)

    def one_group(totals, inputs):
        stream, cotangent = inputs
        result, backward = jax.vjp(forward, stream, *params)
        grads = backward(cotangent)
        totals = tuple((total + grad for total, grad in zip(totals, grads[1:])))
        return (totals, (result.astype(jnp.bfloat16), grads[0]))
    zeros = tuple((jnp.zeros_like(param) for param in params))
    totals, (results, input_grads) = lax.scan(one_group, zeros, (streams, cotangents))
    return (results.reshape(SEQS, LENGTH, D), input_grads.reshape(SEQS, LENGTH, D), totals[0], totals[1], totals[2], totals[3], totals[4], totals[5], totals[6], totals[7], totals[8], totals[9], totals[10], totals[11])
```

```python
import functools
import math

import jax
import jax.numpy as jnp
from jax import lax
from jax.experimental import pallas as pl
from jax.experimental.pallas import tpu as pltpu
from jax.sharding import PartitionSpec as P

EPS = 1e-06
MESH = pl.DeviceIdType.MESH
LANES = 128
CHUNK = 256


def from_behind(value, axis, steps):
    count = lax.axis_size(axis)
    initial, last = (max(0, -steps), min(count, count - steps))
    return lax.ppermute(value, axis, [(source, source + steps) for source in range(initial, last)])


def prefix(part, axis, combine, identity, reverse):
    count = lax.axis_size(axis)
    place = lax.axis_index(axis)
    ahead = count - 1 - place if reverse else place
    gathered = jax.tree.map(lambda a: lax.all_gather(a, axis), part)
    state = jax.tree.map(lambda a, e: jnp.zeros_like(a) + jnp.asarray(e, a.dtype), part, identity)

    def one(lap, state):
        source = count - 1 - lap if reverse else lap
        return combine(
            state, jax.tree.map(lambda a: lax.dynamic_index_in_dim(a, source, 0, False), gathered)
        )

    return lax.fori_loop(0, ahead, one, state)


def norm_rows(values):
    scale = lax.rsqrt(jnp.mean(values * values, axis=-1, keepdims=True) + EPS)
    return (scale, values * scale)


def link_forward(earlier, latter):
    return (earlier[0] * latter[0], latter[0] * earlier[1] + latter[1])


def link_backward(earlier, latter):
    return (earlier[0] * latter[0], latter[1] + latter[0] * earlier[1])


def contract_last(left_side, right_side):
    return lax.dot_general(
        left_side, right_side, (((1,), (1,)), ((), ())), preferred_element_type=jnp.float32
    )


def contract_first(left_side, right_side):
    return lax.dot_general(
        left_side, right_side, (((0,), (0,)), ((), ())), preferred_element_type=jnp.float32
    )


def dot_nn(left_side, right_side):
    return jnp.dot(left_side, right_side, preferred_element_type=jnp.float32)


def remote(src, dst, send, recv, seq, head):
    return pltpu.make_async_remote_copy(
        src_ref=src, dst_ref=dst, send_sem=send, recv_sem=recv,
        device_id={"seq": seq, "head": head}, device_id_type=MESH,
    )


def ffn_kernel(
    seq_count, xn_ref, g_ref, wg_ref, wu_ref, wd_ref,
    mix_ref, gx_ref, dw_ref, dh_ref, r1_ref, e_ref, r2_ref, f_ref, sib_ref, peer_ref,
    x_all, g_all, w_all, hid, gg, gu, dv, va, vb, acc, ld,
    tok_s, tok_r, fwd_s, fwd_r, s1_s, s1_r, z_s, z_r, y_s, y_r, c1_s, c1_r, c2_s, c2_r, c3_s, c3_r,
    sib_s, sib_r, peer_s, peer_r, loc,
):
    far = seq_count // 8
    rows = wg_ref.shape[0]
    pair = 2 * rows
    tokens, half = xn_ref.shape
    span = w_all.shape[2]
    chunks = span // CHUNK
    tiles = wg_ref.shape[1] // LANES
    base, extra = tiles // 4, tiles % 4
    s = lax.axis_index("seq")
    h = lax.axis_index("head")
    x = s % 2
    y = (s // 2) % 2
    zl = (s // 4) % 2
    zh = s // 8
    a = zl * 2 + x
    weights = (wg_ref, wu_ref, wd_ref)

    def seq_of(zh_, zl_, y_, x_):
        return ((zh_ * 2 + zl_) * 2 + y_) * 2 + x_

    def peer(d):
        zl_, x_ = (zl + d // 2) % 2, (x + d % 2) % 2
        return zl_ * 2 + x_, seq_of(zh, zl_, y, x_), zl_, x_

    def first_tile(a_):
        low = base * a_ + jnp.minimum(a_, extra)
        high = base * a_ + jnp.maximum(a_ - (4 - extra), 0)
        return jnp.where(h == 0, low, high)

    def wide(zl_):
        return zl_ == h

    def block_rows(zh_, zl_, y_):
        return pl.ds(pl.multiple_of(((zh_ * 2 + zl_) * 2 + y_) * pair, 32), pair)

    def cols(c, width=CHUNK):
        return pl.ds(pl.multiple_of(c * CHUNK, CHUNK), width)

    def by_width(c, is_wide, run):
        narrow = (c == chunks - 1) & jnp.logical_not(is_wide)
        pl.when(narrow)(lambda: run(LANES))
        pl.when(jnp.logical_not(narrow))(lambda: run(CHUNK))

    y_seq = seq_of(zh, zl, 1 - y, x)

    def z_seq(q):
        return seq_of((zh + q) % far, zl, y, x)

    barrier = pltpu.get_barrier_semaphore()
    partners = [(peer(d)[1], h) for d in (1, 2, 3)] + [(s, 1 - h), (y_seq, h)]
    partners += [(z_seq(q), h) for q in range(1, far)]
    for seq, head in partners:
        pl.semaphore_signal(barrier, inc=1, device_id={"seq": seq, "head": head}, device_id_type=MESH)
    pl.semaphore_wait(barrier, len(partners))

    def s1_send(c, d, w, width):
        a_, seq, zl_, _ = peer(d)
        col = pl.multiple_of((first_tile(a_) + 2 * c) * LANES, LANES)
        return remote(
            weights[w].at[:, pl.ds(col, width)],
            w_all.at[w, pl.ds(pl.multiple_of(s * rows, 32), rows), cols(c, width)],
            s1_s.at[c, d - 1, w], s1_r.at[c, d - 1, w], seq, h,
        )

    def s1_recv(c, d, w, width):
        _, seq, _, _ = peer(d)
        return remote(
            weights[w].at[:, pl.ds(0, width)],
            w_all.at[w, pl.ds(pl.multiple_of(seq * rows, 32), rows), cols(c, width)],
            s1_s.at[c, d - 1, w], s1_r.at[c, d - 1, w], seq, h,
        )

    def s1_own(c, w, width):
        col = pl.multiple_of((first_tile(a) + 2 * c) * LANES, LANES)
        return pltpu.make_async_copy(
            weights[w].at[:, pl.ds(col, width)],
            w_all.at[w, pl.ds(pl.multiple_of(s * rows, 32), rows), cols(c, width)],
            loc.at[c, w],
        )

    def s1_start(c):
        for d in (1, 2, 3):
            def go(width, d=d):
                for w in range(3):
                    s1_send(c, d, w, width).start()
            by_width(c, wide(peer(d)[2]), go)

        def own(width):
            for w in range(3):
                s1_own(c, w, width).start()
        by_width(c, wide(zl), own)

    def s1_wait(c):
        def got(width):
            for w in range(3):
                s1_own(c, w, width).wait()
                for d in (1, 2, 3):
                    s1_recv(c, d, w, width).wait_recv()
        by_width(c, wide(zl), got)

    def s1_drain(c):
        for d in (1, 2, 3):
            def go(width, d=d):
                for w in range(3):
                    s1_send(c, d, w, width).wait_send()
            by_width(c, wide(peer(d)[2]), go)

    def z_copy(c, q, zl_, width, incoming):
        zh_ = (zh - q + far) % far if incoming else zh
        part = w_all.at[:, block_rows(zh_, zl_, y), cols(c, width)]
        return remote(part, part, z_s.at[c, q - 1, zl_], z_r.at[c, q - 1, zl_], z_seq(q), h)

    def y_copy(c, q, zl_, width, incoming):
        part = w_all.at[:, block_rows((zh - q + far) % far, zl_, 1 - y if incoming else y), cols(c, width)]
        return remote(part, part, y_s.at[c, q, zl_], y_r.at[c, q, zl_], y_seq, h)

    def z_start(c):
        def go(width):
            for q in range(1, far):
                for zl_ in range(2):
                    z_copy(c, q, zl_, width, False).start()
            for zl_ in range(2):
                y_copy(c, 0, zl_, width, False).start()
        by_width(c, wide(zl), go)

    def z_forward(c):
        def go(width):
            for q in range(1, far):
                for zl_ in range(2):
                    z_copy(c, q, zl_, width, True).wait_recv()
                    y_copy(c, q, zl_, width, False).start()
        by_width(c, wide(zl), go)

    def y_wait(c):
        def go(width):
            for q in range(far):
                for zl_ in range(2):
                    y_copy(c, q, zl_, width, True).wait_recv()
        by_width(c, wide(zl), go)

    def zy_drain(c):
        def go(width):
            for zl_ in range(2):
                for q in range(1, far):
                    z_copy(c, q, zl_, width, False).wait_send()
                for q in range(far):
                    y_copy(c, q, zl_, width, False).wait_send()
        by_width(c, wide(zl), go)

    half_cols = pl.ds(pl.multiple_of(h * half, LANES), half)

    def tok_rows(a_):
        return pl.ds(pl.multiple_of(a_ * tokens, 32), tokens)

    def tok_copy(k, d, incoming):
        src = xn_ref if k == 0 else g_ref.at[:, half_cols]
        dst = (x_all, g_all)[k]
        a_, seq, _, _ = peer(d)
        return remote(
            src, dst.at[tok_rows(a_ if incoming else a), half_cols],
            tok_s.at[k, d - 1], tok_r.at[k, d - 1], seq, h,
        )

    def fwd_copy(k, d, incoming):
        dst = (x_all, g_all)[k]
        side = pl.ds(pl.multiple_of((1 - h if incoming else h) * half, LANES), half)
        part = dst.at[tok_rows(peer(d)[0]), side]
        return remote(part, part, fwd_s.at[k, d], fwd_r.at[k, d], s, 1 - h)

    own_x = pltpu.make_async_copy(xn_ref, x_all.at[tok_rows(a), half_cols], loc.at[chunks, 0])
    own_g = pltpu.make_async_copy(g_ref, g_all.at[tok_rows(a), :], loc.at[chunks, 1])

    s1_start(0)
    for d in (1, 2, 3):
        tok_copy(1, d, False).start()
        tok_copy(0, d, False).start()
    own_x.start()
    own_g.start()
    pl.loop(1, chunks)(s1_start)

    @pl.when(jnp.logical_not(wide(zl)))
    def _():
        w_all[:, :, pl.ds(span - LANES, LANES)] = jnp.zeros((3, w_all.shape[1], LANES), jnp.bfloat16)

    @pl.loop(0, chunks)
    def _(c):
        s1_wait(c)
        z_start(c)

    z_forward(0)
    z_forward(1)
    own_x.wait()
    fwd_copy(0, 0, False).start()
    own_g.wait()
    for d in (1, 2, 3):
        for k in (1, 0):
            tok_copy(k, d, True).wait_recv()
            fwd_copy(k, d, False).start()
    fwd_copy(0, 0, True).wait_recv()
    for d in (1, 2, 3):
        for k in (1, 0):
            fwd_copy(k, d, True).wait_recv()

    def r1_copy(c, zh_, zl_, incoming):
        return remote(
            dh_ref.at[c, :, block_rows(zh_, zl_, 1 - y), :], r1_ref.at[c, :, zh_ * 2 + zl_],
            c1_s.at[c, zh_, zl_], c1_r.at[c, zh_, zl_], y_seq, h,
        )

    def r1_start(c):
        for zh_ in range(far):
            for zl_ in range(2):
                r1_copy(c, zh_, zl_, False).start()

    def r2_copy(c, q, zl_):
        return remote(
            e_ref.at[c, :, ((zh + q) % far) * 2 + zl_], r2_ref.at[c, q - 1, :, zl_],
            c2_s.at[c, q - 1, zl_], c2_r.at[c, q - 1, zl_], z_seq(q), h,
        )

    def add_into(first, second, blocks):
        @pl.loop(0, 3)
        def _(w):
            @pl.loop(0, blocks)
            def _(b):
                total = first[w, b].astype(jnp.float32) + second[w, b].astype(jnp.float32)
                first[w, b] = total.astype(jnp.bfloat16)

    def sum_near(c):
        loads = []
        for zh_ in range(far):
            for zl_ in range(2):
                loads.append(pltpu.make_async_copy(
                    dh_ref.at[c, :, block_rows(zh_, zl_, y), :], va.at[:, zh_ * 2 + zl_], loc.at[chunks + 1 + zh_, zl_]
                ))
        for load in loads:
            load.start()
        for zh_ in range(far):
            for zl_ in range(2):
                r1_copy(c, zh_, zl_, True).wait_recv()
        other = pltpu.make_async_copy(r1_ref.at[c], vb, loc.at[chunks, 2])
        other.start()
        for load in loads:
            load.wait()
        other.wait()
        add_into(va, vb, 2 * far)
        back = pltpu.make_async_copy(va, e_ref.at[c], loc.at[chunks, 2])
        back.start()
        back.wait()
        for q in range(1, far):
            for zl_ in range(2):
                r2_copy(c, q, zl_).start()

    def c3_copy(c, d, width, incoming):
        a_, seq, zl_, x_ = peer(d)
        col = pl.multiple_of((first_tile(a_ if incoming else a) + 2 * c) * LANES, LANES)
        return remote(
            f_ref.at[c, :, zl_, pl.ds(pl.multiple_of(x_ * rows, 32), rows), pl.ds(0, width)],
            dw_ref.at[:, :, pl.ds(col, width)],
            c3_s.at[c, d - 1], c3_r.at[c, d - 1], seq, h,
        )

    def c3_own(c, width):
        col = pl.multiple_of((first_tile(a) + 2 * c) * LANES, LANES)
        return pltpu.make_async_copy(
            f_ref.at[c, :, zl, pl.ds(pl.multiple_of(x * rows, 32), rows), pl.ds(0, width)],
            dw_ref.at[:, :, pl.ds(col, width)], loc.at[c, 0],
        )

    def sum_far(c):
        mine = pltpu.make_async_copy(e_ref.at[c, :, pl.ds(zh * 2, 2)], va.at[:, pl.ds(0, 2)], loc.at[chunks, 0])
        mine.start()
        mine.wait()
        for q in range(1, far):
            for zl_ in range(2):
                r2_copy(c, q, zl_).wait_recv()
            other = pltpu.make_async_copy(r2_ref.at[c, q - 1], vb.at[:, pl.ds(0, 2)], loc.at[chunks, 0])
            other.start()
            other.wait()
            add_into(va, vb, 2)
        back = pltpu.make_async_copy(va.at[:, pl.ds(0, 2)], f_ref.at[c], loc.at[chunks, 0])
        back.start()
        back.wait()

        def go(width):
            for d in (1, 2, 3):
                c3_copy(c, d, width, False).start()
            c3_own(c, width).start()
        by_width(c, wide(zl), go)

    def forward_chunk(c):
        @pl.loop(0, 4)
        def _(i):
            r = tok_rows(i)
            xb = x_all[r, :]
            gate = dot_nn(xb, w_all[0, :, cols(c)])
            up = dot_nn(xb, w_all[1, :, cols(c)])
            gh = dot_nn(g_all[r, :], w_all[2, :, cols(c)])
            k0, k1 = 0.7978845608028654, 0.044715
            th = jnp.tanh(k0 * (gate + k1 * gate * gate * gate))
            cdf = 0.5 * (1.0 + th)
            act = gate * cdf
            slope = cdf + 0.5 * gate * (1.0 - th * th) * k0 * (1.0 + 3.0 * k1 * gate * gate)
            hid[r, cols(c)] = (act * up).astype(jnp.bfloat16)
            gu[r, cols(c)] = (gh * act).astype(jnp.bfloat16)
            gg[r, cols(c)] = (gh * up * slope).astype(jnp.bfloat16)

    def weight_chunk(c):
        for w, (left, right) in enumerate(((x_all, gg), (x_all, gu), (g_all, hid))):
            @pl.loop(0, x_all.shape[1] // 512)
            def _(j):
                r = pl.ds(pl.multiple_of(j * 512, 512), 512)
                dv[w, r, :] = contract_first(left[:, r], right[:, cols(c)]).astype(jnp.bfloat16)
            pltpu.make_async_copy(dv.at[w], dh_ref.at[c, w], loc.at[chunks, w]).start()
        for w in range(3):
            pltpu.make_async_copy(dv.at[w], dh_ref.at[c, w], loc.at[chunks, w]).wait()
        r1_start(c)

    @pl.loop(0, chunks)
    def _(c):
        y_wait(c)
        forward_chunk(c)
        weight_chunk(c)
        pl.when(c + 2 < chunks)(lambda: z_forward(c + 2))
        pl.when(c >= 1)(lambda: sum_near(c - 1))
        pl.when(c >= 2)(lambda: sum_far(c - 2))

    def product(which, r, d_rows):
        if which == 0:
            return contract_last(gg[r, :], w_all[0, d_rows, :]) + contract_last(gu[r, :], w_all[1, d_rows, :])
        return contract_last(hid[r, :], w_all[2, d_rows, :])

    stage = (x_all, g_all)
    outs = (gx_ref, mix_ref)

    def sib_copy(which, k):
        r = pl.ds(pl.multiple_of(k * tokens, 32), tokens)
        return remote(
            stage[which].at[r, pl.ds(0, half)], sib_ref.at[which, k], sib_s.at[which, k], sib_r.at[which, k], s, 1 - h
        )

    def peer_copy(which, k, d):
        r = pl.ds(pl.multiple_of(k * tokens, 32), tokens)
        return remote(
            stage[which].at[r, pl.ds(half, half)], peer_ref.at[which, k], peer_s.at[which, k], peer_r.at[which, k],
            peer(d)[1], h,
        )

    steps = half // 256

    def token_sums(which):
        @pl.loop(0, 4)
        def _(k):
            d = 3 - k
            r = tok_rows(peer(d)[0])
            kr = pl.ds(pl.multiple_of(k * tokens, 32), tokens)

            @pl.loop(0, steps)
            def _(j):
                dr = pl.ds(pl.multiple_of((1 - h) * half + j * 256, 256), 256)
                stage[which][kr, pl.ds(pl.multiple_of(j * 256, 256), 256)] = product(which, r, dr).astype(jnp.bfloat16)
            sib_copy(which, k).start()

            @pl.loop(0, steps)
            def _(j):
                dr = pl.ds(pl.multiple_of(h * half + j * 256, 256), 256)
                acc[:, pl.ds(pl.multiple_of(j * 256, 256), 256)] = product(which, r, dr)
            sib_copy(which, k).wait_recv()
            load = pltpu.make_async_copy(sib_ref.at[which, k], ld, loc.at[chunks, 0])
            load.start()
            load.wait()
            acc[...] += ld[...].astype(jnp.float32)

            @pl.when(d != 0)
            def _():
                stage[which][kr, pl.ds(half, half)] = acc[...].astype(jnp.bfloat16)
                peer_copy(which, k, d).start()

    def token_finish(which):
        for k in range(3):
            peer_copy(which, k, 3 - k).wait_recv()
            load = pltpu.make_async_copy(peer_ref.at[which, k], ld, loc.at[chunks, 0])
            load.start()
            load.wait()
            acc[...] += ld[...].astype(jnp.float32)
        store = pltpu.make_async_copy(acc, outs[which], loc.at[chunks, 0])
        store.start()
        store.wait()
        for k in range(4):
            sib_copy(which, k).wait_send()
        for k in range(3):
            peer_copy(which, k, 3 - k).wait_send()

    for d in (1, 2, 3):
        for k in (0, 1):
            tok_copy(k, d, False).wait_send()
            fwd_copy(k, d, False).wait_send()
    fwd_copy(0, 0, False).wait_send()
    token_sums(0)
    token_finish(0)
    sum_near(chunks - 1)
    sum_far(chunks - 2)
    token_sums(1)
    token_finish(1)
    sum_far(chunks - 1)

    @pl.loop(0, chunks)
    def _(c):
        s1_drain(c)
        zy_drain(c)
        for zh_ in range(far):
            for zl_ in range(2):
                r1_copy(c, zh_, zl_, False).wait_send()
        for q in range(1, far):
            for zl_ in range(2):
                r2_copy(c, q, zl_).wait_send()

        def sent(width):
            for d in (1, 2, 3):
                c3_copy(c, d, width, False).wait_send()
            c3_own(c, width).wait()
        by_width(c, wide(zl), sent)
        for d in (1, 2, 3):
            by_width(c, wide(peer(d)[2]), lambda width, d=d: c3_copy(c, d, width, True).wait_recv())


def feed_forward(seq_count, xn_half, cotangent, w_gate, w_up, w_down):
    tokens, half = xn_half.shape
    width = cotangent.shape[1]
    rows, units = w_gate.shape
    pair, far = 2 * rows, seq_count // 8
    chunks = -(-units // (4 * CHUNK))
    span = chunks * CHUNK
    bf, f32 = jnp.bfloat16, jnp.float32
    any_space = pl.BlockSpec(memory_space=pl.ANY)
    outs = [
        ((tokens, half), f32), ((tokens, half), f32), ((3, rows, units), bf),
        ((chunks, 3, width, CHUNK), bf), ((chunks, 3, 2 * far, pair, CHUNK), bf), ((chunks, 3, 2 * far, pair, CHUNK), bf),
        ((chunks, far - 1, 3, 2, pair, CHUNK), bf), ((chunks, 3, 2, pair, CHUNK), bf),
        ((2, 4, tokens, half), bf), ((2, 3, tokens, half), bf),
    ]
    sem = pltpu.SemaphoreType.DMA
    scratch = [
        pltpu.VMEM((4 * tokens, width), bf), pltpu.VMEM((4 * tokens, width), bf), pltpu.VMEM((3, width, span), bf),
        pltpu.VMEM((4 * tokens, span), bf), pltpu.VMEM((4 * tokens, span), bf), pltpu.VMEM((4 * tokens, span), bf),
        pltpu.VMEM((3, width, CHUNK), bf), pltpu.VMEM((3, 2 * far, pair, CHUNK), bf), pltpu.VMEM((3, 2 * far, pair, CHUNK), bf),
        pltpu.VMEM((tokens, half), f32), pltpu.VMEM((tokens, half), bf),
    ]
    for shape in (
        (2, 3), (2, 4), (chunks, 3, 3), (chunks, far - 1, 2), (chunks, far, 2), (chunks, far, 2),
        (chunks, far - 1, 2), (chunks, 3), (2, 4), (2, 3),
    ):
        scratch += [sem(shape), sem(shape)]
    scratch.append(sem((chunks + 1 + far, 3)))
    flops = 18 * 4 * tokens * width * span
    results = pl.pallas_call(
        functools.partial(ffn_kernel, seq_count),
        out_shape=[jax.ShapeDtypeStruct(shape, kind) for shape, kind in outs],
        in_specs=[any_space] * 5,
        out_specs=[any_space] * len(outs),
        scratch_shapes=scratch,
        compiler_params=pltpu.CompilerParams(
            collective_id=0, has_side_effects=True, vmem_limit_bytes=63 * 2**20
        ),
        cost_estimate=pl.CostEstimate(flops=flops, bytes_accessed=100 * 2**20, transcendentals=4 * tokens * span),
        name="feed_forward",
    )(xn_half, cotangent, w_gate, w_up, w_down)
    return results[0], results[1], results[2]


def gathered_feed_forward(block_input, residual, xn_second, out_grad, w_gate, w_up, w_down):
    model_width = block_input.shape[2]
    token_rows = xn_second.shape[0]
    hidden_width = w_gate.shape[1]
    pieces = (
        lax.all_gather(w_gate, "seq", axis=0, tiled=True),
        lax.all_gather(w_up, "seq", axis=0, tiled=True),
    )
    columns = xn_second
    gate = jnp.dot(columns, pieces[0], preferred_element_type=jnp.float32)
    up_value = jnp.dot(columns, pieces[1], preferred_element_type=jnp.float32)
    activated, gelu_back = jax.vjp(jax.nn.gelu, gate)
    hidden = (activated * up_value).astype(jnp.bfloat16)
    partial_mix = contract_last(hidden, lax.all_gather(w_down, "seq", axis=0, tiled=True))
    mixed = lax.psum(partial_mix, "head")
    block_output = (
        (residual.reshape(token_rows, model_width) + mixed)
        .astype(jnp.bfloat16)
        .reshape(block_input.shape)
    )
    cotangent = out_grad.reshape(token_rows, model_width)
    columns = cotangent
    grad_hidden = jnp.dot(
        columns,
        lax.all_gather(w_down, "seq", axis=0, tiled=True),
        preferred_element_type=jnp.float32,
    )
    grad_gate = gelu_back(grad_hidden * up_value)[0].astype(jnp.bfloat16)
    grad_up = (grad_hidden * activated).astype(jnp.bfloat16)
    pieces = (
        lax.all_gather(w_gate, "seq", axis=0, tiled=True),
        lax.all_gather(w_up, "seq", axis=0, tiled=True),
    )
    block_value = contract_last(grad_gate, pieces[0]) + contract_last(grad_up, pieces[1])
    grad_xn_second = lax.psum(block_value, "head").reshape(block_input.shape)
    stacked = jnp.concatenate([grad_gate, grad_up], axis=1)
    local_rows = w_gate.shape[0]
    seq_count = lax.axis_size("seq")
    turns = math.gcd(local_rows, 8)
    per_turn = local_rows // turns
    input_view = xn_second.reshape(token_rows, seq_count, local_rows)
    grad_view = cotangent.reshape(token_rows, seq_count, local_rows)

    def grad_turn(turn, collected):
        first_row = turn * per_turn
        input_cols = lax.dynamic_slice_in_dim(input_view, first_row, per_turn, 2).reshape(
            token_rows, seq_count * per_turn
        )
        grad_cols = lax.dynamic_slice_in_dim(grad_view, first_row, per_turn, 2).reshape(
            token_rows, seq_count * per_turn
        )
        term = jnp.concatenate(
            [contract_first(input_cols, stacked), contract_first(grad_cols, hidden)], axis=1
        )
        share = lax.psum_scatter(term, "seq", scatter_dimension=0, tiled=True)
        return lax.dynamic_update_slice_in_dim(collected, share, first_row, 0)

    weight_grads = lax.fori_loop(
        0, turns, grad_turn, jnp.zeros((local_rows, 3 * hidden_width), jnp.float32)
    )
    w_gate_grad = weight_grads[:, :hidden_width]
    w_up_grad = weight_grads[:, hidden_width : 2 * hidden_width]
    w_down_grad = weight_grads[:, 2 * hidden_width :]
    return block_output, grad_xn_second, w_gate_grad, w_up_grad, w_down_grad


def shards(
    block_input,
    norm_gain,
    conv_weight,
    conv_bias,
    recur_weight,
    recur_bias,
    input_weight,
    input_bias,
    decay_param,
    mlp_gain,
    w_gate,
    w_up,
    w_down,
    out_grad,
):
    sequences, span_len, model_width = block_input.shape
    lru_width = conv_bias.shape[0]
    heads_here = recur_weight.shape[0]
    block_width = recur_weight.shape[1]
    token_rows = sequences * span_len
    head_at = lax.axis_index("head")
    stream = block_input.astype(jnp.float32)
    first_scale, first_hat = norm_rows(stream)
    xn_first = (first_hat * norm_gain).astype(jnp.bfloat16)
    own_input = lax.dynamic_slice_in_dim(xn_first, head_at * lru_width, lru_width, 2)
    edge_rows = from_behind(own_input[:, span_len - 3 :, :], "seq", 1)
    padded = jnp.concatenate([edge_rows, own_input], axis=1).astype(jnp.float32)
    conv_sum = conv_bias + conv_weight[0] * padded[:, 3 : 3 + span_len]
    for offset in range(1, 4):
        conv_sum = conv_sum + conv_weight[offset] * padded[:, 3 - offset : 3 - offset + span_len]
    conv_out = conv_sum.astype(jnp.bfloat16)
    conv_blocks = conv_out.reshape(token_rows, heads_here, block_width)
    recur_pre = (
        jnp.einsum(
            "tnh,nhk->tnk", conv_blocks, recur_weight, preferred_element_type=jnp.float32
        ).reshape(sequences, span_len, lru_width)
        + recur_bias
    )
    input_pre = (
        jnp.einsum(
            "tnh,nhk->tnk", conv_blocks, input_weight, preferred_element_type=jnp.float32
        ).reshape(sequences, span_len, lru_width)
        + input_bias
    )
    recur_gate = jax.nn.sigmoid(recur_pre)
    input_gate = jax.nn.sigmoid(input_pre)
    rate = jax.nn.softplus(-decay_param)
    log_decay = -8.0 * rate * recur_gate
    decay = jnp.exp(log_decay)
    multiplier = jnp.sqrt(-jnp.expm1(2.0 * log_decay))
    conv_float = conv_out.astype(jnp.float32)
    pushed = multiplier * input_gate * conv_float
    decay_prod, local_state = lax.associative_scan(link_forward, (decay, pushed), axis=1)
    ones_edge = jnp.ones((sequences, lru_width), jnp.float32)
    zeros_edge = jnp.zeros((sequences, lru_width), jnp.float32)
    entering = prefix(
        (decay_prod[:, -1], local_state[:, -1]), "seq", link_forward, (ones_edge, zeros_edge), False
    )
    state = local_state + decay_prod * entering[1][:, None, :]
    state_full = lax.all_gather(state.astype(jnp.bfloat16), "head", axis=2, tiled=True)
    residual = stream + state_full.astype(jnp.float32)
    second_scale, second_hat = norm_rows(residual)
    xn_second = (second_hat * mlp_gain).astype(jnp.bfloat16).reshape(token_rows, model_width)
    seq_count = lax.axis_size("seq")
    if seq_count % 8 == 0 and w_gate.shape[0] % 32 == 0:
        xn_half = lax.dynamic_slice_in_dim(xn_second, head_at * lru_width, lru_width, 1)
        mixed_half, grad_half, weight_grads = feed_forward(
            seq_count, xn_half, out_grad.reshape(token_rows, model_width), w_gate, w_up, w_down
        )
        mixed = lax.all_gather(mixed_half, "head", axis=1, tiled=True).reshape(block_input.shape)
        grad_xn_second = lax.all_gather(grad_half, "head", axis=1, tiled=True).reshape(block_input.shape)
        block_output = (residual + mixed).astype(jnp.bfloat16)
        w_gate_grad, w_up_grad, w_down_grad = [weight_grads[w].astype(jnp.float32) for w in range(3)]
    else:
        block_output, grad_xn_second, w_gate_grad, w_up_grad, w_down_grad = gathered_feed_forward(
            block_input, residual, xn_second, out_grad, w_gate, w_up, w_down
        )
    weighted_second = grad_xn_second * mlp_gain
    mlp_gain_local = jnp.sum(grad_xn_second * second_hat, axis=(0, 1))
    grad_residual = out_grad.astype(jnp.float32) + second_scale * (
        weighted_second
        - second_hat * jnp.mean(weighted_second * second_hat, axis=-1, keepdims=True)
    )
    grad_state = lax.dynamic_slice_in_dim(grad_residual, head_at * lru_width, lru_width, 2)
    next_decay = jnp.concatenate([decay[:, 1:], jnp.ones_like(decay[:, :1])], axis=1)
    flipped = lax.associative_scan(
        link_forward, (jnp.flip(next_decay, 1), jnp.flip(grad_state, 1)), axis=1
    )
    after_prod = jnp.flip(flipped[0], 1)
    local_adjoint = jnp.flip(flipped[1], 1)
    leaving = (decay_prod[:, -1], decay[:, 0] * local_adjoint[:, 0])
    arriving = prefix(leaving, "seq", link_backward, (ones_edge, zeros_edge), True)
    adjoint = local_adjoint + after_prod * arriving[1][:, None, :]
    previous = jnp.concatenate([entering[1][:, None, :], state[:, :-1]], axis=1)
    grad_mult = adjoint * input_gate * conv_float
    grad_log = adjoint * previous * decay - grad_mult * decay * decay / multiplier
    grad_recur_pre = (grad_log * (-8.0 * rate) * recur_gate * (1.0 - recur_gate)).astype(
        jnp.bfloat16
    )
    grad_input_pre = (adjoint * multiplier * conv_float * input_gate * (1.0 - input_gate)).astype(
        jnp.bfloat16
    )
    decay_local = jnp.sum(grad_log * 8.0 * recur_gate, axis=(0, 1)) * jax.nn.sigmoid(-decay_param)
    recur_blocks = grad_recur_pre.reshape(token_rows, heads_here, block_width)
    input_blocks = grad_input_pre.reshape(token_rows, heads_here, block_width)
    back_gates = jnp.einsum(
        "tnk,nhk->tnh", recur_blocks, recur_weight, preferred_element_type=jnp.float32
    )
    back_gates = back_gates + jnp.einsum(
        "tnk,nhk->tnh", input_blocks, input_weight, preferred_element_type=jnp.float32
    )
    grad_conv = (
        adjoint * multiplier * input_gate + back_gates.reshape(sequences, span_len, lru_width)
    ).astype(jnp.bfloat16)
    recur_weight_local = jnp.einsum(
        "tnh,tnk->nhk", conv_blocks, recur_blocks, preferred_element_type=jnp.float32
    )
    input_weight_local = jnp.einsum(
        "tnh,tnk->nhk", conv_blocks, input_blocks, preferred_element_type=jnp.float32
    )
    recur_bias_local = jnp.sum(grad_recur_pre.astype(jnp.float32), axis=(0, 1))
    input_bias_local = jnp.sum(grad_input_pre.astype(jnp.float32), axis=(0, 1))
    later_rows = from_behind(grad_conv[:, :3, :], "seq", -1)
    grad_padded = jnp.concatenate([grad_conv, later_rows], axis=1).astype(jnp.float32)
    grad_conv_float = grad_conv.astype(jnp.float32)
    grad_own_input = conv_weight[0] * grad_padded[:, 0:span_len]
    for offset in range(1, 4):
        grad_own_input = (
            grad_own_input + conv_weight[offset] * grad_padded[:, offset : offset + span_len]
        )
    conv_weight_local = jnp.stack(
        [
            jnp.sum(grad_conv_float * padded[:, 3 - offset : 3 - offset + span_len], axis=(0, 1))
            for offset in range(4)
        ]
    )
    conv_bias_local = jnp.sum(grad_conv_float, axis=(0, 1))
    grad_xn_first = lax.all_gather(
        grad_own_input.astype(jnp.bfloat16), "head", axis=2, tiled=True
    ).astype(grad_own_input.dtype)
    weighted_first = grad_xn_first * norm_gain
    norm_gain_local = jnp.sum(grad_xn_first * first_hat, axis=(0, 1))
    input_grad = grad_residual + first_scale * (
        weighted_first - first_hat * jnp.mean(weighted_first * first_hat, axis=-1, keepdims=True)
    )
    summed = lax.psum(
        (
            norm_gain_local,
            conv_weight_local,
            conv_bias_local,
            recur_weight_local,
            recur_bias_local,
            input_weight_local,
            input_bias_local,
            decay_local,
            mlp_gain_local,
        ),
        "seq",
    )
    return (
        block_output,
        input_grad,
        summed[0],
        summed[1],
        summed[2],
        summed[3],
        summed[4],
        summed[5],
        summed[6],
        summed[7],
        summed[8],
        w_gate_grad,
        w_up_grad,
        w_down_grad,
    )


def solution(mesh):
    placed = (
        P(None, "seq", None),
        P(),
        P(None, "head"),
        P("head"),
        P("head", None, None),
        P("head"),
        P("head", None, None),
        P("head"),
        P("head"),
        P(),
        P("seq", "head"),
        P("seq", "head"),
        P("seq", "head"),
        P(None, "seq", None),
    )
    return jax.shard_map(
        shards,
        mesh=mesh,
        in_specs=placed,
        out_specs=(
            P(None, "seq", None),
            P(None, "seq", None),
            P(),
            P(None, "head"),
            P("head"),
            P("head", None, None),
            P("head"),
            P("head", None, None),
            P("head"),
            P("head"),
            P(),
            P("seq", "head"),
            P("seq", "head"),
            P("seq", "head"),
        ),
        check_vma=False,
    )
```

```python
import functools
import math

import jax
import jax.numpy as jnp
from jax import lax
from jax.experimental import pallas as pl
from jax.experimental.pallas import tpu as pltpu
from jax.sharding import PartitionSpec as P

EPS = 1e-06
MESH = pl.DeviceIdType.MESH
LANES = 128
CHUNK = 256


def from_behind(value, axis, steps):
    count = lax.axis_size(axis)
    initial, last = (max(0, -steps), min(count, count - steps))
    return lax.ppermute(value, axis, [(source, source + steps) for source in range(initial, last)])


def prefix(part, axis, combine, identity, reverse):
    count = lax.axis_size(axis)
    place = lax.axis_index(axis)
    ahead = count - 1 - place if reverse else place
    gathered = jax.tree.map(lambda a: lax.all_gather(a, axis), part)
    state = jax.tree.map(lambda a, e: jnp.zeros_like(a) + jnp.asarray(e, a.dtype), part, identity)

    def one(lap, state):
        source = count - 1 - lap if reverse else lap
        return combine(
            state, jax.tree.map(lambda a: lax.dynamic_index_in_dim(a, source, 0, False), gathered)
        )

    return lax.fori_loop(0, ahead, one, state)


def norm_rows(values):
    scale = lax.rsqrt(jnp.mean(values * values, axis=-1, keepdims=True) + EPS)
    return (scale, values * scale)


def link_forward(earlier, latter):
    return (earlier[0] * latter[0], latter[0] * earlier[1] + latter[1])


def link_backward(earlier, latter):
    return (earlier[0] * latter[0], latter[1] + latter[0] * earlier[1])


def contract_last(left_side, right_side):
    return lax.dot_general(
        left_side, right_side, (((1,), (1,)), ((), ())), preferred_element_type=jnp.float32
    )


def contract_first(left_side, right_side):
    return lax.dot_general(
        left_side, right_side, (((0,), (0,)), ((), ())), preferred_element_type=jnp.float32
    )


def dot_nn(left_side, right_side):
    return jnp.dot(left_side, right_side, preferred_element_type=jnp.float32)


def remote(src, dst, send, recv, seq, head):
    return pltpu.make_async_remote_copy(
        src_ref=src, dst_ref=dst, send_sem=send, recv_sem=recv,
        device_id={"seq": seq, "head": head}, device_id_type=MESH,
    )


def ffn_kernel(
    seq_count, xn_ref, g_ref, wg_ref, wu_ref, wd_ref,
    mix_ref, gx_ref, dw_ref, dh_ref, r1_ref, e_ref, r2_ref, f_ref, sib_ref, peer_ref,
    x_all, g_all, w_all, hid, gg, gu, dv, va, vb, acc, ld,
    tok_s, tok_r, fwd_s, fwd_r, s1_s, s1_r, z_s, z_r, y_s, y_r, c1_s, c1_r, c2_s, c2_r, c3_s, c3_r,
    sib_s, sib_r, peer_s, peer_r, loc,
):
    far = seq_count // 8
    rows = wg_ref.shape[0]
    pair = 2 * rows
    tokens, half = xn_ref.shape
    span = w_all.shape[2]
    chunks = span // CHUNK
    tiles = wg_ref.shape[1] // LANES
    base, extra = tiles // 4, tiles % 4
    s = lax.axis_index("seq")
    h = lax.axis_index("head")
    x = s % 2
    y = (s // 2) % 2
    zl = (s // 4) % 2
    zh = s // 8
    a = zl * 2 + x
    weights = (wg_ref, wu_ref, wd_ref)

    def seq_of(zh_, zl_, y_, x_):
        return ((zh_ * 2 + zl_) * 2 + y_) * 2 + x_

    def peer(d):
        zl_, x_ = (zl + d // 2) % 2, (x + d % 2) % 2
        return zl_ * 2 + x_, seq_of(zh, zl_, y, x_), zl_, x_

    def first_tile(a_):
        low = base * a_ + jnp.minimum(a_, extra)
        high = base * a_ + jnp.maximum(a_ - (4 - extra), 0)
        return jnp.where(h == 0, low, high)

    def wide(zl_):
        return zl_ == h

    def block_rows(zh_, zl_, y_):
        return pl.ds(pl.multiple_of(((zh_ * 2 + zl_) * 2 + y_) * pair, 32), pair)

    def cols(c, width=CHUNK):
        return pl.ds(pl.multiple_of(c * CHUNK, CHUNK), width)

    def by_width(c, is_wide, run):
        narrow = (c == chunks - 1) & jnp.logical_not(is_wide)
        pl.when(narrow)(lambda: run(LANES))
        pl.when(jnp.logical_not(narrow))(lambda: run(CHUNK))

    y_seq = seq_of(zh, zl, 1 - y, x)

    def z_seq(q):
        return seq_of((zh + q) % far, zl, y, x)

    barrier = pltpu.get_barrier_semaphore()
    partners = [(peer(d)[1], h) for d in (1, 2, 3)] + [(s, 1 - h), (y_seq, h)]
    partners += [(z_seq(q), h) for q in range(1, far)]
    for seq, head in partners:
        pl.semaphore_signal(barrier, inc=1, device_id={"seq": seq, "head": head}, device_id_type=MESH)
    pl.semaphore_wait(barrier, len(partners))

    def s1_send(c, d, w, width):
        a_, seq, zl_, _ = peer(d)
        col = pl.multiple_of((first_tile(a_) + 2 * c) * LANES, LANES)
        return remote(
            weights[w].at[:, pl.ds(col, width)],
            w_all.at[w, pl.ds(pl.multiple_of(s * rows, 32), rows), cols(c, width)],
            s1_s.at[c, d - 1, w], s1_r.at[c, d - 1, w], seq, h,
        )

    def s1_recv(c, d, w, width):
        _, seq, _, _ = peer(d)
        return remote(
            weights[w].at[:, pl.ds(0, width)],
            w_all.at[w, pl.ds(pl.multiple_of(seq * rows, 32), rows), cols(c, width)],
            s1_s.at[c, d - 1, w], s1_r.at[c, d - 1, w], seq, h,
        )

    def s1_own(c, w, width):
        col = pl.multiple_of((first_tile(a) + 2 * c) * LANES, LANES)
        return pltpu.make_async_copy(
            weights[w].at[:, pl.ds(col, width)],
            w_all.at[w, pl.ds(pl.multiple_of(s * rows, 32), rows), cols(c, width)],
            loc.at[c, w],
        )

    def s1_start(c):
        for d in (1, 2, 3):
            def go(width, d=d):
                for w in range(3):
                    s1_send(c, d, w, width).start()
            by_width(c, wide(peer(d)[2]), go)

        def own(width):
            for w in range(3):
                s1_own(c, w, width).start()
        by_width(c, wide(zl), own)

    def s1_wait(c):
        def got(width):
            for w in range(3):
                s1_own(c, w, width).wait()
                for d in (1, 2, 3):
                    s1_recv(c, d, w, width).wait_recv()
        by_width(c, wide(zl), got)

    def s1_drain(c):
        for d in (1, 2, 3):
            def go(width, d=d):
                for w in range(3):
                    s1_send(c, d, w, width).wait_send()
            by_width(c, wide(peer(d)[2]), go)

    def z_copy(c, q, zl_, width, incoming):
        zh_ = (zh - q + far) % far if incoming else zh
        part = w_all.at[:, block_rows(zh_, zl_, y), cols(c, width)]
        return remote(part, part, z_s.at[c, q - 1, zl_], z_r.at[c, q - 1, zl_], z_seq(q), h)

    def y_copy(c, q, zl_, width, incoming):
        part = w_all.at[:, block_rows((zh - q + far) % far, zl_, 1 - y if incoming else y), cols(c, width)]
        return remote(part, part, y_s.at[c, q, zl_], y_r.at[c, q, zl_], y_seq, h)

    def z_start(c):
        def go(width):
            for q in range(1, far):
                for zl_ in range(2):
                    z_copy(c, q, zl_, width, False).start()
            for zl_ in range(2):
                y_copy(c, 0, zl_, width, False).start()
        by_width(c, wide(zl), go)

    def z_forward(c):
        def go(width):
            for q in range(1, far):
                for zl_ in range(2):
                    z_copy(c, q, zl_, width, True).wait_recv()
                    y_copy(c, q, zl_, width, False).start()
        by_width(c, wide(zl), go)

    def y_wait(c):
        def go(width):
            for q in range(far):
                for zl_ in range(2):
                    y_copy(c, q, zl_, width, True).wait_recv()
        by_width(c, wide(zl), go)

    def zy_drain(c):
        def go(width):
            for zl_ in range(2):
                for q in range(1, far):
                    z_copy(c, q, zl_, width, False).wait_send()
                for q in range(far):
                    y_copy(c, q, zl_, width, False).wait_send()
        by_width(c, wide(zl), go)

    half_cols = pl.ds(pl.multiple_of(h * half, LANES), half)

    def tok_rows(a_):
        return pl.ds(pl.multiple_of(a_ * tokens, 32), tokens)

    def tok_copy(k, d, incoming):
        src = xn_ref if k == 0 else g_ref.at[:, half_cols]
        dst = (x_all, g_all)[k]
        a_, seq, _, _ = peer(d)
        return remote(
            src, dst.at[tok_rows(a_ if incoming else a), half_cols],
            tok_s.at[k, d - 1], tok_r.at[k, d - 1], seq, h,
        )

    def fwd_copy(k, d, incoming):
        dst = (x_all, g_all)[k]
        side = pl.ds(pl.multiple_of((1 - h if incoming else h) * half, LANES), half)
        part = dst.at[tok_rows(peer(d)[0]), side]
        return remote(part, part, fwd_s.at[k, d], fwd_r.at[k, d], s, 1 - h)

    own_x = pltpu.make_async_copy(xn_ref, x_all.at[tok_rows(a), half_cols], loc.at[chunks, 0])
    own_g = pltpu.make_async_copy(g_ref, g_all.at[tok_rows(a), :], loc.at[chunks, 1])

    s1_start(0)
    for d in (1, 2, 3):
        tok_copy(1, d, False).start()
        tok_copy(0, d, False).start()
    own_x.start()
    own_g.start()
    pl.loop(1, chunks)(s1_start)

    @pl.when(jnp.logical_not(wide(zl)))
    def _():
        w_all[:, :, pl.ds(span - LANES, LANES)] = jnp.zeros((3, w_all.shape[1], LANES), jnp.bfloat16)

    @pl.loop(0, chunks)
    def _(c):
        s1_wait(c)
        z_start(c)

    z_forward(0)
    z_forward(1)
    own_x.wait()
    fwd_copy(0, 0, False).start()
    own_g.wait()
    for d in (1, 2, 3):
        for k in (1, 0):
            tok_copy(k, d, True).wait_recv()
            fwd_copy(k, d, False).start()
    fwd_copy(0, 0, True).wait_recv()
    for d in (1, 2, 3):
        for k in (1, 0):
            fwd_copy(k, d, True).wait_recv()

    def r1_copy(c, zh_, zl_, incoming):
        return remote(
            dh_ref.at[c, :, block_rows(zh_, zl_, 1 - y), :], r1_ref.at[c, :, zh_ * 2 + zl_],
            c1_s.at[c, zh_, zl_], c1_r.at[c, zh_, zl_], y_seq, h,
        )

    def r1_start(c):
        for zh_ in range(far):
            for zl_ in range(2):
                r1_copy(c, zh_, zl_, False).start()

    def r2_copy(c, q, zl_):
        return remote(
            e_ref.at[c, :, ((zh + q) % far) * 2 + zl_], r2_ref.at[c, q - 1, :, zl_],
            c2_s.at[c, q - 1, zl_], c2_r.at[c, q - 1, zl_], z_seq(q), h,
        )

    def add_into(first, second, blocks):
        @pl.loop(0, 3)
        def _(w):
            @pl.loop(0, blocks)
            def _(b):
                total = first[w, b].astype(jnp.float32) + second[w, b].astype(jnp.float32)
                first[w, b] = total.astype(jnp.bfloat16)

    def sum_near(c):
        loads = []
        for zh_ in range(far):
            for zl_ in range(2):
                loads.append(pltpu.make_async_copy(
                    dh_ref.at[c, :, block_rows(zh_, zl_, y), :], va.at[:, zh_ * 2 + zl_], loc.at[chunks + 1 + zh_, zl_]
                ))
        for load in loads:
            load.start()
        for zh_ in range(far):
            for zl_ in range(2):
                r1_copy(c, zh_, zl_, True).wait_recv()
        other = pltpu.make_async_copy(r1_ref.at[c], vb, loc.at[chunks, 2])
        other.start()
        for load in loads:
            load.wait()
        other.wait()
        add_into(va, vb, 2 * far)
        back = pltpu.make_async_copy(va, e_ref.at[c], loc.at[chunks, 2])
        back.start()
        back.wait()
        for q in range(1, far):
            for zl_ in range(2):
                r2_copy(c, q, zl_).start()

    def c3_copy(c, d, width, incoming):
        a_, seq, zl_, x_ = peer(d)
        col = pl.multiple_of((first_tile(a_ if incoming else a) + 2 * c) * LANES, LANES)
        return remote(
            f_ref.at[c, :, zl_, pl.ds(pl.multiple_of(x_ * rows, 32), rows), pl.ds(0, width)],
            dw_ref.at[:, :, pl.ds(col, width)],
            c3_s.at[c, d - 1], c3_r.at[c, d - 1], seq, h,
        )

    def c3_own(c, width):
        col = pl.multiple_of((first_tile(a) + 2 * c) * LANES, LANES)
        return pltpu.make_async_copy(
            f_ref.at[c, :, zl, pl.ds(pl.multiple_of(x * rows, 32), rows), pl.ds(0, width)],
            dw_ref.at[:, :, pl.ds(col, width)], loc.at[c, 0],
        )

    def sum_far(c):
        mine = pltpu.make_async_copy(e_ref.at[c, :, pl.ds(zh * 2, 2)], va.at[:, pl.ds(0, 2)], loc.at[chunks, 0])
        mine.start()
        mine.wait()
        for q in range(1, far):
            for zl_ in range(2):
                r2_copy(c, q, zl_).wait_recv()
            other = pltpu.make_async_copy(r2_ref.at[c, q - 1], vb.at[:, pl.ds(0, 2)], loc.at[chunks, 0])
            other.start()
            other.wait()
            add_into(va, vb, 2)
        back = pltpu.make_async_copy(va.at[:, pl.ds(0, 2)], f_ref.at[c], loc.at[chunks, 0])
        back.start()
        back.wait()

        def go(width):
            for d in (1, 2, 3):
                c3_copy(c, d, width, False).start()
            c3_own(c, width).start()
        by_width(c, wide(zl), go)

    def forward_chunk(c):
        @pl.loop(0, 4)
        def _(i):
            r = tok_rows(i)
            xb = x_all[r, :]
            gate = dot_nn(xb, w_all[0, :, cols(c)])
            up = dot_nn(xb, w_all[1, :, cols(c)])
            gh = dot_nn(g_all[r, :], w_all[2, :, cols(c)])
            k0, k1 = 0.7978845608028654, 0.044715
            th = jnp.tanh(k0 * (gate + k1 * gate * gate * gate))
            cdf = 0.5 * (1.0 + th)
            act = gate * cdf
            slope = cdf + 0.5 * gate * (1.0 - th * th) * k0 * (1.0 + 3.0 * k1 * gate * gate)
            hid[r, cols(c)] = (act * up).astype(jnp.bfloat16)
            gu[r, cols(c)] = (gh * act).astype(jnp.bfloat16)
            gg[r, cols(c)] = (gh * up * slope).astype(jnp.bfloat16)

    def weight_chunk(c):
        for w, (left, right) in enumerate(((x_all, gg), (x_all, gu), (g_all, hid))):
            @pl.loop(0, x_all.shape[1] // 512)
            def _(j):
                r = pl.ds(pl.multiple_of(j * 512, 512), 512)
                dv[w, r, :] = contract_first(left[:, r], right[:, cols(c)]).astype(jnp.bfloat16)
            pltpu.make_async_copy(dv.at[w], dh_ref.at[c, w], loc.at[chunks, w]).start()
        for w in range(3):
            pltpu.make_async_copy(dv.at[w], dh_ref.at[c, w], loc.at[chunks, w]).wait()
        r1_start(c)

    @pl.loop(0, chunks)
    def _(c):
        y_wait(c)
        forward_chunk(c)
        weight_chunk(c)
        pl.when(c + 2 < chunks)(lambda: z_forward(c + 2))
        pl.when(c >= 1)(lambda: sum_near(c - 1))
        pl.when(c >= 2)(lambda: sum_far(c - 2))

    def product(which, r, d_rows):
        if which == 0:
            return contract_last(gg[r, :], w_all[0, d_rows, :]) + contract_last(gu[r, :], w_all[1, d_rows, :])
        return contract_last(hid[r, :], w_all[2, d_rows, :])

    stage = (x_all, g_all)
    outs = (gx_ref, mix_ref)

    def sib_copy(which, k):
        r = pl.ds(pl.multiple_of(k * tokens, 32), tokens)
        return remote(
            stage[which].at[r, pl.ds(0, half)], sib_ref.at[which, k], sib_s.at[which, k], sib_r.at[which, k], s, 1 - h
        )

    def peer_copy(which, k, d):
        r = pl.ds(pl.multiple_of(k * tokens, 32), tokens)
        return remote(
            stage[which].at[r, pl.ds(half, half)], peer_ref.at[which, k], peer_s.at[which, k], peer_r.at[which, k],
            peer(d)[1], h,
        )

    steps = half // 256

    def token_sums(which):
        @pl.loop(0, 4)
        def _(k):
            d = 3 - k
            r = tok_rows(peer(d)[0])
            kr = pl.ds(pl.multiple_of(k * tokens, 32), tokens)

            @pl.loop(0, steps)
            def _(j):
                dr = pl.ds(pl.multiple_of((1 - h) * half + j * 256, 256), 256)
                stage[which][kr, pl.ds(pl.multiple_of(j * 256, 256), 256)] = product(which, r, dr).astype(jnp.bfloat16)
            sib_copy(which, k).start()

            @pl.loop(0, steps)
            def _(j):
                dr = pl.ds(pl.multiple_of(h * half + j * 256, 256), 256)
                acc[:, pl.ds(pl.multiple_of(j * 256, 256), 256)] = product(which, r, dr)
            sib_copy(which, k).wait_recv()
            load = pltpu.make_async_copy(sib_ref.at[which, k], ld, loc.at[chunks, 0])
            load.start()
            load.wait()
            acc[...] += ld[...].astype(jnp.float32)

            @pl.when(d != 0)
            def _():
                stage[which][kr, pl.ds(half, half)] = acc[...].astype(jnp.bfloat16)
                peer_copy(which, k, d).start()

    def token_finish(which):
        for k in range(3):
            peer_copy(which, k, 3 - k).wait_recv()
            load = pltpu.make_async_copy(peer_ref.at[which, k], ld, loc.at[chunks, 0])
            load.start()
            load.wait()
            acc[...] += ld[...].astype(jnp.float32)
        store = pltpu.make_async_copy(acc, outs[which], loc.at[chunks, 0])
        store.start()
        store.wait()
        for k in range(4):
            sib_copy(which, k).wait_send()
        for k in range(3):
            peer_copy(which, k, 3 - k).wait_send()

    for d in (1, 2, 3):
        for k in (0, 1):
            tok_copy(k, d, False).wait_send()
            fwd_copy(k, d, False).wait_send()
    fwd_copy(0, 0, False).wait_send()
    token_sums(0)
    token_finish(0)
    sum_near(chunks - 1)
    sum_far(chunks - 2)
    token_sums(1)
    token_finish(1)
    sum_far(chunks - 1)

    @pl.loop(0, chunks)
    def _(c):
        s1_drain(c)
        zy_drain(c)
        for zh_ in range(far):
            for zl_ in range(2):
                r1_copy(c, zh_, zl_, False).wait_send()
        for q in range(1, far):
            for zl_ in range(2):
                r2_copy(c, q, zl_).wait_send()

        def sent(width):
            for d in (1, 2, 3):
                c3_copy(c, d, width, False).wait_send()
            c3_own(c, width).wait()
        by_width(c, wide(zl), sent)
        for d in (1, 2, 3):
            by_width(c, wide(peer(d)[2]), lambda width, d=d: c3_copy(c, d, width, True).wait_recv())


def feed_forward(seq_count, xn_half, cotangent, w_gate, w_up, w_down):
    tokens, half = xn_half.shape
    width = cotangent.shape[1]
    rows, units = w_gate.shape
    pair, far = 2 * rows, seq_count // 8
    chunks = -(-units // (4 * CHUNK))
    span = chunks * CHUNK
    bf, f32 = jnp.bfloat16, jnp.float32
    any_space = pl.BlockSpec(memory_space=pl.ANY)
    outs = [
        ((tokens, half), f32), ((tokens, half), f32), ((3, rows, units), bf),
        ((chunks, 3, width, CHUNK), bf), ((chunks, 3, 2 * far, pair, CHUNK), bf), ((chunks, 3, 2 * far, pair, CHUNK), bf),
        ((chunks, far - 1, 3, 2, pair, CHUNK), bf), ((chunks, 3, 2, pair, CHUNK), bf),
        ((2, 4, tokens, half), bf), ((2, 3, tokens, half), bf),
    ]
    sem = pltpu.SemaphoreType.DMA
    scratch = [
        pltpu.VMEM((4 * tokens, width), bf), pltpu.VMEM((4 * tokens, width), bf), pltpu.VMEM((3, width, span), bf),
        pltpu.VMEM((4 * tokens, span), bf), pltpu.VMEM((4 * tokens, span), bf), pltpu.VMEM((4 * tokens, span), bf),
        pltpu.VMEM((3, width, CHUNK), bf), pltpu.VMEM((3, 2 * far, pair, CHUNK), bf), pltpu.VMEM((3, 2 * far, pair, CHUNK), bf),
        pltpu.VMEM((tokens, half), f32), pltpu.VMEM((tokens, half), bf),
    ]
    for shape in (
        (2, 3), (2, 4), (chunks, 3, 3), (chunks, far - 1, 2), (chunks, far, 2), (chunks, far, 2),
        (chunks, far - 1, 2), (chunks, 3), (2, 4), (2, 3),
    ):
        scratch += [sem(shape), sem(shape)]
    scratch.append(sem((chunks + 1 + far, 3)))
    flops = 18 * 4 * tokens * width * span
    results = pl.pallas_call(
        functools.partial(ffn_kernel, seq_count),
        out_shape=[jax.ShapeDtypeStruct(shape, kind) for shape, kind in outs],
        in_specs=[any_space] * 5,
        out_specs=[any_space] * len(outs),
        scratch_shapes=scratch,
        compiler_params=pltpu.CompilerParams(
            collective_id=0, has_side_effects=True, vmem_limit_bytes=63 * 2**20
        ),
        cost_estimate=pl.CostEstimate(flops=flops, bytes_accessed=100 * 2**20, transcendentals=4 * tokens * span),
        name="feed_forward",
    )(xn_half, cotangent, w_gate, w_up, w_down)
    return results[0], results[1], results[2]


def half_window(head, half):
    return pl.ds(pl.multiple_of(head * half, LANES), half)


def greet(partners):
    barrier = pltpu.get_barrier_semaphore()
    for seq, head in partners:
        pl.semaphore_signal(barrier, inc=1, device_id={"seq": seq, "head": head}, device_id_type=MESH)
    return barrier


def greet_all(seq_count, s, h):
    barrier = pltpu.get_barrier_semaphore()

    @pl.loop(1, seq_count)
    def _(q):
        seq = (s + q) % seq_count
        pl.semaphore_signal(barrier, inc=1, device_id={"seq": seq, "head": h}, device_id_type=MESH)

    pl.semaphore_signal(barrier, inc=1, device_id={"seq": s, "head": 1 - h}, device_id_type=MESH)
    pl.semaphore_wait(barrier, seq_count)


def one_minus_square(log_decay):
    twice = 2.0 * log_decay
    series = 1.0 + twice * (1 / 2 + twice * (1 / 6 + twice * (1 / 24 + twice * (1 / 120 + twice * (1 / 720)))))
    return jnp.where(twice > -0.25, -twice * series, 1.0 - jnp.exp(twice))


def shifted(value, step, keep, fill):
    return jnp.where(keep, pltpu.roll(value, step % 8, 0), fill)


def recur_forward_kernel(
    seq_count, sequences, x_ref, gain_ref, cw_ref, cb_ref, rw_ref, rb_ref, iw_ref, ib_ref, rate_ref, mgain_ref,
    xn2_ref, res_ref, scale_ref, state_ref, rg_ref, ig_ref, conv_ref, ext_ref,
    a_ref, b_ref, halo, ends, ent, part, part_in, halo_s, halo_r, end_s, end_r, part_s, part_r,
):
    s = lax.axis_index("seq")
    h = lax.axis_index("head")
    rows, width = x_ref.shape
    half = width // 2
    span = rows // sequences
    groups = span // 8
    mine = half_window(h, half)
    greet_all(seq_count, s, h)

    def normed(r, count):
        full = x_ref[pl.ds(r, count), :].astype(jnp.float32)
        scale = lax.rsqrt(jnp.sum(full * full, axis=1, keepdims=True) * (1.0 / width) + EPS)
        own = x_ref[pl.ds(r, count), mine].astype(jnp.float32)
        return ((own * scale) * gain_ref[:, mine]).astype(jnp.bfloat16).astype(jnp.float32)

    for q in range(sequences):
        halo[0, q] = normed(q * span + span - 16, 16)[8:]
    halo_out = remote(halo.at[0], halo.at[1], halo_s, halo_r, jnp.minimum(s + 1, seq_count - 1), h)
    pl.when(s + 1 < seq_count)(halo_out.start)
    for q in range(sequences):
        @pl.loop(0, span // 16)
        def _(i, q=q):
            r = pl.multiple_of(i * 16, 16)
            ext_ref[q, pl.ds(8 + r, 16), :] = normed(pl.multiple_of(q * span + r, 16), 16)

    @pl.when(s > 0)
    def _():
        halo_out.wait_recv()
        for q in range(sequences):
            ext_ref[q, pl.ds(0, 8), :] = halo[1, q]

    @pl.when(s == 0)
    def _():
        for q in range(sequences):
            ext_ref[q, pl.ds(0, 8), :] = jnp.zeros((8, half), jnp.float32)

    block = rw_ref.shape[1]

    @pl.loop(0, half // block)
    def _(n):
        lanes = pl.ds(pl.multiple_of(n * block, block), block)
        for q in range(sequences):
            total = cb_ref[:, lanes]
            for k in range(4):
                total = total + cw_ref[pl.ds(k, 1), lanes] * ext_ref[q, pl.ds(8 - k, span), lanes]
            conv_ref[pl.ds(q * span, span), lanes] = total.astype(jnp.bfloat16)
        low = conv_ref[:, lanes]
        rg_ref[:, lanes] = jax.nn.sigmoid(dot_nn(low, rw_ref[n]) + rb_ref[:, lanes])
        ig_ref[:, lanes] = jax.nn.sigmoid(dot_nn(low, iw_ref[n]) + ib_ref[:, lanes])

        @pl.loop(0, rows // 64)
        def _(i):
            r = pl.ds(pl.multiple_of(i * 64, 64), 64)
            log_decay = -8.0 * rate_ref[:, lanes] * rg_ref[r, lanes]
            a_ref[r, lanes] = jnp.exp(log_decay)
            mult = jnp.sqrt(one_minus_square(log_decay))
            b_ref[r, lanes] = mult * ig_ref[r, lanes] * conv_ref[r, lanes].astype(jnp.float32)

    row_ids = lax.broadcasted_iota(jnp.int32, (8, half), 0)

    def scan_group(g, carry):
        out = []
        for q in range(sequences):
            r = pl.ds(pl.multiple_of(q * span + g * 8, 8), 8)
            a, b = a_ref[r, :], b_ref[r, :]
            for k in (1, 2, 4):
                keep = row_ids >= k
                b = b + a * shifted(b, k, keep, 0.0)
                a = a * shifted(a, k, keep, 1.0)
            b = b + a * carry[2 * q]
            a = a * carry[2 * q + 1]
            a_ref[r, :] = a
            b_ref[r, :] = b
            out += [b[7:8], a[7:8]]
        return tuple(out)

    first = []
    for q in range(sequences):
        first += [jnp.zeros((1, half), jnp.float32), jnp.ones((1, half), jnp.float32)]
    last = lax.fori_loop(0, groups, scan_group, tuple(first))
    for q in range(sequences):
        part_end = pl.ds(q, 1)
        ends[s, part_end, :] = last[2 * q + 1]
        ends[s, pl.ds(sequences + q, 1), :] = last[2 * q]

    def end_copy(target, source):
        return remote(ends.at[source], ends.at[source], end_s.at[target], end_r.at[source], target, h)

    @pl.loop(1, seq_count)
    def _(q):
        pl.when(s + q < seq_count)(lambda: end_copy(s + q, s).start())

    ent[...] = jnp.zeros_like(ent)

    @pl.loop(0, seq_count)
    def _(source):
        @pl.when(source < s)
        def _():
            end_copy(s, source).wait_recv()
            got = ends[source]
            ent[...] = got[:sequences] * ent[...] + got[sequences:]

    for q in range(sequences):
        entering = ent[pl.ds(q, 1), :]
        state_ref[q, pl.ds(0, 8), :] = jnp.broadcast_to(entering, (8, half))

        @pl.loop(0, span // 16)
        def _(i, q=q, entering=entering):
            t = pl.multiple_of(i * 16, 16)
            r = pl.ds(pl.multiple_of(q * span + t, 16), 16)
            state = b_ref[r, :] + a_ref[r, :] * ent[pl.ds(q, 1), :]
            state_ref[q, pl.ds(8 + t, 16), :] = state
            residual = x_ref[r, mine].astype(jnp.float32) + state.astype(jnp.bfloat16).astype(jnp.float32)
            res_ref[r, :] = residual
            part[r, :] = jnp.broadcast_to(jnp.sum(residual * residual, axis=1, keepdims=True), (16, LANES))

    other = remote(part, part_in, part_s, part_r, s, 1 - h)
    other.start()
    other.wait_recv()

    @pl.loop(0, rows // 16)
    def _(i):
        r = pl.ds(pl.multiple_of(i * 16, 16), 16)
        scale = lax.rsqrt((part[r, :] + part_in[r, :]) * (1.0 / width) + EPS)
        scale_ref[r, :] = scale
        xn2_ref[r, :] = ((res_ref[r, :] * scale[:, :1]) * mgain_ref[:, mine]).astype(jnp.bfloat16)

    other.wait_send()
    pl.when(s + 1 < seq_count)(halo_out.wait_send)

    @pl.loop(1, seq_count)
    def _(q):
        pl.when(s + q < seq_count)(lambda: end_copy(s + q, s).wait_send())


def recur_backward_kernel(
    seq_count, sequences, gx_ref, g_ref, x_ref, res_ref, scale_ref, state_ref, rg_ref, ig_ref, conv_ref, ext_ref,
    gain_ref, cw_ref, rw_ref, iw_ref, rate_ref, sig_ref, mgain_ref,
    out_ref, vec_ref, rwg_ref, iwg_ref,
    gres, dec, adj, gconv, halo, ends, arr, part, part_in, fin,
    halo_s, halo_r, end_s, end_r, part_s, part_r, fin_s, fin_r, loc,
):
    s = lax.axis_index("seq")
    h = lax.axis_index("head")
    rows, half = gx_ref.shape
    width = 2 * half
    span = rows // sequences
    groups = span // 8
    mine = half_window(h, half)
    greet_all(seq_count, s, h)
    vec_ref[...] = jnp.zeros_like(vec_ref)
    other = [remote(part.at[i], part_in.at[i], part_s.at[i], part_r.at[i], s, 1 - h) for i in range(2)]

    @pl.loop(0, rows // 16)
    def _(i):
        r = pl.ds(pl.multiple_of(i * 16, 16), 16)
        hat = res_ref[r, :] * scale_ref[r, :1]
        product = gx_ref[r, :] * hat
        vec_ref[pl.ds(9, 1), :] += jnp.sum(product, axis=0, keepdims=True)
        part[0, r, :] = jnp.broadcast_to(jnp.sum(product * mgain_ref[:, mine], axis=1, keepdims=True), (16, LANES))

    other[0].start()
    for q in range(sequences):
        @pl.loop(0, span // 16)
        def _(i, q=q):
            t = pl.multiple_of(i * 16, 16)
            r = pl.ds(pl.multiple_of(q * span + t, 16), 16)
            dec[q, pl.ds(t, 16), :] = jnp.exp(-8.0 * rate_ref[...] * rg_ref[r, :])
    other[0].wait_recv()

    @pl.loop(0, rows // 16)
    def _(i):
        r = pl.ds(pl.multiple_of(i * 16, 16), 16)
        scale = scale_ref[r, :1]
        hat = res_ref[r, :] * scale
        mean = ((part[0, r, :] + part_in[0, r, :]) * (1.0 / width))[:, :1]
        gres[r, :] = g_ref[r, mine].astype(jnp.float32) + scale * (gx_ref[r, :] * mgain_ref[:, mine] - hat * mean)

    row_ids = lax.broadcasted_iota(jnp.int32, (8, half), 0)

    def scan_group(i, carry):
        g = groups - 1 - i
        out = []
        for q in range(sequences):
            t = pl.multiple_of(g * 8, 8)
            r = pl.ds(pl.multiple_of(q * span + t, 8), 8)
            here = dec[q, pl.ds(t, 8), :]
            a, b = shifted(here, -1, row_ids < 7, carry[3 * q + 2]), gres[r, :]
            for k in (1, 2, 4):
                keep = row_ids < 8 - k
                b = b + a * shifted(b, -k, keep, 0.0)
                a = a * shifted(a, -k, keep, 1.0)
            b = b + a * carry[3 * q]
            a = a * carry[3 * q + 1]
            fin[r, :] = a
            adj[r, :] = b
            out += [b[:1], a[:1], here[:1]]
        return tuple(out)

    first = []
    for q in range(sequences):
        one = jnp.ones((1, half), jnp.float32)
        first += [jnp.zeros((1, half), jnp.float32), one, one]
    last = lax.fori_loop(0, groups, scan_group, tuple(first))
    for q in range(sequences):
        ends[s, pl.ds(q, 1), :] = last[3 * q + 1] * last[3 * q + 2]
        ends[s, pl.ds(sequences + q, 1), :] = last[3 * q] * last[3 * q + 2]

    def end_copy(target, source):
        return remote(ends.at[source], ends.at[source], end_s.at[target], end_r.at[source], target, h)

    @pl.loop(1, seq_count)
    def _(q):
        pl.when(s >= q)(lambda: end_copy(jnp.maximum(s - q, 0), s).start())

    arr[...] = jnp.zeros_like(arr)

    @pl.loop(1, seq_count)
    def _(q):
        source = seq_count - q

        @pl.when(source > s)
        def _():
            end_copy(s, source).wait_recv()
            got = ends[source]
            arr[...] = got[:sequences] * arr[...] + got[sequences:]

    for q in range(sequences):
        @pl.loop(0, span // 16)
        def _(i, q=q):
            r = pl.ds(pl.multiple_of(q * span + i * 16, 16), 16)
            adj[r, :] += fin[r, :] * arr[pl.ds(q, 1), :]

    block = rw_ref.shape[1]

    @pl.loop(0, half // block)
    def _(n):
        lanes = pl.ds(pl.multiple_of(n * block, block), block)
        rate = rate_ref[:, lanes]
        sums = [jnp.zeros((1, block), jnp.float32)] * 3
        for q in range(sequences):
            for i in range(2):
                t = i * (span // 2)
                count = span // 2
                r = pl.ds(q * span + t, count)
                rg, ig, conv = rg_ref[r, lanes], ig_ref[r, lanes], conv_ref[r, lanes].astype(jnp.float32)
                a = adj[r, lanes]
                decay = dec[q, pl.ds(t, count), lanes]
                mult = jnp.sqrt(one_minus_square(-8.0 * rate * rg))
                previous = state_ref[q, pl.ds(7 + t, count), lanes]
                grad_mult = a * ig * conv
                grad_log = a * previous * decay - grad_mult * decay * decay / mult
                pre_r = (grad_log * (-8.0 * rate) * rg * (1.0 - rg)).astype(jnp.bfloat16)
                pre_i = (a * mult * conv * ig * (1.0 - ig)).astype(jnp.bfloat16)
                sums[0] = sums[0] + jnp.sum(grad_log * rg, axis=0, keepdims=True)
                sums[1] = sums[1] + jnp.sum(pre_r.astype(jnp.float32), axis=0, keepdims=True)
                sums[2] = sums[2] + jnp.sum(pre_i.astype(jnp.float32), axis=0, keepdims=True)
                back = contract_last(pre_r, rw_ref[n]) + contract_last(pre_i, iw_ref[n])
                gconv[q, pl.ds(t, count), lanes] = (
                    (a * mult * ig + back).astype(jnp.bfloat16).astype(jnp.float32)
                )
                low = conv_ref[r, lanes]
                if q == 0 and i == 0:
                    rwg_ref[n] = contract_first(low, pre_r)
                    iwg_ref[n] = contract_first(low, pre_i)
                else:
                    rwg_ref[n] += contract_first(low, pre_r)
                    iwg_ref[n] += contract_first(low, pre_i)
        vec_ref[pl.ds(8, 1), lanes] = sums[0] * 8.0 * sig_ref[:, lanes]
        vec_ref[pl.ds(6, 1), lanes] = sums[1]
        vec_ref[pl.ds(7, 1), lanes] = sums[2]

    for q in range(sequences):
        halo[0, q] = gconv[q, pl.ds(0, 8), :]
    halo_out = remote(halo.at[0], halo.at[1], halo_s, halo_r, jnp.maximum(s - 1, 0), h)
    pl.when(s > 0)(halo_out.start)

    @pl.loop(0, half // block)
    def _(n):
        lanes = pl.ds(pl.multiple_of(n * block, block), block)
        for k in range(5):
            total = jnp.zeros((1, block), jnp.float32)
            for q in range(sequences):
                value = gconv[q, pl.ds(0, span), lanes]
                if k < 4:
                    value = value * ext_ref[q, pl.ds(8 - k, span), lanes]
                total = total + jnp.sum(value, axis=0, keepdims=True)
            vec_ref[pl.ds(1 + k, 1), lanes] = total

    @pl.when(s + 1 < seq_count)
    def _():
        halo_out.wait_recv()
        for q in range(sequences):
            gconv[q, pl.ds(span, 8), :] = halo[1, q]

    @pl.when(s + 1 == seq_count)
    def _():
        for q in range(sequences):
            gconv[q, pl.ds(span, 8), :] = jnp.zeros((8, half), jnp.float32)

    @pl.loop(0, half // block)
    def _(n):
        lanes = pl.ds(pl.multiple_of(n * block, block), block)
        for q in range(sequences):
            total = cw_ref[pl.ds(0, 1), lanes] * gconv[q, pl.ds(0, span), lanes]
            for k in range(1, 4):
                total = total + cw_ref[pl.ds(k, 1), lanes] * gconv[q, pl.ds(k, span), lanes]
            adj[pl.ds(q * span, span), lanes] = total

    def first_norm(r):
        full = x_ref[r, :].astype(jnp.float32)
        scale = lax.rsqrt(jnp.sum(full * full, axis=1, keepdims=True) * (1.0 / width) + EPS)
        return scale, x_ref[r, mine].astype(jnp.float32) * scale

    for q in range(sequences):
        @pl.loop(0, span // 16)
        def _(i, q=q):
            t = pl.multiple_of(i * 16, 16)
            r = pl.ds(pl.multiple_of(q * span + t, 16), 16)
            product = adj[r, :] * first_norm(r)[1]
            vec_ref[pl.ds(0, 1), :] += jnp.sum(product, axis=0, keepdims=True)
            part[1, r, :] = jnp.broadcast_to(
                jnp.sum(product * gain_ref[:, mine], axis=1, keepdims=True), (16, LANES)
            )
    other[1].start()
    other[1].wait_recv()

    @pl.loop(0, rows // 16)
    def _(i):
        r = pl.ds(pl.multiple_of(i * 16, 16), 16)
        scale, hat = first_norm(r)
        mean = ((part[1, r, :] + part_in[1, r, :]) * (1.0 / width))[:, :1]
        fin[r, :] = gres[r, :] + scale * (adj[r, :] * gain_ref[:, mine] - hat * mean)

    near = pltpu.make_async_copy(fin, out_ref.at[:, mine], loc)
    near.start()
    away = remote(fin, out_ref.at[:, mine], fin_s, fin_r, s, 1 - h)
    away.start()
    for i in range(2):
        other[i].wait_send()
    pl.when(s > 0)(halo_out.wait_send)

    @pl.loop(1, seq_count)
    def _(q):
        pl.when(s >= q)(lambda: end_copy(jnp.maximum(s - q, 0), s).wait_send())

    near.wait()
    away.wait()


def recur_forward(seq_count, sequences, x, norm_gain, conv_weight, conv_bias, recur_weight, recur_bias, input_weight,
                  input_bias, rate, mlp_gain):
    rows, width = x.shape
    half = width // 2
    span = rows // sequences
    bf, f32 = jnp.bfloat16, jnp.float32
    sem = pltpu.SemaphoreType.DMA
    vmem = pl.BlockSpec(memory_space=pltpu.VMEM)
    outs = [
        ((rows, half), bf), ((rows, half), f32), ((rows, LANES), f32), ((sequences, span + 8, half), f32),
        ((rows, half), f32), ((rows, half), f32), ((rows, half), bf), ((sequences, span + 8, half), f32),
    ]
    return pl.pallas_call(
        functools.partial(recur_forward_kernel, seq_count, sequences),
        out_shape=[jax.ShapeDtypeStruct(shape, kind) for shape, kind in outs],
        in_specs=[vmem] * 10,
        out_specs=[vmem] * len(outs),
        scratch_shapes=[
            pltpu.VMEM((rows, half), f32), pltpu.VMEM((rows, half), f32), pltpu.VMEM((2, sequences, 8, half), f32),
            pltpu.VMEM((seq_count, 2 * sequences, half), f32), pltpu.VMEM((sequences, half), f32),
            pltpu.VMEM((rows, LANES), f32), pltpu.VMEM((rows, LANES), f32),
            sem, sem, sem((seq_count,)), sem((seq_count,)), sem, sem,
        ],
        compiler_params=pltpu.CompilerParams(
            collective_id=1, has_side_effects=True, vmem_limit_bytes=60 * 2**20
        ),
        name="recur_forward",
    )(x, norm_gain[None], conv_weight, conv_bias[None], recur_weight, recur_bias[None], input_weight, input_bias[None],
      rate[None], mlp_gain[None])


def recur_backward(seq_count, sequences, grad_half, cotangent, x, saved, norm_gain, conv_weight, recur_weight,
                   input_weight, rate, slope, mlp_gain):
    rows, width = x.shape
    half = width // 2
    span = rows // sequences
    bf, f32 = jnp.bfloat16, jnp.float32
    sem = pltpu.SemaphoreType.DMA
    vmem = pl.BlockSpec(memory_space=pltpu.VMEM)
    outs = [((rows, width), f32), ((16, half), f32), (recur_weight.shape, f32), (recur_weight.shape, f32)]
    args = (grad_half, cotangent, x, *saved, norm_gain[None], conv_weight, recur_weight, input_weight, rate[None],
            slope[None], mlp_gain[None])
    return pl.pallas_call(
        functools.partial(recur_backward_kernel, seq_count, sequences),
        out_shape=[jax.ShapeDtypeStruct(shape, kind) for shape, kind in outs],
        in_specs=[vmem] * len(args),
        out_specs=[pl.BlockSpec(memory_space=pl.ANY)] + [vmem] * 3,
        scratch_shapes=[
            pltpu.VMEM((rows, half), f32), pltpu.VMEM((sequences, span, half), f32), pltpu.VMEM((rows, half), f32),
            pltpu.VMEM((sequences, span + 8, half), f32), pltpu.VMEM((2, sequences, 8, half), f32),
            pltpu.VMEM((seq_count, 2 * sequences, half), f32), pltpu.VMEM((sequences, half), f32),
            pltpu.VMEM((2, rows, LANES), f32), pltpu.VMEM((2, rows, LANES), f32), pltpu.VMEM((rows, half), f32),
            sem, sem, sem((seq_count,)), sem((seq_count,)), sem((2,)), sem((2,)), sem, sem, sem,
        ],
        compiler_params=pltpu.CompilerParams(
            collective_id=2, has_side_effects=True, vmem_limit_bytes=60 * 2**20
        ),
        name="recur_backward",
    )(*args)


def gathered_shards(
    block_input,
    norm_gain,
    conv_weight,
    conv_bias,
    recur_weight,
    recur_bias,
    input_weight,
    input_bias,
    decay_param,
    mlp_gain,
    w_gate,
    w_up,
    w_down,
    out_grad,
):
    sequences, span_len, model_width = block_input.shape
    lru_width = conv_bias.shape[0]
    heads_here = recur_weight.shape[0]
    block_width = recur_weight.shape[1]
    token_rows = sequences * span_len
    head_at = lax.axis_index("head")
    stream = block_input.astype(jnp.float32)
    first_scale, first_hat = norm_rows(stream)
    xn_first = (first_hat * norm_gain).astype(jnp.bfloat16)
    own_input = lax.dynamic_slice_in_dim(xn_first, head_at * lru_width, lru_width, 2)
    edge_rows = from_behind(own_input[:, span_len - 3 :, :], "seq", 1)
    padded = jnp.concatenate([edge_rows, own_input], axis=1).astype(jnp.float32)
    conv_sum = conv_bias + conv_weight[0] * padded[:, 3 : 3 + span_len]
    for offset in range(1, 4):
        conv_sum = conv_sum + conv_weight[offset] * padded[:, 3 - offset : 3 - offset + span_len]
    conv_out = conv_sum.astype(jnp.bfloat16)
    conv_blocks = conv_out.reshape(token_rows, heads_here, block_width)
    recur_pre = (
        jnp.einsum(
            "tnh,nhk->tnk", conv_blocks, recur_weight, preferred_element_type=jnp.float32
        ).reshape(sequences, span_len, lru_width)
        + recur_bias
    )
    input_pre = (
        jnp.einsum(
            "tnh,nhk->tnk", conv_blocks, input_weight, preferred_element_type=jnp.float32
        ).reshape(sequences, span_len, lru_width)
        + input_bias
    )
    recur_gate = jax.nn.sigmoid(recur_pre)
    input_gate = jax.nn.sigmoid(input_pre)
    rate = jax.nn.softplus(-decay_param)
    log_decay = -8.0 * rate * recur_gate
    decay = jnp.exp(log_decay)
    multiplier = jnp.sqrt(-jnp.expm1(2.0 * log_decay))
    conv_float = conv_out.astype(jnp.float32)
    pushed = multiplier * input_gate * conv_float
    decay_prod, local_state = lax.associative_scan(link_forward, (decay, pushed), axis=1)
    ones_edge = jnp.ones((sequences, lru_width), jnp.float32)
    zeros_edge = jnp.zeros((sequences, lru_width), jnp.float32)
    entering = prefix(
        (decay_prod[:, -1], local_state[:, -1]), "seq", link_forward, (ones_edge, zeros_edge), False
    )
    state = local_state + decay_prod * entering[1][:, None, :]
    state_full = lax.all_gather(state.astype(jnp.bfloat16), "head", axis=2, tiled=True)
    residual = stream + state_full.astype(jnp.float32)
    second_scale, second_hat = norm_rows(residual)
    xn_second = (second_hat * mlp_gain).astype(jnp.bfloat16).reshape(token_rows, model_width)
    hidden_width = w_gate.shape[1]
    pieces = (
        lax.all_gather(w_gate, "seq", axis=0, tiled=True),
        lax.all_gather(w_up, "seq", axis=0, tiled=True),
    )
    columns = xn_second
    gate = jnp.dot(columns, pieces[0], preferred_element_type=jnp.float32)
    up_value = jnp.dot(columns, pieces[1], preferred_element_type=jnp.float32)
    activated, gelu_back = jax.vjp(jax.nn.gelu, gate)
    hidden = (activated * up_value).astype(jnp.bfloat16)
    partial_mix = contract_last(hidden, lax.all_gather(w_down, "seq", axis=0, tiled=True))
    mixed = lax.psum(partial_mix, "head")
    block_output = (
        (residual.reshape(token_rows, model_width) + mixed)
        .astype(jnp.bfloat16)
        .reshape(block_input.shape)
    )
    cotangent = out_grad.reshape(token_rows, model_width)
    columns = cotangent
    grad_hidden = jnp.dot(
        columns,
        lax.all_gather(w_down, "seq", axis=0, tiled=True),
        preferred_element_type=jnp.float32,
    )
    grad_gate = gelu_back(grad_hidden * up_value)[0].astype(jnp.bfloat16)
    grad_up = (grad_hidden * activated).astype(jnp.bfloat16)
    pieces = (
        lax.all_gather(w_gate, "seq", axis=0, tiled=True),
        lax.all_gather(w_up, "seq", axis=0, tiled=True),
    )
    block_value = contract_last(grad_gate, pieces[0]) + contract_last(grad_up, pieces[1])
    grad_xn_second = lax.psum(block_value, "head").reshape(block_input.shape)
    stacked = jnp.concatenate([grad_gate, grad_up], axis=1)
    local_rows = w_gate.shape[0]
    seq_count = lax.axis_size("seq")
    turns = math.gcd(local_rows, 8)
    per_turn = local_rows // turns
    input_view = xn_second.reshape(token_rows, seq_count, local_rows)
    grad_view = cotangent.reshape(token_rows, seq_count, local_rows)

    def grad_turn(turn, collected):
        first_row = turn * per_turn
        input_cols = lax.dynamic_slice_in_dim(input_view, first_row, per_turn, 2).reshape(
            token_rows, seq_count * per_turn
        )
        grad_cols = lax.dynamic_slice_in_dim(grad_view, first_row, per_turn, 2).reshape(
            token_rows, seq_count * per_turn
        )
        term = jnp.concatenate(
            [contract_first(input_cols, stacked), contract_first(grad_cols, hidden)], axis=1
        )
        share = lax.psum_scatter(term, "seq", scatter_dimension=0, tiled=True)
        return lax.dynamic_update_slice_in_dim(collected, share, first_row, 0)

    weight_grads = lax.fori_loop(
        0, turns, grad_turn, jnp.zeros((local_rows, 3 * hidden_width), jnp.float32)
    )
    w_gate_grad = weight_grads[:, :hidden_width]
    w_up_grad = weight_grads[:, hidden_width : 2 * hidden_width]
    w_down_grad = weight_grads[:, 2 * hidden_width :]
    weighted_second = grad_xn_second * mlp_gain
    mlp_gain_local = jnp.sum(grad_xn_second * second_hat, axis=(0, 1))
    grad_residual = out_grad.astype(jnp.float32) + second_scale * (
        weighted_second
        - second_hat * jnp.mean(weighted_second * second_hat, axis=-1, keepdims=True)
    )
    grad_state = lax.dynamic_slice_in_dim(grad_residual, head_at * lru_width, lru_width, 2)
    next_decay = jnp.concatenate([decay[:, 1:], jnp.ones_like(decay[:, :1])], axis=1)
    flipped = lax.associative_scan(
        link_forward, (jnp.flip(next_decay, 1), jnp.flip(grad_state, 1)), axis=1
    )
    after_prod = jnp.flip(flipped[0], 1)
    local_adjoint = jnp.flip(flipped[1], 1)
    leaving = (decay_prod[:, -1], decay[:, 0] * local_adjoint[:, 0])
    arriving = prefix(leaving, "seq", link_backward, (ones_edge, zeros_edge), True)
    adjoint = local_adjoint + after_prod * arriving[1][:, None, :]
    previous = jnp.concatenate([entering[1][:, None, :], state[:, :-1]], axis=1)
    grad_mult = adjoint * input_gate * conv_float
    grad_log = adjoint * previous * decay - grad_mult * decay * decay / multiplier
    grad_recur_pre = (grad_log * (-8.0 * rate) * recur_gate * (1.0 - recur_gate)).astype(
        jnp.bfloat16
    )
    grad_input_pre = (adjoint * multiplier * conv_float * input_gate * (1.0 - input_gate)).astype(
        jnp.bfloat16
    )
    decay_local = jnp.sum(grad_log * 8.0 * recur_gate, axis=(0, 1)) * jax.nn.sigmoid(-decay_param)
    recur_blocks = grad_recur_pre.reshape(token_rows, heads_here, block_width)
    input_blocks = grad_input_pre.reshape(token_rows, heads_here, block_width)
    back_gates = jnp.einsum(
        "tnk,nhk->tnh", recur_blocks, recur_weight, preferred_element_type=jnp.float32
    )
    back_gates = back_gates + jnp.einsum(
        "tnk,nhk->tnh", input_blocks, input_weight, preferred_element_type=jnp.float32
    )
    grad_conv = (
        adjoint * multiplier * input_gate + back_gates.reshape(sequences, span_len, lru_width)
    ).astype(jnp.bfloat16)
    recur_weight_local = jnp.einsum(
        "tnh,tnk->nhk", conv_blocks, recur_blocks, preferred_element_type=jnp.float32
    )
    input_weight_local = jnp.einsum(
        "tnh,tnk->nhk", conv_blocks, input_blocks, preferred_element_type=jnp.float32
    )
    recur_bias_local = jnp.sum(grad_recur_pre.astype(jnp.float32), axis=(0, 1))
    input_bias_local = jnp.sum(grad_input_pre.astype(jnp.float32), axis=(0, 1))
    later_rows = from_behind(grad_conv[:, :3, :], "seq", -1)
    grad_padded = jnp.concatenate([grad_conv, later_rows], axis=1).astype(jnp.float32)
    grad_conv_float = grad_conv.astype(jnp.float32)
    grad_own_input = conv_weight[0] * grad_padded[:, 0:span_len]
    for offset in range(1, 4):
        grad_own_input = (
            grad_own_input + conv_weight[offset] * grad_padded[:, offset : offset + span_len]
        )
    conv_weight_local = jnp.stack(
        [
            jnp.sum(grad_conv_float * padded[:, 3 - offset : 3 - offset + span_len], axis=(0, 1))
            for offset in range(4)
        ]
    )
    conv_bias_local = jnp.sum(grad_conv_float, axis=(0, 1))
    grad_xn_first = lax.all_gather(
        grad_own_input.astype(jnp.bfloat16), "head", axis=2, tiled=True
    ).astype(grad_own_input.dtype)
    weighted_first = grad_xn_first * norm_gain
    norm_gain_local = jnp.sum(grad_xn_first * first_hat, axis=(0, 1))
    input_grad = grad_residual + first_scale * (
        weighted_first - first_hat * jnp.mean(weighted_first * first_hat, axis=-1, keepdims=True)
    )
    summed = lax.psum(
        (
            norm_gain_local,
            conv_weight_local,
            conv_bias_local,
            recur_weight_local,
            recur_bias_local,
            input_weight_local,
            input_bias_local,
            decay_local,
            mlp_gain_local,
        ),
        "seq",
    )
    return (
        block_output,
        input_grad,
        summed[0],
        summed[1],
        summed[2],
        summed[3],
        summed[4],
        summed[5],
        summed[6],
        summed[7],
        summed[8],
        w_gate_grad,
        w_up_grad,
        w_down_grad,
    )


def shards(
    block_input,
    norm_gain,
    conv_weight,
    conv_bias,
    recur_weight,
    recur_bias,
    input_weight,
    input_bias,
    decay_param,
    mlp_gain,
    w_gate,
    w_up,
    w_down,
    out_grad,
):
    seq_count = lax.axis_size("seq")
    sequences, span_len, width = block_input.shape
    if seq_count % 8 or w_gate.shape[0] % 32:
        return gathered_shards(
            block_input, norm_gain, conv_weight, conv_bias, recur_weight, recur_bias, input_weight, input_bias,
            decay_param, mlp_gain, w_gate, w_up, w_down, out_grad,
        )
    rows = sequences * span_len
    stream = block_input.reshape(rows, width)
    cotangent = out_grad.reshape(rows, width)
    rate = jax.nn.softplus(-decay_param)
    slope = jax.nn.sigmoid(-decay_param)
    xn_half, *saved = recur_forward(
        seq_count, sequences, stream, norm_gain, conv_weight, conv_bias, recur_weight, recur_bias, input_weight,
        input_bias, rate, mlp_gain,
    )
    mixed_half, grad_half, weight_grads = feed_forward(seq_count, xn_half, cotangent, w_gate, w_up, w_down)
    block_half = (saved[0] + mixed_half).astype(jnp.bfloat16)
    block_output = lax.all_gather(block_half, "head", axis=1, tiled=True).reshape(block_input.shape)
    input_grad, vectors, recur_local, input_local = recur_backward(
        seq_count, sequences, grad_half, cotangent, stream, saved, norm_gain, conv_weight, recur_weight,
        input_weight, rate, slope, mlp_gain,
    )
    vectors, recur_weight_grad, input_weight_grad = lax.psum((vectors, recur_local, input_local), "seq")
    gains = lax.all_gather(jnp.stack([vectors[0], vectors[9]]), "head", axis=1, tiled=True)
    return (
        block_output,
        input_grad.reshape(block_input.shape),
        gains[0],
        vectors[1:5],
        vectors[5],
        recur_weight_grad,
        vectors[6],
        input_weight_grad,
        vectors[7],
        vectors[8],
        gains[1],
        weight_grads[0].astype(jnp.float32),
        weight_grads[1].astype(jnp.float32),
        weight_grads[2].astype(jnp.float32),
    )


def solution(mesh):
    placed = (
        P(None, "seq", None),
        P(),
        P(None, "head"),
        P("head"),
        P("head", None, None),
        P("head"),
        P("head", None, None),
        P("head"),
        P("head"),
        P(),
        P("seq", "head"),
        P("seq", "head"),
        P("seq", "head"),
        P(None, "seq", None),
    )
    return jax.shard_map(
        shards,
        mesh=mesh,
        in_specs=placed,
        out_specs=(
            P(None, "seq", None),
            P(None, "seq", None),
            P(),
            P(None, "head"),
            P("head"),
            P("head", None, None),
            P("head"),
            P("head", None, None),
            P("head"),
            P("head"),
            P(),
            P("seq", "head"),
            P("seq", "head"),
            P("seq", "head"),
        ),
        check_vma=False,
    )
```

```python
import functools
import math

import jax
import jax.numpy as jnp
from jax import lax
from jax.experimental import pallas as pl
from jax.experimental.pallas import tpu as pltpu
from jax.sharding import PartitionSpec as P

EPS = 1e-06
MESH = pl.DeviceIdType.MESH
LANES = 128
CHUNK = 256


def from_behind(value, axis, steps):
    count = lax.axis_size(axis)
    initial, last = (max(0, -steps), min(count, count - steps))
    return lax.ppermute(value, axis, [(source, source + steps) for source in range(initial, last)])


def prefix(part, axis, combine, identity, reverse):
    count = lax.axis_size(axis)
    place = lax.axis_index(axis)
    ahead = count - 1 - place if reverse else place
    gathered = jax.tree.map(lambda a: lax.all_gather(a, axis), part)
    state = jax.tree.map(lambda a, e: jnp.zeros_like(a) + jnp.asarray(e, a.dtype), part, identity)

    def one(lap, state):
        source = count - 1 - lap if reverse else lap
        return combine(
            state, jax.tree.map(lambda a: lax.dynamic_index_in_dim(a, source, 0, False), gathered)
        )

    return lax.fori_loop(0, ahead, one, state)


def norm_rows(values):
    scale = lax.rsqrt(jnp.mean(values * values, axis=-1, keepdims=True) + EPS)
    return (scale, values * scale)


def link_forward(earlier, latter):
    return (earlier[0] * latter[0], latter[0] * earlier[1] + latter[1])


def link_backward(earlier, latter):
    return (earlier[0] * latter[0], latter[1] + latter[0] * earlier[1])


def contract_last(left_side, right_side):
    return lax.dot_general(
        left_side, right_side, (((1,), (1,)), ((), ())), preferred_element_type=jnp.float32
    )


def contract_first(left_side, right_side):
    return lax.dot_general(
        left_side, right_side, (((0,), (0,)), ((), ())), preferred_element_type=jnp.float32
    )


def dot_nn(left_side, right_side):
    return jnp.dot(left_side, right_side, preferred_element_type=jnp.float32)


def remote(src, dst, send, recv, seq, head):
    return pltpu.make_async_remote_copy(
        src_ref=src, dst_ref=dst, send_sem=send, recv_sem=recv,
        device_id={"seq": seq, "head": head}, device_id_type=MESH,
    )


def half_window(head, half):
    return pl.ds(pl.multiple_of(head * half, LANES), half)


def greet_all(seq_count, s, h):
    barrier = pltpu.get_barrier_semaphore()

    @pl.loop(1, seq_count)
    def _(q):
        seq = (s + q) % seq_count
        pl.semaphore_signal(barrier, inc=1, device_id={"seq": seq, "head": h}, device_id_type=MESH)

    pl.semaphore_signal(barrier, inc=1, device_id={"seq": s, "head": 1 - h}, device_id_type=MESH)
    pl.semaphore_wait(barrier, seq_count)


def one_minus_square(log_decay):
    twice = 2.0 * log_decay
    series = 1.0 + twice * (1 / 2 + twice * (1 / 6 + twice * (1 / 24 + twice * (1 / 120 + twice * (1 / 720)))))
    return jnp.where(twice > -0.25, -twice * series, 1.0 - jnp.exp(twice))


def shifted(value, step, keep, fill):
    return jnp.where(keep, pltpu.roll(value, step % 8, 0), fill)


def block_kernel(
    seq_count, sequences, x_ref, g_ref, wg_ref, wu_ref, wd_ref,
    gain_ref, cw_ref, cb_ref, rw_ref, rb_ref, iw_ref, ib_ref, rate_ref, sig_ref, mgain_ref,
    out_ref, ingrad_ref, dw_ref, vec_ref, mat_ref,
    dh_ref, r1_ref, e_ref, r2_ref, f_ref, sib_ref, peer_ref, xn_half, rg_keep, ig_keep, conv_keep, ext_keep, state_keep,
    res_keep, ma_ref, mb_ref,
    x_all, g_all, w_all, ld, halos, ends_all, ent, arr, part, part_in, scales, vec_in,
    tok_s, tok_r, fwd_s, fwd_r, s1_s, s1_r, z_s, z_r, y_s, y_r, c1_s, c1_r, c2_s, c2_r, c3_s, c3_r,
    sib_s, sib_r, peer_s, peer_r, halo_s, halo_r, end_s, end_r, part_s, part_r, fin_s, fin_r, ma_s, ma_r, mb_s, mb_r, mc_s, mc_r, md_s, md_r, va_s, va_r, vb_s, vb_r, keep, loc,
):
    far = seq_count // 8
    rows = wg_ref.shape[0]
    pair = 2 * rows
    tokens, half = x_ref.shape[0], x_ref.shape[1] // 2
    span = w_all.shape[2]
    chunks = span // CHUNK
    tiles = wg_ref.shape[1] // LANES
    base, extra = tiles // 4, tiles % 4
    s = lax.axis_index("seq")
    h = lax.axis_index("head")
    x = s % 2
    y = (s // 2) % 2
    zl = (s // 4) % 2
    zh = s // 8
    a = zl * 2 + x
    weights = (wg_ref, wu_ref, wd_ref)

    def seq_of(zh_, zl_, y_, x_):
        return ((zh_ * 2 + zl_) * 2 + y_) * 2 + x_

    def peer(d):
        zl_, x_ = (zl + d // 2) % 2, (x + d % 2) % 2
        return zl_ * 2 + x_, seq_of(zh, zl_, y, x_), zl_, x_

    def first_tile(a_):
        low = base * a_ + jnp.minimum(a_, extra)
        high = base * a_ + jnp.maximum(a_ - (4 - extra), 0)
        return jnp.where(h == 0, low, high)

    def wide(zl_):
        return zl_ == h

    def block_rows(zh_, zl_, y_):
        return pl.ds(pl.multiple_of(((zh_ * 2 + zl_) * 2 + y_) * pair, 32), pair)

    def cols(c, width=CHUNK):
        return pl.ds(pl.multiple_of(c * CHUNK, CHUNK), width)

    def by_width(c, is_wide, run):
        narrow = (c == chunks - 1) & jnp.logical_not(is_wide)
        pl.when(narrow)(lambda: run(LANES))
        pl.when(jnp.logical_not(narrow))(lambda: run(CHUNK))

    y_seq = seq_of(zh, zl, 1 - y, x)

    def z_seq(q):
        return seq_of((zh + q) % far, zl, y, x)

    model = 2 * half
    length = tokens // sequences
    groups = length // 8
    mine = half_window(h, half)
    block = rw_ref.shape[1]
    heads = half // block
    f32, bf = jnp.float32, jnp.bfloat16
    greet_all(seq_count, s, h)

    def s1_send(c, d, w, width):
        a_, seq, zl_, _ = peer(d)
        col = pl.multiple_of((first_tile(a_) + 2 * c) * LANES, LANES)
        return remote(
            weights[w].at[:, pl.ds(col, width)],
            w_all.at[w, pl.ds(pl.multiple_of(s * rows, 32), rows), cols(c, width)],
            s1_s.at[c, d - 1, w], s1_r.at[c, d - 1, w], seq, h,
        )

    def s1_recv(c, d, w, width):
        _, seq, _, _ = peer(d)
        return remote(
            weights[w].at[:, pl.ds(0, width)],
            w_all.at[w, pl.ds(pl.multiple_of(seq * rows, 32), rows), cols(c, width)],
            s1_s.at[c, d - 1, w], s1_r.at[c, d - 1, w], seq, h,
        )

    def s1_own(c, w, width):
        col = pl.multiple_of((first_tile(a) + 2 * c) * LANES, LANES)
        return pltpu.make_async_copy(
            weights[w].at[:, pl.ds(col, width)],
            w_all.at[w, pl.ds(pl.multiple_of(s * rows, 32), rows), cols(c, width)],
            loc.at[c, w],
        )

    def s1_start(c):
        for d in (1, 2, 3):
            def go(width, d=d):
                for w in range(3):
                    s1_send(c, d, w, width).start()
            by_width(c, wide(peer(d)[2]), go)

        def own(width):
            for w in range(3):
                s1_own(c, w, width).start()
        by_width(c, wide(zl), own)

    def s1_wait(c):
        def got(width):
            for w in range(3):
                s1_own(c, w, width).wait()
                for d in (1, 2, 3):
                    s1_recv(c, d, w, width).wait_recv()
        by_width(c, wide(zl), got)

    def s1_drain(c):
        for d in (1, 2, 3):
            def go(width, d=d):
                for w in range(3):
                    s1_send(c, d, w, width).wait_send()
            by_width(c, wide(peer(d)[2]), go)

    def z_copy(c, q, zl_, width, incoming):
        zh_ = (zh - q + far) % far if incoming else zh
        part = w_all.at[:, block_rows(zh_, zl_, y), cols(c, width)]
        return remote(part, part, z_s.at[c, q - 1, zl_], z_r.at[c, q - 1, zl_], z_seq(q), h)

    def y_copy(c, q, zl_, width, incoming):
        part = w_all.at[:, block_rows((zh - q + far) % far, zl_, 1 - y if incoming else y), cols(c, width)]
        return remote(part, part, y_s.at[c, q, zl_], y_r.at[c, q, zl_], y_seq, h)

    def z_start(c):
        def go(width):
            for q in range(1, far):
                for zl_ in range(2):
                    z_copy(c, q, zl_, width, False).start()
            for zl_ in range(2):
                y_copy(c, 0, zl_, width, False).start()
        by_width(c, wide(zl), go)

    def z_forward(c):
        def go(width):
            for q in range(1, far):
                for zl_ in range(2):
                    z_copy(c, q, zl_, width, True).wait_recv()
                    y_copy(c, q, zl_, width, False).start()
        by_width(c, wide(zl), go)

    def y_wait(c):
        def go(width):
            for q in range(far):
                for zl_ in range(2):
                    y_copy(c, q, zl_, width, True).wait_recv()
        by_width(c, wide(zl), go)

    def zy_drain(c):
        def go(width):
            for zl_ in range(2):
                for q in range(1, far):
                    z_copy(c, q, zl_, width, False).wait_send()
                for q in range(far):
                    y_copy(c, q, zl_, width, False).wait_send()
        by_width(c, wide(zl), go)

    half_cols = pl.ds(pl.multiple_of(h * half, LANES), half)

    def tok_rows(a_):
        return pl.ds(pl.multiple_of(a_ * tokens, 32), tokens)

    def tok_copy(k, d, incoming):
        src = xn_half if k == 0 else g_ref.at[:, half_cols]
        dst = (x_all, g_all)[k]
        here = a
        if d == 3:
            here = peer(2)[0]
            src = dst.at[tok_rows(here), half_cols]
        return remote(
            src, dst.at[tok_rows(peer(d)[0] if incoming else here), half_cols],
            tok_s.at[k, d - 1], tok_r.at[k, d - 1], peer(1 if d == 3 else d)[1], h,
        )

    def fwd_copy(k, d, incoming):
        dst = (x_all, g_all)[k]
        side = pl.ds(pl.multiple_of((1 - h if incoming else h) * half, LANES), half)
        part = dst.at[tok_rows(peer(d)[0]), side]
        return remote(part, part, fwd_s.at[k, d], fwd_r.at[k, d], s, 1 - h)

    own_x = pltpu.make_async_copy(xn_half, x_all.at[tok_rows(a), half_cols], loc.at[chunks, 0])
    own_g = pltpu.make_async_copy(g_ref, g_all.at[tok_rows(a), :], loc.at[chunks, 1])

    def tok_start(k):
        tok_copy(k, 2, False).start()
        tok_copy(k, 1, False).start()

    def tok_turn(k):
        tok_copy(k, 2, True).wait_recv()
        tok_copy(k, 3, False).start()
        fwd_copy(k, 2, False).start()

    def tok_last(k):
        for d in (1, 3):
            tok_copy(k, d, True).wait_recv()
            fwd_copy(k, d, False).start()

    def tok_wait(k):
        for d in ((1, 2, 3) if k else (0, 1, 2, 3)):
            fwd_copy(k, d, True).wait_recv()

    def r1_copy(c, zh_, zl_, incoming):
        return remote(
            dh_ref.at[c, :, block_rows(zh_, zl_, 1 - y), :], r1_ref.at[c, :, pl.ds((zh_ * 2 + zl_) * pair, pair)],
            c1_s.at[c, zh_, zl_], c1_r.at[c, zh_, zl_], y_seq, h,
        )

    def r1_start(c, steps_away):
        for q in steps_away:
            for zl_ in range(2):
                r1_copy(c, (zh + q) % far, zl_, False).start()

    def r2_copy(c, q, zl_):
        return remote(
            e_ref.at[c, :, pl.ds(pl.multiple_of((((zh + q) % far) * 2 + zl_) * pair, 32), pair)], r2_ref.at[c, q - 1, :, pl.ds(zl_ * pair, pair)],
            c2_s.at[c, q - 1, zl_], c2_r.at[c, q - 1, zl_], z_seq(q), h,
        )

    def add_into(first, second, blocks):
        @pl.loop(0, 3)
        def _(w):
            @pl.loop(0, blocks)
            def _(b):
                r = pl.ds(pl.multiple_of(b * pair, 32), pair)
                total = first[w, r, :].astype(jnp.float32) + second[w, r, :].astype(jnp.float32)
                first[w, r, :] = total.astype(jnp.bfloat16)

    def plane_rows(zh_):
        return pl.ds(pl.multiple_of(zh_ * 2 * pair, 32), 2 * pair)

    def sum_near(c, q, va, vb):
        zh_ = (zh + q) % far
        loads = []
        for zl_ in range(2):
            loads.append(pltpu.make_async_copy(
                dh_ref.at[c, :, block_rows(zh_, zl_, y), :], va.at[:, pl.ds(zl_ * pair, pair)], loc.at[chunks + 1, zl_]
            ))
            loads[-1].start()
        for zl_ in range(2):
            r1_copy(c, zh_, zl_, True).wait_recv()
        loads.append(pltpu.make_async_copy(r1_ref.at[c, :, plane_rows(zh_)], vb, loc.at[chunks, 2]))
        loads[-1].start()
        for load in loads:
            load.wait()
        add_into(va, vb, 2)
        back = pltpu.make_async_copy(va, e_ref.at[c, :, plane_rows(zh_)], loc.at[chunks, 2])
        back.start()
        back.wait()
        if q:
            for zl_ in range(2):
                r2_copy(c, q, zl_).start()

    def near_all(c, va, vb):
        for q in list(range(1, far)) + [0]:
            sum_near(c, q, va, vb)

    def c3_copy(c, d, width, incoming):
        a_, seq, zl_, x_ = peer(d)
        col = pl.multiple_of((first_tile(a_ if incoming else a) + 2 * c) * LANES, LANES)
        return remote(
            f_ref.at[c, :, pl.ds(pl.multiple_of((zl_ * 2 + x_) * rows, 32), rows), pl.ds(0, width)],
            dw_ref.at[:, :, pl.ds(col, width)],
            c3_s.at[c, d - 1], c3_r.at[c, d - 1], seq, h,
        )

    def c3_own(c, width):
        col = pl.multiple_of((first_tile(a) + 2 * c) * LANES, LANES)
        return pltpu.make_async_copy(
            f_ref.at[c, :, pl.ds(pl.multiple_of(a * rows, 32), rows), pl.ds(0, width)],
            dw_ref.at[:, :, pl.ds(col, width)], loc.at[c, 0],
        )

    def sum_far(c, va, vb):
        first, second = va, vb
        kept = pltpu.make_async_copy(
            e_ref.at[c, :, pl.ds(pl.multiple_of(zh * 2 * pair, 32), 2 * pair)], first, loc.at[chunks, 0]
        )
        kept.start()
        kept.wait()
        for q in range(1, far):
            for zl_ in range(2):
                r2_copy(c, q, zl_).wait_recv()
            other = pltpu.make_async_copy(r2_ref.at[c, q - 1], second, loc.at[chunks, 0])
            other.start()
            other.wait()
            add_into(va, vb, 2)
        back = pltpu.make_async_copy(first, f_ref.at[c], loc.at[chunks, 0])
        back.start()
        back.wait()

        def go(width):
            for d in (1, 2, 3):
                c3_copy(c, d, width, False).start()
            c3_own(c, width).start()
        by_width(c, wide(zl), go)

    def forward_chunk(c, hid, gg, gu):
        @pl.loop(0, 4)
        def _(i):
            r = tok_rows(i)
            xb = x_all[r, :]
            gate = dot_nn(xb, w_all[0, :, cols(c)])
            up = dot_nn(xb, w_all[1, :, cols(c)])
            gh = dot_nn(g_all[r, :], w_all[2, :, cols(c)])
            k0, k1 = 0.7978845608028654, 0.044715
            th = jnp.tanh(k0 * (gate + k1 * gate * gate * gate))
            cdf = 0.5 * (1.0 + th)
            act = gate * cdf
            slope = cdf + 0.5 * gate * (1.0 - th * th) * k0 * (1.0 + 3.0 * k1 * gate * gate)
            hid[r, cols(c)] = (act * up).astype(jnp.bfloat16)
            gu[r, cols(c)] = (gh * act).astype(jnp.bfloat16)
            gg[r, cols(c)] = (gh * up * slope).astype(jnp.bfloat16)

    def weight_chunk(c, hid, gg, gu, dv):
        for w, (left, right) in enumerate(((x_all, gg), (x_all, gu), (g_all, hid))):
            @pl.loop(0, x_all.shape[1] // 512)
            def _(j):
                r = pl.ds(pl.multiple_of(j * 512, 512), 512)
                dv[w, r, :] = contract_first(left[:, r], right[:, cols(c)]).astype(jnp.bfloat16)
            pltpu.make_async_copy(dv.at[w], dh_ref.at[c, w], loc.at[chunks, w]).start()
        for w in range(3):
            pltpu.make_async_copy(dv.at[w], dh_ref.at[c, w], loc.at[chunks, w]).wait()

    def product(which, r, d_rows, hid, gg, gu):
        if which == 0:
            return contract_last(gg[r, :], w_all[0, d_rows, :]) + contract_last(gu[r, :], w_all[1, d_rows, :])
        return contract_last(hid[r, :], w_all[2, d_rows, :])

    def pairs(i):
        return pl.ds(pl.multiple_of(i * 16, 16), 16)

    def head_lanes(n):
        return pl.ds(pl.multiple_of(n * block, block), block)

    def end_copy(side, target, source):
        part_ends = ends_all.at[side, source]
        return remote(part_ends, part_ends, end_s.at[side, target], end_r.at[side, source], target, h)

    def part_copy(i):
        return remote(part.at[i], part_in.at[i], part_s.at[i], part_r.at[i], s, 1 - h)

    def halo_copy(side):
        target = jnp.minimum(s + 1, seq_count - 1) if side == 0 else jnp.maximum(s - 1, 0)
        return remote(halos.at[side, 0], halos.at[side, 1], halo_s.at[side], halo_r.at[side], target, h)

    row_ids = lax.broadcasted_iota(jnp.int32, (8, half), 0)

    place, plane, planes = s % 4, s // 4, seq_count // 4
    quarter = 2 * heads * block // 4
    piece = quarter // planes
    mat = w_all.at[0, pl.ds(0, 4 * quarter), pl.ds(2 * CHUNK, block)]
    got_a = w_all.at[1, pl.ds(0, 3 * quarter), pl.ds(2 * CHUNK, block)]
    got_b = w_all.at[2, pl.ds(quarter, (planes - 1) * piece), pl.ds(2 * CHUNK, block)]
    own_sum = w_all.at[2, pl.ds(0, quarter), pl.ds(2 * CHUNK, block)]

    def mate(i):
        return plane * 4 + (place + i) % 4

    def layer(j):
        return (plane + j) % planes * 4 + place

    def rows_at(start, count):
        return pl.ds(pl.multiple_of(start, 32), count)

    def mat_a(i):
        return remote(
            mat.at[rows_at((place + i) % 4 * quarter, quarter)], ma_ref.at[pl.ds((i - 1) * quarter, quarter)],
            ma_s.at[i - 1], ma_r.at[i - 1], mate(i), h,
        )

    def mat_b(j):
        return remote(
            own_sum.at[rows_at((plane + j) % planes * piece, piece)], mb_ref.at[pl.ds((j - 1) * piece, piece)],
            mb_s.at[j - 1], mb_r.at[j - 1], layer(j), h,
        )

    def mat_c(j, incoming):
        source = (plane - j + planes) % planes if incoming else plane
        part_rows = mat_ref.at[rows_at(place * quarter + source * piece, piece)]
        return remote(part_rows, part_rows, mc_s.at[j - 1], mc_r.at[j - 1], layer(j), h)

    def mat_d(i, incoming):
        source = (place - i + 4) % 4 if incoming else place
        part_rows = mat_ref.at[rows_at(source * quarter, quarter)]
        return remote(part_rows, part_rows, md_s.at[i - 1], md_r.at[i - 1], mate(i), h)

    def take(src, dst, i):
        load = pltpu.make_async_copy(src, dst, keep.at[i])
        load.start()
        load.wait()

    def matrices_start():
        for i in (1, 2, 3):
            mat_a(i).start()

    def matrices_plane():
        for i in (1, 2, 3):
            mat_a(i).wait_recv()
        take(ma_ref, got_a, 8)

        @pl.loop(0, quarter // 32)
        def _(i):
            total = mat[rows_at(place * quarter + i * 32, 32), :].astype(f32)
            for k in range(3):
                total = total + got_a[rows_at(k * quarter + i * 32, 32), :].astype(f32)
            own_sum[rows_at(i * 32, 32), :] = total.astype(bf)
        for j in range(1, planes):
            mat_b(j).start()

    def matrices_across():
        for j in range(1, planes):
            mat_b(j).wait_recv()
        take(mb_ref, got_b, 8)

        @pl.loop(0, piece // 32)
        def _(i):
            r = rows_at(plane * piece + i * 32, 32)
            total = own_sum[r, :].astype(f32)
            for k in range(planes - 1):
                total = total + got_b[rows_at(k * piece + i * 32, 32), :].astype(f32)
            own_sum[r, :] = total.astype(bf)
        take(own_sum.at[rows_at(plane * piece, piece)], mat_ref.at[rows_at(place * quarter + plane * piece, piece)], 8)
        for j in range(1, planes):
            mat_c(j, False).start()

    def matrices_spread():
        for j in range(1, planes):
            mat_c(j, True).wait_recv()
        for i in (1, 2, 3):
            mat_d(i, False).start()

    def matrices_end():
        for i in (1, 2, 3):
            mat_d(i, True).wait_recv()
            mat_d(i, False).wait_send()
            mat_a(i).wait_send()
        for j in range(1, planes):
            mat_b(j).wait_send()
            mat_c(j, False).wait_send()

    def vec_copy(level, k):
        if level == 0:
            return remote(vec_ref, vec_in.at[k - 1], va_s.at[k - 1], va_r.at[k - 1], mate(k), h)
        return remote(vec_ref, vec_in.at[2 + k], vb_s.at[k - 1], vb_r.at[k - 1], layer(k), h)

    def vectors_start(level):
        for k in range(1, (4, planes)[level]):
            vec_copy(level, k).start()

    def vectors_sum(level):
        count = (4, planes)[level]
        for k in range(1, count):
            vec_copy(level, k).wait()
        total = vec_ref[...]
        for k in range(1, count):
            total = total + vec_in[(0, 3)[level] + k - 1]
        vec_ref[...] = total

    s1_start(0)
    s1_start(1)
    own_g.start()
    tok_start(1)

    @pl.when(jnp.logical_not(wide(zl)))
    def _():
        w_all[:, :, pl.ds(span - LANES, LANES)] = jnp.zeros((3, w_all.shape[1], LANES), bf)

    def recur_forward(xin, rg, ig, conv, ext, prod, run):
        load = pltpu.make_async_copy(x_ref, xin, loc.at[chunks, 0])
        load.start()
        load.wait()

        def normed(r, count):
            full = xin[pl.ds(r, count), :].astype(f32)
            scale = lax.rsqrt(jnp.sum(full * full, axis=1, keepdims=True) * (1.0 / model) + EPS)
            scales[0, pl.ds(r, count), :] = jnp.broadcast_to(scale, (count, LANES))
            own = xin[pl.ds(r, count), mine].astype(f32)
            return ((own * scale) * gain_ref[:, mine]).astype(bf).astype(f32)

        for q in range(sequences):
            halos[0, 0, q] = normed(q * length + length - 16, 16)[8:]
        pl.when(s + 1 < seq_count)(halo_copy(0).start)
        for q in range(sequences):
            @pl.loop(0, length // 16)
            def _(i, q=q):
                r = pl.multiple_of(i * 16, 16)
                ext[q, pl.ds(8 + r, 16), :] = normed(pl.multiple_of(q * length + r, 16), 16)

        @pl.when(s > 0)
        def _():
            halo_copy(0).wait_recv()
            for q in range(sequences):
                ext[q, pl.ds(0, 8), :] = halos[0, 1, q]

        @pl.when(s == 0)
        def _():
            for q in range(sequences):
                ext[q, pl.ds(0, 8), :] = jnp.zeros((8, half), f32)

        saves = [pltpu.make_async_copy(ext, ext_keep, keep.at[0])]
        saves[0].start()
        s1_wait(0)
        z_start(0)
        s1_start(2)

        @pl.loop(0, heads)
        def _(n):
            lanes = head_lanes(n)
            for q in range(sequences):
                total = cb_ref[:, lanes]
                for k in range(4):
                    total = total + cw_ref[pl.ds(k, 1), lanes] * ext[q, pl.ds(8 - k, length), lanes]
                conv[pl.ds(q * length, length), lanes] = total.astype(bf)
            low = conv[:, lanes]
            rg[:, lanes] = jax.nn.sigmoid(dot_nn(low, rw_ref[n]) + rb_ref[:, lanes])
            ig[:, lanes] = jax.nn.sigmoid(dot_nn(low, iw_ref[n]) + ib_ref[:, lanes])

            @pl.loop(0, tokens // 64)
            def _(i):
                r = pl.ds(pl.multiple_of(i * 64, 64), 64)
                log_decay = -8.0 * rate_ref[:, lanes] * rg[r, lanes]
                prod[r, lanes] = jnp.exp(log_decay)
                mult = jnp.sqrt(one_minus_square(log_decay))
                run[r, lanes] = mult * ig[r, lanes] * conv[r, lanes].astype(f32)

        for i, (src, dst) in enumerate(((rg, rg_keep), (ig, ig_keep), (conv, conv_keep))):
            saves.append(pltpu.make_async_copy(src, dst, keep.at[1 + i]))
            saves[-1].start()
        s1_wait(1)
        z_start(1)
        s1_start(3)

        def scan_group(g, carry):
            out = []
            for q in range(sequences):
                r = pl.ds(pl.multiple_of(q * length + g * 8, 8), 8)
                a_, b_ = prod[r, :], run[r, :]
                for k in (1, 2, 4):
                    inside = row_ids >= k
                    b_ = b_ + a_ * shifted(b_, k, inside, 0.0)
                    a_ = a_ * shifted(a_, k, inside, 1.0)
                b_ = b_ + a_ * carry[2 * q]
                a_ = a_ * carry[2 * q + 1]
                prod[r, :] = a_
                run[r, :] = b_
                out += [b_[7:8], a_[7:8]]
            return tuple(out)

        first = []
        for q in range(sequences):
            first += [jnp.zeros((1, half), f32), jnp.ones((1, half), f32)]
        last = lax.fori_loop(0, groups, scan_group, tuple(first))
        for q in range(sequences):
            ends_all[0, s, pl.ds(q, 1), :] = last[2 * q + 1]
            ends_all[0, s, pl.ds(sequences + q, 1), :] = last[2 * q]

        @pl.loop(1, seq_count)
        def _(q):
            pl.when(s + q < seq_count)(lambda: end_copy(0, s + q, s).start())

        tok_turn(1)
        ent[...] = jnp.zeros_like(ent)

        @pl.loop(0, seq_count)
        def _(source):
            @pl.when(source < s)
            def _():
                end_copy(0, s, source).wait_recv()
                got = ends_all[0, source]
                ent[...] = got[:sequences] * ent[...] + got[sequences:]

        for q in range(sequences):
            @pl.loop(0, length // 16)
            def _(i, q=q):
                r = pl.ds(pl.multiple_of(q * length + i * 16, 16), 16)
                state = run[r, :] + prod[r, :] * ent[pl.ds(q, 1), :]
                run[r, :] = state
                residual = xin[r, mine].astype(f32) + state.astype(bf).astype(f32)
                prod[r, :] = residual
                part[0, r, :] = jnp.broadcast_to(jnp.sum(residual * residual, axis=1, keepdims=True), (16, LANES))

        part_copy(0).start()
        for i, (src, dst) in enumerate(((run, state_keep), (prod, res_keep))):
            saves.append(pltpu.make_async_copy(src, dst, keep.at[4 + i]))
            saves[-1].start()
        part_copy(0).wait_recv()

        @pl.loop(0, tokens // 16)
        def _(i):
            r = pairs(i)
            scale = lax.rsqrt((part[0, r, :] + part_in[0, r, :]) * (1.0 / model) + EPS)
            scales[1, r, :] = scale
            ld[r, :] = ((prod[r, :] * scale[:, :1]) * mgain_ref[:, mine]).astype(bf)

        saves.append(pltpu.make_async_copy(ld, xn_half, keep.at[6]))
        saves[-1].start()
        for save in saves:
            save.wait()

    pl.run_scoped(
        recur_forward,
        pltpu.VMEM((tokens, model), bf), pltpu.VMEM((tokens, half), f32), pltpu.VMEM((tokens, half), f32),
        pltpu.VMEM((tokens, half), bf), pltpu.VMEM((sequences, length + 8, half), f32),
        pltpu.VMEM((tokens, half), f32), pltpu.VMEM((tokens, half), f32),
    )
    tok_start(0)
    own_x.start()
    s1_wait(2)
    z_start(2)
    s1_wait(3)
    z_start(3)
    own_x.wait()
    fwd_copy(0, 0, False).start()
    z_forward(0)
    own_g.wait()
    tok_turn(0)
    tok_last(1)
    z_forward(1)
    z_forward(2)
    tok_last(0)
    tok_wait(1)
    tok_wait(0)

    stage = (x_all, g_all)
    steps = half // 256

    def slot(k):
        return pl.ds(pl.multiple_of(k * tokens, 32), tokens)

    def sib_copy(which, k):
        return remote(
            stage[which].at[slot(k), pl.ds(0, half)], sib_ref.at[which, k], sib_s.at[which, k], sib_r.at[which, k],
            s, 1 - h,
        )

    def peer_copy(which, k):
        zl_step, x_step = k // 2, 1 - k // 2
        seq = seq_of(zh, (zl + zl_step) % 2, y, (x + x_step) % 2)
        return remote(
            stage[which].at[slot(k), pl.ds(half, half)], peer_ref.at[which, k], peer_s.at[which, k], peer_r.at[which, k],
            seq, h,
        )

    def fetch(src):
        load = pltpu.make_async_copy(src, ld, loc.at[chunks, 0])
        load.start()
        load.wait()

    def add_slot(which, k, src):
        fetch(src)

        @pl.loop(0, tokens // 64)
        def _(i):
            r = pl.ds(pl.multiple_of(k * tokens + i * 64, 64), 64)
            lanes = pl.ds(half, half)
            total = stage[which][r, lanes].astype(f32) + ld[pl.ds(pl.multiple_of(i * 64, 64), 64), :].astype(f32)
            stage[which][r, lanes] = total.astype(bf)

    def combine(which, k):
        sib_copy(which, k).wait_recv()
        add_slot(which, k, sib_ref.at[which, k])
        if k == 2:
            peer_copy(which, 0).wait_recv()
            add_slot(which, k, peer_ref.at[which, 0])
        peer_copy(which, k).start()

    def compute_sums(which, k, hid, gg, gu):
        zl_step, x_step = 1 - k % 2, 1 - k // 2
        r = tok_rows(((zl + zl_step) % 2) * 2 + (x + x_step) % 2)

        def one(side, base_col):
            @pl.loop(0, steps)
            def _(j):
                dr = pl.ds(pl.multiple_of(side * half + j * 256, 256), 256)
                value = product(which, r, dr, hid, gg, gu)
                stage[which][slot(k), pl.ds(pl.multiple_of(base_col + j * 256, 256), 256)] = value.astype(bf)

        one(1 - h, 0)
        sib_copy(which, k).start()
        one(h, half)

    def feed_forward(hid, gg, gu, dv, va, vb):
        @pl.loop(0, chunks)
        def _(c):
            y_wait(c)
            forward_chunk(c, hid, gg, gu)
            weight_chunk(c, hid, gg, gu, dv)
            away, near = range(1, far), (0,)
            pl.when(c == 0)(lambda: r1_start(0, away))

            @pl.when(c == 1)
            def _():
                z_forward(3)
                r1_start(0, near)

            pl.when(c >= 1)(lambda: r1_start(c, (*away, *near)))

        for k in (0, 1, 2, 3):
            for d in (1, 2, 3) if k == 0 else ():
                for i in (0, 1):
                    tok_copy(i, d, False).wait_send()
                    fwd_copy(i, d, False).wait_send()
            if k == 0:
                fwd_copy(0, 0, False).wait_send()
            compute_sums(0, k, hid, gg, gu)
            if k in (1, 2):
                combine(0, k - 1)
            if k == 1:
                near_all(0, va, vb)

        @pl.loop(0, 4)
        def _(k):
            compute_sums(1, k, hid, gg, gu)
        combine(0, 2)
        near_all(1, va, vb)
        sum_far(0, va, vb)

    wide_buf = pltpu.VMEM((4 * tokens, span), bf)
    pl.run_scoped(
        feed_forward, wide_buf, wide_buf, wide_buf, pltpu.VMEM((3, model, CHUNK), bf),
        pltpu.VMEM((3, 2 * pair, CHUNK), bf), pltpu.VMEM((3, 2 * pair, CHUNK), bf),
    )
    pl.loop(0, chunks)(zy_drain)
    held = 2 * pair
    va, vb = w_all.at[:, pl.ds(0, held), pl.ds(0, CHUNK)], w_all.at[:, pl.ds(held, held), pl.ds(0, CHUNK)]

    def recur_backward(fin, adj, gres, rg, ig, gconv, ext, wsum):
        spare = [x_all.at[slot(k), pl.ds(0, half)] for k in range(4)]
        for k in range(4):
            sib_copy(0, k).wait_send()
        conv, own_x_half, own_g_half = spare[0], spare[1], spare[2]
        loads = [
            pltpu.make_async_copy(conv_keep, conv, keep.at[0]),
            pltpu.make_async_copy(x_ref.at[:, mine], own_x_half, keep.at[1]),
            pltpu.make_async_copy(g_ref.at[:, mine], own_g_half, keep.at[2]),
            pltpu.make_async_copy(rg_keep, rg, keep.at[3]),
            pltpu.make_async_copy(ig_keep, ig, keep.at[4]),
            pltpu.make_async_copy(res_keep, adj, keep.at[5]),
        ]
        for q in range(sequences):
            loads.append(pltpu.make_async_copy(
                state_keep.at[pl.ds(q * length, length)], ext.at[q, pl.ds(8, length)], keep.at[6 + q]
            ))
        for load in loads:
            load.start()

        def widen(first):
            @pl.loop(0, tokens // 64)
            def _(i):
                r = pl.ds(pl.multiple_of(i * 64, 64), 64)
                if first:
                    own = x_all[pl.ds(pl.multiple_of(3 * tokens + i * 64, 64), 64), pl.ds(half, half)]
                    fin[r, :] = own.astype(f32) + ld[r, :].astype(f32)
                else:
                    fin[r, :] += ld[r, :].astype(f32)

        sib_copy(0, 3).wait_recv()
        fetch(sib_ref.at[0, 3])
        widen(True)
        peer_copy(0, 1).wait_recv()
        fetch(peer_ref.at[0, 1])
        widen(False)
        combine(1, 0)
        combine(1, 1)
        vec_ref[...] = jnp.zeros_like(vec_ref)
        for load in loads:
            load.wait()
        for q in range(sequences):
            ext[q, pl.ds(0, 8), :] = jnp.broadcast_to(ent[pl.ds(q, 1), :], (8, half))

            @pl.loop(0, length // 16)
            def _(i, q=q):
                r = pl.ds(pl.multiple_of(q * length + i * 16, 16), 16)
                gconv[q, pairs(i), :] = jnp.exp(-8.0 * rate_ref[...] * rg[r, :])
        peer_copy(0, 2).wait_recv()
        fetch(peer_ref.at[0, 2])
        widen(False)

        @pl.loop(0, tokens // 16)
        def _(i):
            r = pairs(i)
            hat = adj[r, :] * scales[1, r, :1]
            product_ = fin[r, :] * hat
            vec_ref[pl.ds(9, 1), :] += jnp.sum(product_, axis=0, keepdims=True)
            part[1, r, :] = jnp.broadcast_to(jnp.sum(product_ * mgain_ref[:, mine], axis=1, keepdims=True), (16, LANES))

        part_copy(1).start()
        part_copy(1).wait_recv()

        @pl.loop(0, tokens // 16)
        def _(i):
            r = pairs(i)
            scale = scales[1, r, :1]
            hat = adj[r, :] * scale
            mean = ((part[1, r, :] + part_in[1, r, :]) * (1.0 / model))[:, :1]
            own = x_all[pl.ds(pl.multiple_of(2 * tokens + i * 16, 16), 16), pl.ds(0, half)].astype(f32)
            gres[r, :] = own + scale * (fin[r, :] * mgain_ref[:, mine] - hat * mean)

        def scan_group(i, carry):
            g = groups - 1 - i
            out = []
            for q in range(sequences):
                t = pl.multiple_of(g * 8, 8)
                r = pl.ds(pl.multiple_of(q * length + t, 8), 8)
                here = gconv[q, pl.ds(t, 8), :]
                a_, b_ = shifted(here, -1, row_ids < 7, carry[3 * q + 2]), gres[r, :]
                for k in (1, 2, 4):
                    inside = row_ids < 8 - k
                    b_ = b_ + a_ * shifted(b_, -k, inside, 0.0)
                    a_ = a_ * shifted(a_, -k, inside, 1.0)
                b_ = b_ + a_ * carry[3 * q]
                a_ = a_ * carry[3 * q + 1]
                fin[r, :] = a_
                adj[r, :] = b_
                out += [b_[:1], a_[:1], here[:1]]
            return tuple(out)

        first = []
        for q in range(sequences):
            one = jnp.ones((1, half), f32)
            first += [jnp.zeros((1, half), f32), one, one]
        last = lax.fori_loop(0, groups, scan_group, tuple(first))
        for q in range(sequences):
            ends_all[1, s, pl.ds(q, 1), :] = last[3 * q + 1] * last[3 * q + 2]
            ends_all[1, s, pl.ds(sequences + q, 1), :] = last[3 * q] * last[3 * q + 2]

        @pl.loop(1, seq_count)
        def _(q):
            pl.when(s >= q)(lambda: end_copy(1, jnp.maximum(s - q, 0), s).start())

        arr[...] = jnp.zeros_like(arr)

        @pl.loop(1, seq_count)
        def _(q):
            source = seq_count - q

            @pl.when(source > s)
            def _():
                end_copy(1, s, source).wait_recv()
                got = ends_all[1, source]
                arr[...] = got[:sequences] * arr[...] + got[sequences:]

        for q in range(sequences):
            @pl.loop(0, length // 16)
            def _(i, q=q):
                r = pl.ds(pl.multiple_of(q * length + i * 16, 16), 16)
                adj[r, :] += fin[r, :] * arr[pl.ds(q, 1), :]

        near_all(2, va, vb)
        combine(1, 2)
        sum_far(1, va, vb)

        @pl.loop(0, heads)
        def _(n):
            lanes = head_lanes(n)
            rate = rate_ref[:, lanes]
            sums = [jnp.zeros((1, block), f32)] * 3
            for q in range(sequences):
                for i in range(2):
                    count = length // 2
                    t = i * count
                    r = pl.ds(q * length + t, count)
                    rg_, ig_ = rg[r, lanes], ig[r, lanes]
                    low = x_all[r, lanes]
                    conv_ = low.astype(f32)
                    a_ = adj[r, lanes]
                    log_decay = -8.0 * rate * rg_
                    decay = jnp.exp(log_decay)
                    mult = jnp.sqrt(one_minus_square(log_decay))
                    previous = ext[q, pl.ds(7 + t, count), lanes]
                    grad_mult = a_ * ig_ * conv_
                    grad_log = a_ * previous * decay - grad_mult * decay * decay / mult
                    pre_r = (grad_log * (-8.0 * rate) * rg_ * (1.0 - rg_)).astype(bf)
                    pre_i = (a_ * mult * conv_ * ig_ * (1.0 - ig_)).astype(bf)
                    sums[0] = sums[0] + jnp.sum(grad_log * rg_, axis=0, keepdims=True)
                    sums[1] = sums[1] + jnp.sum(pre_r.astype(f32), axis=0, keepdims=True)
                    sums[2] = sums[2] + jnp.sum(pre_i.astype(f32), axis=0, keepdims=True)
                    back = contract_last(pre_r, rw_ref[n]) + contract_last(pre_i, iw_ref[n])
                    gconv[q, pl.ds(t, count), lanes] = (a_ * mult * ig_ + back).astype(bf).astype(f32)
                    if q == 0 and i == 0:
                        wsum[0] = contract_first(low, pre_r)
                        wsum[1] = contract_first(low, pre_i)
                    else:
                        wsum[0] += contract_first(low, pre_r)
                        wsum[1] += contract_first(low, pre_i)
            for k in range(2):
                mat[rows_at((k * heads + n) * block, block), :] = wsum[k].astype(bf)
            vec_ref[pl.ds(8, 1), lanes] = sums[0] * 8.0 * sig_ref[:, lanes]
            vec_ref[pl.ds(6, 1), lanes] = sums[1]
            vec_ref[pl.ds(7, 1), lanes] = sums[2]

        for q in range(sequences):
            halos[1, 0, q] = gconv[q, pl.ds(0, 8), :]
        pl.when(s > 0)(halo_copy(1).start)
        matrices_start()
        again = pltpu.make_async_copy(ext_keep, ext, keep.at[2])
        again.start()
        again.wait()

        @pl.loop(0, heads)
        def _(n):
            lanes = head_lanes(n)
            for k in range(5):
                total = jnp.zeros((1, block), f32)
                for q in range(sequences):
                    value = gconv[q, pl.ds(0, length), lanes]
                    if k < 4:
                        value = value * ext[q, pl.ds(8 - k, length), lanes]
                    total = total + jnp.sum(value, axis=0, keepdims=True)
                vec_ref[pl.ds(1 + k, 1), lanes] = total

        matrices_plane()

        @pl.when(s + 1 < seq_count)
        def _():
            halo_copy(1).wait_recv()
            for q in range(sequences):
                gconv[q, pl.ds(length, 8), :] = halos[1, 1, q]

        @pl.when(s + 1 == seq_count)
        def _():
            for q in range(sequences):
                gconv[q, pl.ds(length, 8), :] = jnp.zeros((8, half), f32)

        @pl.loop(0, heads)
        def _(n):
            lanes = head_lanes(n)
            for q in range(sequences):
                total = cw_ref[pl.ds(0, 1), lanes] * gconv[q, pl.ds(0, length), lanes]
                for k in range(1, 4):
                    total = total + cw_ref[pl.ds(k, 1), lanes] * gconv[q, pl.ds(k, length), lanes]
                adj[pl.ds(q * length, length), lanes] = total

        def own_rows(i):
            return x_all[pl.ds(pl.multiple_of(tokens + i * 16, 16), 16), pl.ds(0, half)].astype(f32)

        @pl.loop(0, tokens // 16)
        def _(i):
            r = pairs(i)
            product_ = adj[r, :] * (own_rows(i) * scales[0, r, :1])
            vec_ref[pl.ds(0, 1), :] += jnp.sum(product_, axis=0, keepdims=True)
            part[2, r, :] = jnp.broadcast_to(jnp.sum(product_ * gain_ref[:, mine], axis=1, keepdims=True), (16, LANES))

        part_copy(2).start()
        vectors_start(0)
        matrices_across()
        part_copy(2).wait_recv()

        @pl.loop(0, tokens // 16)
        def _(i):
            r = pairs(i)
            scale = scales[0, r, :1]
            hat = own_rows(i) * scale
            mean = ((part[2, r, :] + part_in[2, r, :]) * (1.0 / model))[:, :1]
            fin[r, :] = gres[r, :] + scale * (adj[r, :] * gain_ref[:, mine] - hat * mean)

        near = pltpu.make_async_copy(fin, ingrad_ref.at[:, mine], keep.at[3])
        near.start()
        away = remote(fin, ingrad_ref.at[:, mine], fin_s.at[0], fin_r.at[0], s, 1 - h)
        away.start()
        vectors_sum(0)
        vectors_start(1)
        matrices_spread()
        near_all(3, va, vb)
        sum_far(2, va, vb)

        res = pltpu.make_async_copy(res_keep, rg, keep.at[4])
        res.start()
        res.wait()

        def absorb(src):
            fetch(src)

            @pl.loop(0, tokens // 64)
            def _(i):
                r = pl.ds(pl.multiple_of(i * 64, 64), 64)
                rg[r, :] += ld[r, :].astype(f32)

        sib_copy(1, 3).wait_recv()
        absorb(sib_ref.at[1, 3])
        for k in (1, 2):
            peer_copy(1, k).wait_recv()
            absorb(peer_ref.at[1, k])

        @pl.loop(0, tokens // 64)
        def _(i):
            r = pl.ds(pl.multiple_of(i * 64, 64), 64)
            own = g_all[pl.ds(pl.multiple_of(3 * tokens + i * 64, 64), 64), pl.ds(half, half)]
            ld[r, :] = (rg[r, :] + own.astype(f32)).astype(bf)

        near_out = pltpu.make_async_copy(ld, out_ref.at[:, mine], keep.at[4])
        near_out.start()
        away_out = remote(ld, out_ref.at[:, mine], fin_s.at[1], fin_r.at[1], s, 1 - h)
        away_out.start()
        sum_far(3, va, vb)
        vectors_sum(1)
        matrices_end()
        near.wait()
        near_out.wait()
        away.wait()
        away_out.wait()

    act = pltpu.VMEM((tokens, half), f32)
    padded = pltpu.VMEM((sequences, length + 8, half), f32)
    pl.run_scoped(
        recur_backward, act, act, act, act, act, padded, padded, pltpu.VMEM((2, block, block), f32),
    )

    @pl.loop(0, chunks)
    def _(c):
        s1_drain(c)
        for zh_ in range(far):
            for zl_ in range(2):
                r1_copy(c, zh_, zl_, False).wait_send()
        for q in range(1, far):
            for zl_ in range(2):
                r2_copy(c, q, zl_).wait_send()

        def sent(width):
            for d in (1, 2, 3):
                c3_copy(c, d, width, False).wait_send()
            c3_own(c, width).wait()
        by_width(c, wide(zl), sent)
        for d in (1, 2, 3):
            by_width(c, wide(peer(d)[2]), lambda width, d=d: c3_copy(c, d, width, True).wait_recv())
    for k in range(4):
        sib_copy(1, k).wait_send()
    for which in range(2):
        for k in range(3):
            peer_copy(which, k).wait_send()
    for i in range(3):
        part_copy(i).wait_send()
    pl.when(s + 1 < seq_count)(halo_copy(0).wait_send)
    pl.when(s > 0)(halo_copy(1).wait_send)

    @pl.loop(1, seq_count)
    def _(q):
        pl.when(s + q < seq_count)(lambda: end_copy(0, s + q, s).wait_send())
        pl.when(s >= q)(lambda: end_copy(1, jnp.maximum(s - q, 0), s).wait_send())


def block_pass(seq_count, sequences, x, cotangent, norm_gain, conv_weight, conv_bias, recur_weight, recur_bias,
               input_weight, input_bias, decay_param, mlp_gain, w_gate, w_up, w_down):
    tokens, width = x.shape
    half = width // 2
    length = tokens // sequences
    rows, units = w_gate.shape
    pair, far = 2 * rows, seq_count // 8
    chunks = -(-units // (4 * CHUNK))
    span = chunks * CHUNK
    matrix = (2 * recur_weight.shape[0] * recur_weight.shape[1], recur_weight.shape[2])
    planes = seq_count // 4
    bf, f32 = jnp.bfloat16, jnp.float32
    any_space = pl.BlockSpec(memory_space=pl.ANY)
    vmem = pl.BlockSpec(memory_space=pltpu.VMEM)
    outs = [
        ((tokens, width), bf), ((tokens, width), f32), ((3, rows, units), bf), ((16, half), f32), (matrix, bf),
        ((chunks, 3, width, CHUNK), bf), ((chunks, 3, 2 * far * pair, CHUNK), bf), ((chunks, 3, 2 * far * pair, CHUNK), bf),
        ((chunks, far - 1, 3, 2 * pair, CHUNK), bf), ((chunks, 3, 2 * pair, CHUNK), bf),
        ((2, 4, tokens, half), bf), ((2, 3, tokens, half), bf),
        ((tokens, half), bf), ((tokens, half), f32), ((tokens, half), f32), ((tokens, half), bf),
        ((sequences, length + 8, half), f32), ((tokens, half), f32), ((tokens, half), f32),
        ((3 * matrix[0] // 4, matrix[1]), bf), ((matrix[0] // 4 // planes * (planes - 1), matrix[1]), bf),
    ]
    sem = pltpu.SemaphoreType.DMA
    scratch = [
        pltpu.VMEM((4 * tokens, width), bf), pltpu.VMEM((4 * tokens, width), bf), pltpu.VMEM((3, width, span), bf),
        pltpu.VMEM((tokens, half), bf), pltpu.VMEM((2, 2, sequences, 8, half), f32),
        pltpu.VMEM((2, seq_count, 2 * sequences, half), f32), pltpu.VMEM((sequences, half), f32),
        pltpu.VMEM((sequences, half), f32), pltpu.VMEM((3, tokens, LANES), f32), pltpu.VMEM((3, tokens, LANES), f32),
        pltpu.VMEM((2, tokens, LANES), f32), pltpu.VMEM((2 + planes, 16, half), f32),
    ]
    for shape in (
        (2, 3), (2, 4), (chunks, 3, 3), (chunks, far - 1, 2), (chunks, far, 2), (chunks, far, 2),
        (chunks, far - 1, 2), (chunks, 3), (2, 4), (2, 3), (2,), (2, seq_count), (3,), (2,),
        (3,), (planes - 1,), (planes - 1,), (3,), (3,), (planes - 1,),
    ):
        scratch += [sem(shape), sem(shape)]
    scratch += [sem((6 + sequences,)), sem((chunks + 1 + far, 3))]
    rate = jax.nn.softplus(-decay_param)[None]
    slope = jax.nn.sigmoid(-decay_param)[None]
    results = pl.pallas_call(
        functools.partial(block_kernel, seq_count, sequences),
        out_shape=[jax.ShapeDtypeStruct(shape, kind) for shape, kind in outs],
        in_specs=[any_space] * 5 + [vmem] * 10,
        out_specs=[any_space] * 3 + [vmem] + [any_space] * (len(outs) - 4),
        scratch_shapes=scratch,
        compiler_params=pltpu.CompilerParams(
            collective_id=0, has_side_effects=True, vmem_limit_bytes=64 * 2**20 - 2**18
        ),
        cost_estimate=pl.CostEstimate(
            flops=18 * 4 * tokens * width * span, bytes_accessed=150 * 2**20, transcendentals=4 * tokens * span
        ),
        name="block_pass",
    )(x, cotangent, w_gate, w_up, w_down, norm_gain[None], conv_weight, conv_bias[None], recur_weight,
      recur_bias[None], input_weight, input_bias[None], rate, slope, mlp_gain[None])
    return results[:5]


def gathered_shards(
    block_input,
    norm_gain,
    conv_weight,
    conv_bias,
    recur_weight,
    recur_bias,
    input_weight,
    input_bias,
    decay_param,
    mlp_gain,
    w_gate,
    w_up,
    w_down,
    out_grad,
):
    sequences, span_len, model_width = block_input.shape
    lru_width = conv_bias.shape[0]
    heads_here = recur_weight.shape[0]
    block_width = recur_weight.shape[1]
    token_rows = sequences * span_len
    head_at = lax.axis_index("head")
    stream = block_input.astype(jnp.float32)
    first_scale, first_hat = norm_rows(stream)
    xn_first = (first_hat * norm_gain).astype(jnp.bfloat16)
    own_input = lax.dynamic_slice_in_dim(xn_first, head_at * lru_width, lru_width, 2)
    edge_rows = from_behind(own_input[:, span_len - 3 :, :], "seq", 1)
    padded = jnp.concatenate([edge_rows, own_input], axis=1).astype(jnp.float32)
    conv_sum = conv_bias + conv_weight[0] * padded[:, 3 : 3 + span_len]
    for offset in range(1, 4):
        conv_sum = conv_sum + conv_weight[offset] * padded[:, 3 - offset : 3 - offset + span_len]
    conv_out = conv_sum.astype(jnp.bfloat16)
    conv_blocks = conv_out.reshape(token_rows, heads_here, block_width)
    recur_pre = (
        jnp.einsum(
            "tnh,nhk->tnk", conv_blocks, recur_weight, preferred_element_type=jnp.float32
        ).reshape(sequences, span_len, lru_width)
        + recur_bias
    )
    input_pre = (
        jnp.einsum(
            "tnh,nhk->tnk", conv_blocks, input_weight, preferred_element_type=jnp.float32
        ).reshape(sequences, span_len, lru_width)
        + input_bias
    )
    recur_gate = jax.nn.sigmoid(recur_pre)
    input_gate = jax.nn.sigmoid(input_pre)
    rate = jax.nn.softplus(-decay_param)
    log_decay = -8.0 * rate * recur_gate
    decay = jnp.exp(log_decay)
    multiplier = jnp.sqrt(-jnp.expm1(2.0 * log_decay))
    conv_float = conv_out.astype(jnp.float32)
    pushed = multiplier * input_gate * conv_float
    decay_prod, local_state = lax.associative_scan(link_forward, (decay, pushed), axis=1)
    ones_edge = jnp.ones((sequences, lru_width), jnp.float32)
    zeros_edge = jnp.zeros((sequences, lru_width), jnp.float32)
    entering = prefix(
        (decay_prod[:, -1], local_state[:, -1]), "seq", link_forward, (ones_edge, zeros_edge), False
    )
    state = local_state + decay_prod * entering[1][:, None, :]
    state_full = lax.all_gather(state.astype(jnp.bfloat16), "head", axis=2, tiled=True)
    residual = stream + state_full.astype(jnp.float32)
    second_scale, second_hat = norm_rows(residual)
    xn_second = (second_hat * mlp_gain).astype(jnp.bfloat16).reshape(token_rows, model_width)
    hidden_width = w_gate.shape[1]
    pieces = (
        lax.all_gather(w_gate, "seq", axis=0, tiled=True),
        lax.all_gather(w_up, "seq", axis=0, tiled=True),
    )
    columns = xn_second
    gate = jnp.dot(columns, pieces[0], preferred_element_type=jnp.float32)
    up_value = jnp.dot(columns, pieces[1], preferred_element_type=jnp.float32)
    activated, gelu_back = jax.vjp(jax.nn.gelu, gate)
    hidden = (activated * up_value).astype(jnp.bfloat16)
    partial_mix = contract_last(hidden, lax.all_gather(w_down, "seq", axis=0, tiled=True))
    mixed = lax.psum(partial_mix, "head")
    block_output = (
        (residual.reshape(token_rows, model_width) + mixed)
        .astype(jnp.bfloat16)
        .reshape(block_input.shape)
    )
    cotangent = out_grad.reshape(token_rows, model_width)
    columns = cotangent
    grad_hidden = jnp.dot(
        columns,
        lax.all_gather(w_down, "seq", axis=0, tiled=True),
        preferred_element_type=jnp.float32,
    )
    grad_gate = gelu_back(grad_hidden * up_value)[0].astype(jnp.bfloat16)
    grad_up = (grad_hidden * activated).astype(jnp.bfloat16)
    pieces = (
        lax.all_gather(w_gate, "seq", axis=0, tiled=True),
        lax.all_gather(w_up, "seq", axis=0, tiled=True),
    )
    block_value = contract_last(grad_gate, pieces[0]) + contract_last(grad_up, pieces[1])
    grad_xn_second = lax.psum(block_value, "head").reshape(block_input.shape)
    stacked = jnp.concatenate([grad_gate, grad_up], axis=1)
    local_rows = w_gate.shape[0]
    seq_count = lax.axis_size("seq")
    turns = math.gcd(local_rows, 8)
    per_turn = local_rows // turns
    input_view = xn_second.reshape(token_rows, seq_count, local_rows)
    grad_view = cotangent.reshape(token_rows, seq_count, local_rows)

    def grad_turn(turn, collected):
        first_row = turn * per_turn
        input_cols = lax.dynamic_slice_in_dim(input_view, first_row, per_turn, 2).reshape(
            token_rows, seq_count * per_turn
        )
        grad_cols = lax.dynamic_slice_in_dim(grad_view, first_row, per_turn, 2).reshape(
            token_rows, seq_count * per_turn
        )
        term = jnp.concatenate(
            [contract_first(input_cols, stacked), contract_first(grad_cols, hidden)], axis=1
        )
        share = lax.psum_scatter(term, "seq", scatter_dimension=0, tiled=True)
        return lax.dynamic_update_slice_in_dim(collected, share, first_row, 0)

    weight_grads = lax.fori_loop(
        0, turns, grad_turn, jnp.zeros((local_rows, 3 * hidden_width), jnp.float32)
    )
    w_gate_grad = weight_grads[:, :hidden_width]
    w_up_grad = weight_grads[:, hidden_width : 2 * hidden_width]
    w_down_grad = weight_grads[:, 2 * hidden_width :]
    weighted_second = grad_xn_second * mlp_gain
    mlp_gain_local = jnp.sum(grad_xn_second * second_hat, axis=(0, 1))
    grad_residual = out_grad.astype(jnp.float32) + second_scale * (
        weighted_second
        - second_hat * jnp.mean(weighted_second * second_hat, axis=-1, keepdims=True)
    )
    grad_state = lax.dynamic_slice_in_dim(grad_residual, head_at * lru_width, lru_width, 2)
    next_decay = jnp.concatenate([decay[:, 1:], jnp.ones_like(decay[:, :1])], axis=1)
    flipped = lax.associative_scan(
        link_forward, (jnp.flip(next_decay, 1), jnp.flip(grad_state, 1)), axis=1
    )
    after_prod = jnp.flip(flipped[0], 1)
    local_adjoint = jnp.flip(flipped[1], 1)
    leaving = (decay_prod[:, -1], decay[:, 0] * local_adjoint[:, 0])
    arriving = prefix(leaving, "seq", link_backward, (ones_edge, zeros_edge), True)
    adjoint = local_adjoint + after_prod * arriving[1][:, None, :]
    previous = jnp.concatenate([entering[1][:, None, :], state[:, :-1]], axis=1)
    grad_mult = adjoint * input_gate * conv_float
    grad_log = adjoint * previous * decay - grad_mult * decay * decay / multiplier
    grad_recur_pre = (grad_log * (-8.0 * rate) * recur_gate * (1.0 - recur_gate)).astype(
        jnp.bfloat16
    )
    grad_input_pre = (adjoint * multiplier * conv_float * input_gate * (1.0 - input_gate)).astype(
        jnp.bfloat16
    )
    decay_local = jnp.sum(grad_log * 8.0 * recur_gate, axis=(0, 1)) * jax.nn.sigmoid(-decay_param)
    recur_blocks = grad_recur_pre.reshape(token_rows, heads_here, block_width)
    input_blocks = grad_input_pre.reshape(token_rows, heads_here, block_width)
    back_gates = jnp.einsum(
        "tnk,nhk->tnh", recur_blocks, recur_weight, preferred_element_type=jnp.float32
    )
    back_gates = back_gates + jnp.einsum(
        "tnk,nhk->tnh", input_blocks, input_weight, preferred_element_type=jnp.float32
    )
    grad_conv = (
        adjoint * multiplier * input_gate + back_gates.reshape(sequences, span_len, lru_width)
    ).astype(jnp.bfloat16)
    recur_weight_local = jnp.einsum(
        "tnh,tnk->nhk", conv_blocks, recur_blocks, preferred_element_type=jnp.float32
    )
    input_weight_local = jnp.einsum(
        "tnh,tnk->nhk", conv_blocks, input_blocks, preferred_element_type=jnp.float32
    )
    recur_bias_local = jnp.sum(grad_recur_pre.astype(jnp.float32), axis=(0, 1))
    input_bias_local = jnp.sum(grad_input_pre.astype(jnp.float32), axis=(0, 1))
    later_rows = from_behind(grad_conv[:, :3, :], "seq", -1)
    grad_padded = jnp.concatenate([grad_conv, later_rows], axis=1).astype(jnp.float32)
    grad_conv_float = grad_conv.astype(jnp.float32)
    grad_own_input = conv_weight[0] * grad_padded[:, 0:span_len]
    for offset in range(1, 4):
        grad_own_input = (
            grad_own_input + conv_weight[offset] * grad_padded[:, offset : offset + span_len]
        )
    conv_weight_local = jnp.stack(
        [
            jnp.sum(grad_conv_float * padded[:, 3 - offset : 3 - offset + span_len], axis=(0, 1))
            for offset in range(4)
        ]
    )
    conv_bias_local = jnp.sum(grad_conv_float, axis=(0, 1))
    grad_xn_first = lax.all_gather(
        grad_own_input.astype(jnp.bfloat16), "head", axis=2, tiled=True
    ).astype(grad_own_input.dtype)
    weighted_first = grad_xn_first * norm_gain
    norm_gain_local = jnp.sum(grad_xn_first * first_hat, axis=(0, 1))
    input_grad = grad_residual + first_scale * (
        weighted_first - first_hat * jnp.mean(weighted_first * first_hat, axis=-1, keepdims=True)
    )
    summed = lax.psum(
        (
            norm_gain_local,
            conv_weight_local,
            conv_bias_local,
            recur_weight_local,
            recur_bias_local,
            input_weight_local,
            input_bias_local,
            decay_local,
            mlp_gain_local,
        ),
        "seq",
    )
    return (
        block_output,
        input_grad,
        summed[0],
        summed[1],
        summed[2],
        summed[3],
        summed[4],
        summed[5],
        summed[6],
        summed[7],
        summed[8],
        w_gate_grad,
        w_up_grad,
        w_down_grad,
    )


def shards(
    block_input,
    norm_gain,
    conv_weight,
    conv_bias,
    recur_weight,
    recur_bias,
    input_weight,
    input_bias,
    decay_param,
    mlp_gain,
    w_gate,
    w_up,
    w_down,
    out_grad,
):
    seq_count = lax.axis_size("seq")
    sequences, span_len, width = block_input.shape
    if seq_count % 8 or w_gate.shape[0] % 32:
        return gathered_shards(
            block_input, norm_gain, conv_weight, conv_bias, recur_weight, recur_bias, input_weight, input_bias,
            decay_param, mlp_gain, w_gate, w_up, w_down, out_grad,
        )
    rows = sequences * span_len
    stream = block_input.reshape(rows, width)
    cotangent = out_grad.reshape(rows, width)
    block_output, input_grad, weight_grads, vectors, matrices = block_pass(
        seq_count, sequences, stream, cotangent, norm_gain, conv_weight, conv_bias, recur_weight, recur_bias,
        input_weight, input_bias, decay_param, mlp_gain, w_gate, w_up, w_down,
    )
    matrices = matrices.astype(jnp.float32).reshape(2, *recur_weight.shape)
    gains = lax.all_gather(jnp.stack([vectors[0], vectors[9]]), "head", axis=1, tiled=True)
    return (
        block_output.reshape(block_input.shape),
        input_grad.reshape(block_input.shape),
        gains[0],
        vectors[1:5],
        vectors[5],
        matrices[0],
        vectors[6],
        matrices[1],
        vectors[7],
        vectors[8],
        gains[1],
        weight_grads[0].astype(jnp.float32),
        weight_grads[1].astype(jnp.float32),
        weight_grads[2].astype(jnp.float32),
    )


def solution(mesh):
    placed = (
        P(None, "seq", None),
        P(),
        P(None, "head"),
        P("head"),
        P("head", None, None),
        P("head"),
        P("head", None, None),
        P("head"),
        P("head"),
        P(),
        P("seq", "head"),
        P("seq", "head"),
        P("seq", "head"),
        P(None, "seq", None),
    )
    return jax.shard_map(
        shards,
        mesh=mesh,
        in_specs=placed,
        out_specs=(
            P(None, "seq", None),
            P(None, "seq", None),
            P(),
            P(None, "head"),
            P("head"),
            P("head", None, None),
            P("head"),
            P("head", None, None),
            P("head"),
            P("head"),
            P(),
            P("seq", "head"),
            P("seq", "head"),
            P("seq", "head"),
        ),
        check_vma=False,
    )
```

```python
import functools
import math

import jax
import jax.numpy as jnp
from jax import lax
from jax.experimental import pallas as pl
from jax.experimental.pallas import tpu as pltpu
from jax.sharding import PartitionSpec as P

EPS = 1e-06
MESH = pl.DeviceIdType.MESH
LANES = 128
CHUNK = 256


def from_behind(value, axis, steps):
    count = lax.axis_size(axis)
    initial, last = (max(0, -steps), min(count, count - steps))
    return lax.ppermute(value, axis, [(source, source + steps) for source in range(initial, last)])


def prefix(part, axis, combine, identity, reverse):
    count = lax.axis_size(axis)
    place = lax.axis_index(axis)
    ahead = count - 1 - place if reverse else place
    gathered = jax.tree.map(lambda a: lax.all_gather(a, axis), part)
    state = jax.tree.map(lambda a, e: jnp.zeros_like(a) + jnp.asarray(e, a.dtype), part, identity)

    def one(lap, state):
        source = count - 1 - lap if reverse else lap
        return combine(
            state, jax.tree.map(lambda a: lax.dynamic_index_in_dim(a, source, 0, False), gathered)
        )

    return lax.fori_loop(0, ahead, one, state)


def norm_rows(values):
    scale = lax.rsqrt(jnp.mean(values * values, axis=-1, keepdims=True) + EPS)
    return (scale, values * scale)


def link_forward(earlier, latter):
    return (earlier[0] * latter[0], latter[0] * earlier[1] + latter[1])


def link_backward(earlier, latter):
    return (earlier[0] * latter[0], latter[1] + latter[0] * earlier[1])


def contract_last(left_side, right_side):
    return lax.dot_general(
        left_side, right_side, (((1,), (1,)), ((), ())), preferred_element_type=jnp.float32
    )


def contract_first(left_side, right_side):
    return lax.dot_general(
        left_side, right_side, (((0,), (0,)), ((), ())), preferred_element_type=jnp.float32
    )


def dot_nn(left_side, right_side):
    return jnp.dot(left_side, right_side, preferred_element_type=jnp.float32)


def remote(src, dst, send, recv, seq, head):
    return pltpu.make_async_remote_copy(
        src_ref=src, dst_ref=dst, send_sem=send, recv_sem=recv,
        device_id={"seq": seq, "head": head}, device_id_type=MESH,
    )


def half_window(head, half):
    return pl.ds(pl.multiple_of(head * half, LANES), half)


def greet_all(seq_count, s, h):
    barrier = pltpu.get_barrier_semaphore()

    @pl.loop(1, seq_count)
    def _(q):
        seq = (s + q) % seq_count
        pl.semaphore_signal(barrier, inc=1, device_id={"seq": seq, "head": h}, device_id_type=MESH)

    pl.semaphore_signal(barrier, inc=1, device_id={"seq": s, "head": 1 - h}, device_id_type=MESH)
    pl.semaphore_wait(barrier, seq_count)


def one_minus_square(log_decay):
    twice = 2.0 * log_decay
    series = 1.0 + twice * (1 / 2 + twice * (1 / 6 + twice * (1 / 24 + twice * (1 / 120 + twice * (1 / 720)))))
    return jnp.where(twice > -0.25, -twice * series, 1.0 - jnp.exp(twice))


def shifted(value, step, keep, fill):
    return jnp.where(keep, pltpu.roll(value, step % 8, 0), fill)


def block_kernel(
    seq_count, sequences, x_ref, g_ref, wg_ref, wu_ref, wd_ref,
    prm_ref, rw_ref, iw_ref,
    out_ref, ingrad_ref, dw_ref, vec_ref, mat_ref,
    dh_ref, r1_ref, e_ref, r2_ref, sib_ref, peer_ref, xn_half, rg_keep, ig_keep, conv_keep, ext_keep, state_keep,
    res_keep, ma_ref, mb_ref,
    x_all, g_all, w_all, ld, halos, ends_all, ent, arr, part, part_in, scales, vec_in,
    tok_s, tok_r, fwd_s, fwd_r, s1_s, s1_r, z_s, z_r, y_s, y_r, c1_s, c1_r, c2_s, c2_r, c3_s, c3_r,
    sib_s, sib_r, peer_s, peer_r, halo_s, halo_r, end_s, end_r, part_s, part_r, fin_s, fin_r, ma_s, ma_r, mb_s, mb_r, mc_s, mc_r, md_s, md_r, va_s, va_r, vb_s, vb_r, sums, keep, loc,
):
    far = seq_count // 8
    rows = wg_ref.shape[0]
    pair = 2 * rows
    tokens, half = x_ref.shape[0], x_ref.shape[1] // 2
    span = w_all.shape[2]
    chunks = span // CHUNK
    tiles = wg_ref.shape[1] // LANES
    base, extra = tiles // 4, tiles % 4
    s = lax.axis_index("seq")
    h = lax.axis_index("head")
    x = s % 2
    y = (s // 2) % 2
    zl = (s // 4) % 2
    zh = s // 8
    a = zl * 2 + x
    weights = (wg_ref, wu_ref, wd_ref)

    def seq_of(zh_, zl_, y_, x_):
        return ((zh_ * 2 + zl_) * 2 + y_) * 2 + x_

    def peer(d):
        zl_, x_ = (zl + d // 2) % 2, (x + d % 2) % 2
        return zl_ * 2 + x_, seq_of(zh, zl_, y, x_), zl_, x_

    def first_tile(a_):
        low = base * a_ + jnp.minimum(a_, extra)
        high = base * a_ + jnp.maximum(a_ - (4 - extra), 0)
        return jnp.where(h == 0, low, high)

    def wide(zl_):
        return zl_ == h

    def block_rows(zh_, zl_, y_):
        return pl.ds(pl.multiple_of(((zh_ * 2 + zl_) * 2 + y_) * pair, 32), pair)

    def cols(c, width=CHUNK):
        return pl.ds(pl.multiple_of(c * CHUNK, CHUNK), width)

    def by_width(c, is_wide, run):
        narrow = (c == chunks - 1) & jnp.logical_not(is_wide)
        pl.when(narrow)(lambda: run(LANES))
        pl.when(jnp.logical_not(narrow))(lambda: run(CHUNK))

    y_seq = seq_of(zh, zl, 1 - y, x)

    def z_seq(q):
        return seq_of((zh + q) % far, zl, y, x)

    model = 2 * half
    length = tokens // sequences
    groups = length // 8
    mine = half_window(h, half)
    block = rw_ref.shape[1]
    heads = half // block
    f32, bf = jnp.float32, jnp.bfloat16
    gain_ref, mgain_ref, cb_ref, rb_ref, ib_ref, rate_ref, sig_ref = [prm_ref.at[pl.ds(i, 1)] for i in range(7)]
    cw_ref = prm_ref.at[pl.ds(8, 4)]
    greet_all(seq_count, s, h)

    def s1_send(c, d, w, width):
        a_, seq, zl_, _ = peer(d)
        col = pl.multiple_of((first_tile(a_) + 2 * c) * LANES, LANES)
        return remote(
            weights[w].at[:, pl.ds(col, width)],
            w_all.at[w, pl.ds(pl.multiple_of(s * rows, 32), rows), cols(c, width)],
            s1_s.at[c, d - 1, w], s1_r.at[c, d - 1, w], seq, h,
        )

    def s1_recv(c, d, w, width):
        _, seq, _, _ = peer(d)
        return remote(
            weights[w].at[:, pl.ds(0, width)],
            w_all.at[w, pl.ds(pl.multiple_of(seq * rows, 32), rows), cols(c, width)],
            s1_s.at[c, d - 1, w], s1_r.at[c, d - 1, w], seq, h,
        )

    def s1_own(c, w, width):
        col = pl.multiple_of((first_tile(a) + 2 * c) * LANES, LANES)
        return pltpu.make_async_copy(
            weights[w].at[:, pl.ds(col, width)],
            w_all.at[w, pl.ds(pl.multiple_of(s * rows, 32), rows), cols(c, width)],
            loc.at[c, w],
        )

    def s1_start(c):
        for d in (1, 2, 3):
            def go(width, d=d):
                for w in range(3):
                    s1_send(c, d, w, width).start()
            by_width(c, wide(peer(d)[2]), go)

        def own(width):
            for w in range(3):
                s1_own(c, w, width).start()
        by_width(c, wide(zl), own)

    def s1_wait(c):
        def got(width):
            for w in range(3):
                s1_own(c, w, width).wait()
                for d in (1, 2, 3):
                    s1_recv(c, d, w, width).wait_recv()
        by_width(c, wide(zl), got)

    def s1_drain(c):
        for d in (1, 2, 3):
            def go(width, d=d):
                for w in range(3):
                    s1_send(c, d, w, width).wait_send()
            by_width(c, wide(peer(d)[2]), go)

    def z_copy(c, q, zl_, width, incoming):
        zh_ = (zh - q + far) % far if incoming else zh
        part = w_all.at[:, block_rows(zh_, zl_, y), cols(c, width)]
        return remote(part, part, z_s.at[c, q - 1, zl_], z_r.at[c, q - 1, zl_], z_seq(q), h)

    def y_copy(c, q, zl_, width, incoming):
        part = w_all.at[:, block_rows((zh - q + far) % far, zl_, 1 - y if incoming else y), cols(c, width)]
        return remote(part, part, y_s.at[c, q, zl_], y_r.at[c, q, zl_], y_seq, h)

    def z_start(c, halves=(0, 1)):
        def go(width):
            for zl_ in halves:
                for q in range(1, far):
                    z_copy(c, q, zl_, width, False).start()
                y_copy(c, 0, zl_, width, False).start()
        by_width(c, wide(zl), go)

    def z_forward(c):
        def go(width):
            for q in range(1, far):
                for zl_ in range(2):
                    z_copy(c, q, zl_, width, True).wait_recv()
                    y_copy(c, q, zl_, width, False).start()
        by_width(c, wide(zl), go)

    def y_wait(c):
        def go(width):
            for q in range(far):
                for zl_ in range(2):
                    y_copy(c, q, zl_, width, True).wait_recv()
        by_width(c, wide(zl), go)

    def zy_drain(c):
        def go(width):
            for zl_ in range(2):
                for q in range(1, far):
                    z_copy(c, q, zl_, width, False).wait_send()
                for q in range(far):
                    y_copy(c, q, zl_, width, False).wait_send()
        by_width(c, wide(zl), go)

    half_cols = pl.ds(pl.multiple_of(h * half, LANES), half)

    def tok_rows(a_):
        return pl.ds(pl.multiple_of(a_ * tokens, 32), tokens)

    def tok_copy(k, d, incoming):
        src = xn_half if k == 0 else g_ref.at[:, half_cols]
        dst = (x_all, g_all)[k]
        here = a
        if d == 3:
            here = peer(2)[0]
            src = dst.at[tok_rows(here), half_cols]
        return remote(
            src, dst.at[tok_rows(peer(d)[0] if incoming else here), half_cols],
            tok_s.at[k, d - 1], tok_r.at[k, d - 1], peer(1 if d == 3 else d)[1], h,
        )

    def fwd_copy(k, d, incoming):
        dst = (x_all, g_all)[k]
        side = pl.ds(pl.multiple_of((1 - h if incoming else h) * half, LANES), half)
        part = dst.at[tok_rows(peer(d)[0]), side]
        return remote(part, part, fwd_s.at[k, d], fwd_r.at[k, d], s, 1 - h)

    own_x = pltpu.make_async_copy(xn_half, x_all.at[tok_rows(a), half_cols], loc.at[chunks, 0])
    own_g = pltpu.make_async_copy(g_ref, g_all.at[tok_rows(a), :], loc.at[chunks, 1])

    def tok_start(k):
        tok_copy(k, 2, False).start()
        tok_copy(k, 1, False).start()

    def tok_turn(k):
        tok_copy(k, 2, True).wait_recv()
        tok_copy(k, 3, False).start()
        fwd_copy(k, 2, False).start()

    def tok_last(k):
        for d in (1, 3):
            tok_copy(k, d, True).wait_recv()
            fwd_copy(k, d, False).start()

    def tok_wait(k):
        for d in ((1, 2, 3) if k else (0, 1, 2, 3)):
            fwd_copy(k, d, True).wait_recv()

    def r1_copy(c, zh_, zl_, width):
        lanes = pl.ds(0, width)
        return remote(
            dh_ref.at[c, :, block_rows(zh_, zl_, 1 - y), lanes],
            r1_ref.at[c, :, pl.ds(pl.multiple_of((zh_ * 2 + zl_) * pair, 32), pair), lanes],
            c1_s.at[c, zh_, zl_], c1_r.at[c, zh_, zl_], y_seq, h,
        )

    def r1_start(c, steps_away):
        def go(width):
            for q in steps_away:
                for zl_ in range(2):
                    r1_copy(c, (zh + q) % far, zl_, width).start()
        by_width(c, wide(zl), go)

    def plane_rows(zh_):
        return pl.ds(pl.multiple_of(zh_ * 2 * pair, 32), 2 * pair)

    def r2_copy(c, q, width, src=None):
        lanes = pl.ds(0, width)
        if src is None:
            src = e_ref.at[c, :, plane_rows((zh + q) % far), lanes]
        else:
            src = src.at[:, :, lanes]
        return remote(src, r2_ref.at[c, q - 1, :, :, lanes], c2_s.at[c, q - 1], c2_r.at[c, q - 1], z_seq(q), h)

    def r2_start(c, q, src=None):
        by_width(c, wide(zl), lambda width: r2_copy(c, q, width, src).start())

    def add_into(first, second):
        @pl.loop(0, 3)
        def _(w):
            @pl.loop(0, 2)
            def _(b):
                r = pl.ds(pl.multiple_of(b * pair, 32), pair)
                first[w, r, :] = first[w, r, :] + second[w, r, :]

    def near_loads(c, q, first, second):
        zh_ = (zh + q) % far
        loads = [
            pltpu.make_async_copy(
                dh_ref.at[c, :, block_rows(zh_, zl_, y), :], first.at[:, pl.ds(zl_ * pair, pair)], sums.at[c, q, zl_]
            )
            for zl_ in range(2)
        ]
        return loads + [pltpu.make_async_copy(r1_ref.at[c, :, plane_rows(zh_)], second, sums.at[c, q, 2])]

    def near_store(c, q, first):
        return pltpu.make_async_copy(first, e_ref.at[c, :, plane_rows((zh + q) % far)], sums.at[c, q, 3])

    def near_issue(c, q, first, second):
        def got(width):
            for zl_ in range(2):
                r1_copy(c, (zh + q) % far, zl_, width).wait_recv()
        by_width(c, wide(zl), got)
        for load in near_loads(c, q, first, second):
            load.start()

    def near_finish(c, q, first, second, direct):
        for load in near_loads(c, q, first, second):
            load.wait()
        add_into(first, second)
        if direct and q:
            r2_start(c, q, first)
        else:
            near_store(c, q, first).start()

    def near_send(c, q, first):
        near_store(c, q, first).wait()
        if q:
            r2_start(c, q)

    def far_loads(c, first, second):
        return [
            pltpu.make_async_copy(e_ref.at[c, :, plane_rows(zh)], first, sums.at[c, 0, 0]),
            pltpu.make_async_copy(r2_ref.at[c, 0], second, sums.at[c, 0, 1]),
        ]

    def far_issue(c, first, second):
        by_width(c, wide(zl), lambda width: r2_copy(c, 1, width).wait_recv())
        for load in far_loads(c, first, second):
            load.start()

    def far_finish(c, first, second):
        for load in far_loads(c, first, second):
            load.wait()
        add_into(first, second)

        def go(width):
            for d in (1, 2, 3):
                c3_copy(c, d, width, False, first).start()
            c3_own(c, width, first).start()
        by_width(c, wide(zl), go)

    def c3_copy(c, d, width, incoming, src):
        a_, seq, zl_, x_ = peer(d)
        col = pl.multiple_of((first_tile(a_ if incoming else a) + 2 * c) * LANES, LANES)
        return remote(
            src.at[:, pl.ds(pl.multiple_of((zl_ * 2 + x_) * rows, 32), rows), pl.ds(0, width)],
            dw_ref.at[:, :, pl.ds(col, width)],
            c3_s.at[c, d - 1], c3_r.at[c, d - 1], seq, h,
        )

    def c3_own(c, width, src):
        col = pl.multiple_of((first_tile(a) + 2 * c) * LANES, LANES)
        return pltpu.make_async_copy(
            src.at[:, pl.ds(pl.multiple_of(a * rows, 32), rows), pl.ds(0, width)],
            dw_ref.at[:, :, pl.ds(col, width)], loc.at[c, 0],
        )

    def forward_chunk(c, hid, gg, gu):
        @pl.loop(0, 4)
        def _(i):
            r = tok_rows(i)
            xb = x_all[r, :]
            gate = dot_nn(xb, w_all[0, :, cols(c)])
            up = dot_nn(xb, w_all[1, :, cols(c)])
            gh = dot_nn(g_all[r, :], w_all[2, :, cols(c)])
            k0, k1 = 0.7978845608028654, 0.044715
            th = jnp.tanh(k0 * (gate + k1 * gate * gate * gate))
            cdf = 0.5 * (1.0 + th)
            act = gate * cdf
            slope = cdf + 0.5 * gate * (1.0 - th * th) * k0 * (1.0 + 3.0 * k1 * gate * gate)
            hid[r, cols(c)] = (act * up).astype(jnp.bfloat16)
            gu[r, cols(c)] = (gh * act).astype(jnp.bfloat16)
            gg[r, cols(c)] = (gh * up * slope).astype(jnp.bfloat16)

    def weight_chunk(c, hid, gg, gu, dv):
        for w, (left, right) in enumerate(((x_all, gg), (x_all, gu), (g_all, hid))):
            @pl.loop(0, x_all.shape[1] // 512)
            def _(j):
                r = pl.ds(pl.multiple_of(j * 512, 512), 512)
                dv[w, r, :] = contract_first(left[:, r], right[:, cols(c)]).astype(jnp.bfloat16)
            pltpu.make_async_copy(dv.at[w], dh_ref.at[c, w], loc.at[chunks, w]).start()
        for w in range(3):
            pltpu.make_async_copy(dv.at[w], dh_ref.at[c, w], loc.at[chunks, w]).wait()

    def product(which, r, d_rows, hid, gg, gu):
        if which == 0:
            return contract_last(gg[r, :], w_all[0, d_rows, :]) + contract_last(gu[r, :], w_all[1, d_rows, :])
        return contract_last(hid[r, :], w_all[2, d_rows, :])

    def pairs(i):
        return pl.ds(pl.multiple_of(i * 16, 16), 16)

    def head_lanes(n):
        return pl.ds(pl.multiple_of(n * block, block), block)

    def near_copy(side, k, incoming):
        source = (place - k + 4) % 4 if incoming else place
        part_ends = ends_all.at[side, source]
        return remote(part_ends, part_ends, end_s.at[side, k - 1], end_r.at[side, k - 1], mate(k), h)

    def far_copy(side, j, incoming):
        step = -j if (side == 0) == incoming else j
        source = plane + step if incoming else plane
        target = plane if incoming else plane + step
        bound = jnp.clip(source, 0, planes - 1), jnp.clip(target, 0, planes - 1)
        part_ends = ends_all.at[side, 4 + bound[0]]
        return remote(
            part_ends, part_ends, end_s.at[side, 2 + j], end_r.at[side, 2 + j], bound[1] * 4 + place, h
        )

    def far_exists(side, incoming, j):
        if (side == 0) == incoming:
            return plane >= j
        return plane + j < planes

    def ends_near(side):
        for k in (1, 2, 3):
            near_copy(side, k, False).start()

    def follow(total, got):
        return total[0] * got[:sequences], got[:sequences] * total[1] + got[sequences:]

    def ends_far(side):
        for k in (1, 2, 3):
            near_copy(side, k, True).wait_recv()
        order = range(4) if side == 0 else range(3, -1, -1)
        total = jnp.ones((sequences, half), f32), jnp.zeros((sequences, half), f32)
        for p in order:
            total = follow(total, ends_all[side, p])
        ends_all[side, 4 + plane, pl.ds(0, sequences), :] = total[0]
        ends_all[side, 4 + plane, pl.ds(sequences, sequences), :] = total[1]
        for j in range(1, planes):
            pl.when(far_exists(side, False, j))(far_copy(side, j, False).start)

    def ends_fold(side, out):
        out[...] = jnp.zeros_like(out)
        for j in range(planes - 1, 0, -1):
            @pl.when(far_exists(side, True, j))
            def _(j=j):
                far_copy(side, j, True).wait_recv()
                got = ends_all[side, 4 + (jnp.maximum(plane - j, 0) if side == 0 else jnp.minimum(plane + j, planes - 1))]
                out[...] = got[:sequences] * out[...] + got[sequences:]
        for p in range(4) if side == 0 else range(3, -1, -1):
            @pl.when(p < place if side == 0 else p > place)
            def _(p=p):
                got = ends_all[side, p]
                out[...] = got[:sequences] * out[...] + got[sequences:]

    def ends_drain(side):
        for k in (1, 2, 3):
            near_copy(side, k, False).wait_send()
        for j in range(1, planes):
            pl.when(far_exists(side, False, j))(far_copy(side, j, False).wait_send)

    def part_copy(i):
        return remote(part.at[i], part_in.at[i], part_s.at[i], part_r.at[i], s, 1 - h)

    def halo_copy(side):
        target = jnp.minimum(s + 1, seq_count - 1) if side == 0 else jnp.maximum(s - 1, 0)
        return remote(halos.at[side, 0], halos.at[side, 1], halo_s.at[side], halo_r.at[side], target, h)

    row_ids = lax.broadcasted_iota(jnp.int32, (8, half), 0)

    place, plane, planes = s % 4, s // 4, seq_count // 4
    quarter = 2 * heads * block // 4
    piece = quarter // planes
    mat = w_all.at[0, pl.ds(0, 4 * quarter), pl.ds(2 * CHUNK, block)]
    got_a = w_all.at[1, pl.ds(0, 3 * quarter), pl.ds(2 * CHUNK, block)]
    got_b = w_all.at[2, pl.ds(quarter, (planes - 1) * piece), pl.ds(2 * CHUNK, block)]
    own_sum = w_all.at[2, pl.ds(0, quarter), pl.ds(2 * CHUNK, block)]

    def mate(i):
        return plane * 4 + (place + i) % 4

    def layer(j):
        return (plane + j) % planes * 4 + place

    def rows_at(start, count):
        return pl.ds(pl.multiple_of(start, 32), count)

    def mat_a(i):
        return remote(
            mat.at[rows_at((place + i) % 4 * quarter, quarter)], ma_ref.at[pl.ds((i - 1) * quarter, quarter)],
            ma_s.at[i - 1], ma_r.at[i - 1], mate(i), h,
        )

    def mat_b(j):
        return remote(
            own_sum.at[rows_at((plane + j) % planes * piece, piece)], mb_ref.at[pl.ds((j - 1) * piece, piece)],
            mb_s.at[j - 1], mb_r.at[j - 1], layer(j), h,
        )

    def mat_c(j, incoming):
        source = (plane - j + planes) % planes if incoming else plane
        part_rows = mat_ref.at[rows_at(place * quarter + source * piece, piece)]
        return remote(part_rows, part_rows, mc_s.at[j - 1], mc_r.at[j - 1], layer(j), h)

    def mat_d(i, incoming):
        source = (place - i + 4) % 4 if incoming else place
        part_rows = mat_ref.at[rows_at(source * quarter, quarter)]
        return remote(part_rows, part_rows, md_s.at[i - 1], md_r.at[i - 1], mate(i), h)

    def take(src, dst, i):
        load = pltpu.make_async_copy(src, dst, keep.at[i])
        load.start()
        load.wait()

    def matrices_start():
        for i in (1, 2, 3):
            mat_a(i).start()

    def matrices_plane():
        for i in (1, 2, 3):
            mat_a(i).wait_recv()
        take(ma_ref, got_a, 8)

        @pl.loop(0, quarter // 32)
        def _(i):
            total = mat[rows_at(place * quarter + i * 32, 32), :].astype(f32)
            for k in range(3):
                total = total + got_a[rows_at(k * quarter + i * 32, 32), :].astype(f32)
            own_sum[rows_at(i * 32, 32), :] = total.astype(bf)
        for j in range(1, planes):
            mat_b(j).start()

    def matrices_across():
        for j in range(1, planes):
            mat_b(j).wait_recv()
        take(mb_ref, got_b, 8)

        @pl.loop(0, piece // 32)
        def _(i):
            r = rows_at(plane * piece + i * 32, 32)
            total = own_sum[r, :].astype(f32)
            for k in range(planes - 1):
                total = total + got_b[rows_at(k * piece + i * 32, 32), :].astype(f32)
            own_sum[r, :] = total.astype(bf)
        take(own_sum.at[rows_at(plane * piece, piece)], mat_ref.at[rows_at(place * quarter + plane * piece, piece)], 8)
        for j in range(1, planes):
            mat_c(j, False).start()

    def matrices_spread():
        for j in range(1, planes):
            mat_c(j, True).wait_recv()
        for i in (1, 2, 3):
            mat_d(i, False).start()

    def matrices_end():
        for i in (1, 2, 3):
            mat_d(i, True).wait_recv()
            mat_d(i, False).wait_send()
            mat_a(i).wait_send()
        for j in range(1, planes):
            mat_b(j).wait_send()
            mat_c(j, False).wait_send()

    def vec_copy(level, k):
        if level == 0:
            return remote(vec_ref, vec_in.at[k - 1], va_s.at[k - 1], va_r.at[k - 1], mate(k), h)
        return remote(vec_ref, vec_in.at[2 + k], vb_s.at[k - 1], vb_r.at[k - 1], layer(k), h)

    def vectors_start(level):
        for k in range(1, (4, planes)[level]):
            vec_copy(level, k).start()

    def vectors_sum(level):
        count = (4, planes)[level]
        for k in range(1, count):
            vec_copy(level, k).wait()
        total = vec_ref[...]
        for k in range(1, count):
            total = total + vec_in[(0, 3)[level] + k - 1]
        vec_ref[...] = total

    own_g.start()

    @pl.when(jnp.logical_not(wide(zl)))
    def _():
        w_all[:, :, pl.ds(span - LANES, LANES)] = jnp.zeros((3, w_all.shape[1], LANES), bf)

    def recur_forward(xin, rg, ig, conv, ext, prod, run):
        load = pltpu.make_async_copy(x_ref, xin, loc.at[chunks, 0])
        load.start()
        load.wait()

        def normed(r, count):
            full = xin[pl.ds(r, count), :].astype(f32)
            scale = lax.rsqrt(jnp.sum(full * full, axis=1, keepdims=True) * (1.0 / model) + EPS)
            scales[0, pl.ds(r, count), :] = jnp.broadcast_to(scale, (count, LANES))
            own = xin[pl.ds(r, count), mine].astype(f32)
            return ((own * scale) * gain_ref[...]).astype(bf).astype(f32)

        for q in range(sequences):
            halos[0, 0, q] = normed(q * length + length - 16, 16)[8:]
        pl.when(s + 1 < seq_count)(halo_copy(0).start)
        s1_start(0)
        s1_start(1)
        for q in range(sequences):
            @pl.loop(0, length // 16)
            def _(i, q=q):
                r = pl.multiple_of(i * 16, 16)
                ext[q, pl.ds(8 + r, 16), :] = normed(pl.multiple_of(q * length + r, 16), 16)

        @pl.when(s > 0)
        def _():
            halo_copy(0).wait_recv()
            for q in range(sequences):
                ext[q, pl.ds(0, 8), :] = halos[0, 1, q]

        @pl.when(s == 0)
        def _():
            for q in range(sequences):
                ext[q, pl.ds(0, 8), :] = jnp.zeros((8, half), f32)

        saves = [pltpu.make_async_copy(ext, ext_keep, keep.at[0])]
        saves[0].start()
        @pl.loop(0, heads)
        def _(n):
            lanes = head_lanes(n)
            for q in range(sequences):
                total = cb_ref[:, lanes]
                for k in range(4):
                    total = total + cw_ref[pl.ds(k, 1), lanes] * ext[q, pl.ds(8 - k, length), lanes]
                conv[pl.ds(q * length, length), lanes] = total.astype(bf)
            low = conv[:, lanes]
            rg[:, lanes] = jax.nn.sigmoid(dot_nn(low, rw_ref[n]) + rb_ref[:, lanes])
            ig[:, lanes] = jax.nn.sigmoid(dot_nn(low, iw_ref[n]) + ib_ref[:, lanes])

            @pl.loop(0, tokens // 64)
            def _(i):
                r = pl.ds(pl.multiple_of(i * 64, 64), 64)
                log_decay = -8.0 * rate_ref[:, lanes] * rg[r, lanes]
                prod[r, lanes] = jnp.exp(log_decay)
                mult = jnp.sqrt(one_minus_square(log_decay))
                run[r, lanes] = mult * ig[r, lanes] * conv[r, lanes].astype(f32)

        for i, (src, dst) in enumerate(((rg, rg_keep), (ig, ig_keep), (conv, conv_keep))):
            saves.append(pltpu.make_async_copy(src, dst, keep.at[1 + i]))
            saves[-1].start()

        def scan_group(g, carry):
            out = []
            for q in range(sequences):
                r = pl.ds(pl.multiple_of(q * length + g * 8, 8), 8)
                a_, b_ = prod[r, :], run[r, :]
                for k in (1, 2, 4):
                    inside = row_ids >= k
                    b_ = b_ + a_ * shifted(b_, k, inside, 0.0)
                    a_ = a_ * shifted(a_, k, inside, 1.0)
                b_ = b_ + a_ * carry[2 * q]
                a_ = a_ * carry[2 * q + 1]
                prod[r, :] = a_
                run[r, :] = b_
                out += [b_[7:8], a_[7:8]]
            return tuple(out)

        first = []
        for q in range(sequences):
            first += [jnp.zeros((1, half), f32), jnp.ones((1, half), f32)]
        last = lax.fori_loop(0, groups, scan_group, tuple(first))
        for q in range(sequences):
            ends_all[0, place, pl.ds(q, 1), :] = last[2 * q + 1]
            ends_all[0, place, pl.ds(sequences + q, 1), :] = last[2 * q]
        ends_near(0)
        ends_far(0)
        s1_wait(0)
        z_start(0)
        tok_start(1)
        own_g.wait()
        ends_fold(0, ent)

        for q in range(sequences):
            @pl.loop(0, length // 16)
            def _(i, q=q):
                r = pl.ds(pl.multiple_of(q * length + i * 16, 16), 16)
                state = run[r, :] + prod[r, :] * ent[pl.ds(q, 1), :]
                run[r, :] = state
                residual = xin[r, mine].astype(f32) + state.astype(bf).astype(f32)
                prod[r, :] = residual
                part[0, r, :] = jnp.broadcast_to(jnp.sum(residual * residual, axis=1, keepdims=True), (16, LANES))

        part_copy(0).start()
        for i, (src, dst) in enumerate(((run, state_keep), (prod, res_keep))):
            saves.append(pltpu.make_async_copy(src, dst, keep.at[4 + i]))
            saves[-1].start()
        part_copy(0).wait_recv()

        @pl.loop(0, tokens // 16)
        def _(i):
            r = pairs(i)
            scale = lax.rsqrt((part[0, r, :] + part_in[0, r, :]) * (1.0 / model) + EPS)
            scales[1, r, :] = scale
            ld[r, :] = ((prod[r, :] * scale[:, :1]) * mgain_ref[...]).astype(bf)

        saves.append(pltpu.make_async_copy(ld, xn_half, keep.at[6]))
        saves[-1].start()
        for save in saves:
            save.wait()

    pl.run_scoped(
        recur_forward,
        pltpu.VMEM((tokens, model), bf), pltpu.VMEM((tokens, half), f32), pltpu.VMEM((tokens, half), f32),
        pltpu.VMEM((tokens, half), bf), pltpu.VMEM((sequences, length + 8, half), f32),
        pltpu.VMEM((tokens, half), f32), pltpu.VMEM((tokens, half), f32),
    )
    tok_start(0)
    own_x.start()
    s1_start(2)
    s1_wait(1)
    z_start(1)
    own_x.wait()
    fwd_copy(0, 0, False).start()
    tok_turn(1)
    s1_start(3)
    z_forward(0)
    s1_wait(2)
    z_start(2)
    tok_last(1)
    tok_turn(0)
    z_forward(1)
    s1_wait(3)
    z_start(3)
    tok_last(0)
    tok_wait(1)
    tok_wait(0)

    stage = (x_all, g_all)
    steps = half // 256

    def slot(k):
        return pl.ds(pl.multiple_of(k * tokens, 32), tokens)

    def sib_copy(which, k):
        return remote(
            stage[which].at[slot(k), pl.ds(0, half)], sib_ref.at[which, k], sib_s.at[which, k], sib_r.at[which, k],
            s, 1 - h,
        )

    def peer_copy(which, k):
        zl_step, x_step = k // 2, 1 - k // 2
        seq = seq_of(zh, (zl + zl_step) % 2, y, (x + x_step) % 2)
        return remote(
            stage[which].at[slot(k), pl.ds(half, half)], peer_ref.at[which, k], peer_s.at[which, k], peer_r.at[which, k],
            seq, h,
        )

    def fetch(src):
        load = pltpu.make_async_copy(src, ld, loc.at[chunks, 0])
        load.start()
        load.wait()

    def add_slot(which, k, src):
        fetch(src)

        @pl.loop(0, tokens // 64)
        def _(i):
            r = pl.ds(pl.multiple_of(k * tokens + i * 64, 64), 64)
            lanes = pl.ds(half, half)
            stage[which][r, lanes] = stage[which][r, lanes] + ld[pl.ds(pl.multiple_of(i * 64, 64), 64), :]

    def combine(which, k):
        sib_copy(which, k).wait_recv()
        add_slot(which, k, sib_ref.at[which, k])
        if k == 2:
            peer_copy(which, 0).wait_recv()
            add_slot(which, k, peer_ref.at[which, 0])
        peer_copy(which, k).start()

    def compute_sums(which, k, hid, gg, gu):
        zl_step, x_step = 1 - k % 2, 1 - k // 2
        r = tok_rows(((zl + zl_step) % 2) * 2 + (x + x_step) % 2)

        def one(side, base_col):
            @pl.loop(0, steps)
            def _(j):
                dr = pl.ds(pl.multiple_of(side * half + j * 256, 256), 256)
                value = product(which, r, dr, hid, gg, gu)
                stage[which][slot(k), pl.ds(pl.multiple_of(base_col + j * 256, 256), 256)] = value.astype(bf)

        one(1 - h, 0)
        sib_copy(which, k).start()
        one(h, half)

    def feed_forward(hid, gg, gu, dv, sum_bufs):
        bufs = [(sum_bufs.at[0], sum_bufs.at[1]), (sum_bufs.at[2], sum_bufs.at[3])]

        @pl.loop(0, chunks)
        def _(c):
            y_wait(c)
            forward_chunk(c, hid, gg, gu)
            weight_chunk(c, hid, gg, gu, dv)
            away, near = range(1, far), (0,)


            @pl.when(c == 0)
            def _():
                z_forward(2)
                r1_start(0, away)

            @pl.when(c == 1)
            def _():
                z_forward(3)
                r1_start(0, near)

            pl.when((c >= 1) & (c < chunks - 1))(lambda: r1_start(c, (*away, *near)))
            pl.when(c == chunks - 1)(lambda: r1_start(c, away))

        for k in (0, 1, 2, 3):
            for d in (1, 2, 3) if k == 0 else ():
                for i in (0, 1):
                    tok_copy(i, d, False).wait_send()
                    fwd_copy(i, d, False).wait_send()
            if k == 0:
                fwd_copy(0, 0, False).wait_send()
            if k == 2:
                near_issue(0, 1, *bufs[0])
            if k == 3:
                near_finish(0, 1, *bufs[0], False)
            compute_sums(0, k, hid, gg, gu)
            if k in (1, 2):
                combine(0, k - 1)
        near_send(0, 1, bufs[0][0])
        near_issue(0, 0, *bufs[1])
        compute_sums(1, 0, hid, gg, gu)
        near_finish(0, 0, *bufs[1], False)
        compute_sums(1, 1, hid, gg, gu)
        combine(0, 2)
        near_issue(1, 1, *bufs[0])
        compute_sums(1, 2, hid, gg, gu)
        near_finish(1, 1, *bufs[0], False)
        near_send(0, 0, bufs[1][0])
        compute_sums(1, 3, hid, gg, gu)
        near_send(1, 1, bufs[0][0])

    wide_buf = pltpu.VMEM((4 * tokens, span), bf)
    pl.run_scoped(
        feed_forward, wide_buf, wide_buf, wide_buf, pltpu.VMEM((3, model, CHUNK), bf),
        pltpu.VMEM((4, 3, 2 * pair, CHUNK), bf),
    )
    pl.loop(0, chunks)(zy_drain)
    held = 2 * pair

    def hold(row, col):
        return w_all.at[:, pl.ds(row * held, held), pl.ds(col * CHUNK, CHUNK)]

    near_slots = {
        (1, 0): (hold(0, 3), hold(1, 3)), (2, 1): (hold(0, 0), hold(1, 0)), (2, 0): (hold(2, 0), hold(3, 0)),
        (3, 1): (hold(0, 1), hold(1, 1)), (3, 0): (hold(2, 1), hold(3, 1)),
    }
    far_slots = [
        (hold(2, 3), hold(3, 3)), (hold(1, 3), hold(1, 0)), (hold(3, 0), hold(1, 1)), (hold(3, 1), hold(3, 3)),
    ]

    def near_first(c, q):
        near_issue(c, q, *near_slots[c, q])

    def near_last(c, q):
        near_finish(c, q, *near_slots[c, q], True)

    def recur_backward(fin, adj, gres, rg, ig, gconv, ext, wsum):
        spare = [x_all.at[slot(k), pl.ds(0, half)] for k in range(4)]
        for k in range(4):
            sib_copy(0, k).wait_send()
        conv, own_x_half, own_g_half = spare[0], spare[1], spare[2]
        loads = [
            pltpu.make_async_copy(conv_keep, conv, keep.at[0]),
            pltpu.make_async_copy(x_ref.at[:, mine], own_x_half, keep.at[1]),
            pltpu.make_async_copy(g_ref.at[:, mine], own_g_half, keep.at[2]),
            pltpu.make_async_copy(rg_keep, rg, keep.at[3]),
            pltpu.make_async_copy(ig_keep, ig, keep.at[4]),
            pltpu.make_async_copy(res_keep, adj, keep.at[5]),
        ]
        for q in range(sequences):
            loads.append(pltpu.make_async_copy(
                state_keep.at[pl.ds(q * length, length)], ext.at[q, pl.ds(8, length)], keep.at[6 + q]
            ))
        for load in loads:
            load.start()

        def widen(first):
            @pl.loop(0, tokens // 64)
            def _(i):
                r = pl.ds(pl.multiple_of(i * 64, 64), 64)
                if first:
                    own = x_all[pl.ds(pl.multiple_of(3 * tokens + i * 64, 64), 64), pl.ds(half, half)]
                    fin[r, :] = own.astype(f32) + ld[r, :].astype(f32)
                else:
                    fin[r, :] += ld[r, :].astype(f32)

        sib_copy(0, 3).wait_recv()
        fetch(sib_ref.at[0, 3])
        widen(True)
        peer_copy(0, 1).wait_recv()
        fetch(peer_ref.at[0, 1])
        widen(False)
        vec_ref[...] = jnp.zeros_like(vec_ref)
        for load in loads:
            load.wait()
        for q in range(sequences):
            ext[q, pl.ds(0, 8), :] = jnp.broadcast_to(ent[pl.ds(q, 1), :], (8, half))

            @pl.loop(0, length // 16)
            def _(i, q=q):
                r = pl.ds(pl.multiple_of(q * length + i * 16, 16), 16)
                gconv[q, pairs(i), :] = jnp.exp(-8.0 * rate_ref[...] * rg[r, :])
        near_first(1, 0)
        peer_copy(0, 2).wait_recv()
        fetch(peer_ref.at[0, 2])
        widen(False)
        near_last(1, 0)
        combine(1, 0)

        @pl.loop(0, tokens // 16)
        def _(i):
            r = pairs(i)
            hat = adj[r, :] * scales[1, r, :1]
            product_ = fin[r, :] * hat
            vec_ref[pl.ds(9, 1), :] += jnp.sum(product_, axis=0, keepdims=True)
            part[1, r, :] = jnp.broadcast_to(jnp.sum(product_ * mgain_ref[...], axis=1, keepdims=True), (16, LANES))

        part_copy(1).start()
        near_send(1, 0, near_slots[1, 0][0])
        far_issue(0, *far_slots[0])
        part_copy(1).wait_recv()

        @pl.loop(0, tokens // 16)
        def _(i):
            r = pairs(i)
            scale = scales[1, r, :1]
            hat = adj[r, :] * scale
            mean = ((part[1, r, :] + part_in[1, r, :]) * (1.0 / model))[:, :1]
            own = x_all[pl.ds(pl.multiple_of(2 * tokens + i * 16, 16), 16), pl.ds(0, half)].astype(f32)
            gres[r, :] = own + scale * (fin[r, :] * mgain_ref[...] - hat * mean)

        far_finish(0, *far_slots[0])

        def scan_group(i, carry):
            g = groups - 1 - i
            out = []
            for q in range(sequences):
                t = pl.multiple_of(g * 8, 8)
                r = pl.ds(pl.multiple_of(q * length + t, 8), 8)
                here = gconv[q, pl.ds(t, 8), :]
                a_, b_ = shifted(here, -1, row_ids < 7, carry[3 * q + 2]), gres[r, :]
                for k in (1, 2, 4):
                    inside = row_ids < 8 - k
                    b_ = b_ + a_ * shifted(b_, -k, inside, 0.0)
                    a_ = a_ * shifted(a_, -k, inside, 1.0)
                b_ = b_ + a_ * carry[3 * q]
                a_ = a_ * carry[3 * q + 1]
                fin[r, :] = a_
                adj[r, :] = b_
                out += [b_[:1], a_[:1], here[:1]]
            return tuple(out)

        first = []
        for q in range(sequences):
            one = jnp.ones((1, half), f32)
            first += [jnp.zeros((1, half), f32), one, one]
        last = lax.fori_loop(0, groups, scan_group, tuple(first))
        for q in range(sequences):
            ends_all[1, place, pl.ds(q, 1), :] = last[3 * q + 1] * last[3 * q + 2]
            ends_all[1, place, pl.ds(sequences + q, 1), :] = last[3 * q] * last[3 * q + 2]
        ends_near(1)
        ends_far(1)
        r1_start(chunks - 1, (0,))
        near_first(2, 1)
        combine(1, 1)
        ends_fold(1, arr)

        for q in range(sequences):
            @pl.loop(0, length // 16)
            def _(i, q=q):
                r = pl.ds(pl.multiple_of(q * length + i * 16, 16), 16)
                adj[r, :] += fin[r, :] * arr[pl.ds(q, 1), :]

        near_last(2, 1)
        near_first(2, 0)
        combine(1, 2)

        @pl.loop(0, heads)
        def _(n):
            lanes = head_lanes(n)
            rate = rate_ref[:, lanes]
            sums = [jnp.zeros((1, block), f32)] * 3
            for q in range(sequences):
                for i in range(2):
                    count = length // 2
                    t = i * count
                    r = pl.ds(q * length + t, count)
                    rg_, ig_ = rg[r, lanes], ig[r, lanes]
                    low = x_all[r, lanes]
                    conv_ = low.astype(f32)
                    a_ = adj[r, lanes]
                    log_decay = -8.0 * rate * rg_
                    decay = jnp.exp(log_decay)
                    mult = jnp.sqrt(one_minus_square(log_decay))
                    previous = ext[q, pl.ds(7 + t, count), lanes]
                    grad_mult = a_ * ig_ * conv_
                    grad_log = a_ * previous * decay - grad_mult * decay * decay / mult
                    pre_r = (grad_log * (-8.0 * rate) * rg_ * (1.0 - rg_)).astype(bf)
                    pre_i = (a_ * mult * conv_ * ig_ * (1.0 - ig_)).astype(bf)
                    sums[0] = sums[0] + jnp.sum(grad_log * rg_, axis=0, keepdims=True)
                    sums[1] = sums[1] + jnp.sum(pre_r.astype(f32), axis=0, keepdims=True)
                    sums[2] = sums[2] + jnp.sum(pre_i.astype(f32), axis=0, keepdims=True)
                    back = contract_last(pre_r, rw_ref[n]) + contract_last(pre_i, iw_ref[n])
                    gconv[q, pl.ds(t, count), lanes] = (a_ * mult * ig_ + back).astype(bf).astype(f32)
                    if q == 0 and i == 0:
                        wsum[0] = contract_first(low, pre_r)
                        wsum[1] = contract_first(low, pre_i)
                    else:
                        wsum[0] += contract_first(low, pre_r)
                        wsum[1] += contract_first(low, pre_i)
            for k in range(2):
                mat[rows_at((k * heads + n) * block, block), :] = wsum[k].astype(bf)
            vec_ref[pl.ds(8, 1), lanes] = sums[0] * 8.0 * sig_ref[:, lanes]
            vec_ref[pl.ds(6, 1), lanes] = sums[1]
            vec_ref[pl.ds(7, 1), lanes] = sums[2]

        near_last(2, 0)
        for q in range(sequences):
            halos[1, 0, q] = gconv[q, pl.ds(0, 8), :]
        pl.when(s > 0)(halo_copy(1).start)
        matrices_start()
        far_issue(1, *far_slots[1])
        near_send(2, 0, near_slots[2, 0][0])
        again = pltpu.make_async_copy(ext_keep, ext, keep.at[2])
        again.start()
        again.wait()

        @pl.loop(0, heads)
        def _(n):
            lanes = head_lanes(n)
            for k in range(5):
                total = jnp.zeros((1, block), f32)
                for q in range(sequences):
                    value = gconv[q, pl.ds(0, length), lanes]
                    if k < 4:
                        value = value * ext[q, pl.ds(8 - k, length), lanes]
                    total = total + jnp.sum(value, axis=0, keepdims=True)
                vec_ref[pl.ds(1 + k, 1), lanes] = total

        far_finish(1, *far_slots[1])

        @pl.when(s + 1 < seq_count)
        def _():
            halo_copy(1).wait_recv()
            for q in range(sequences):
                gconv[q, pl.ds(length, 8), :] = halos[1, 1, q]

        @pl.when(s + 1 == seq_count)
        def _():
            for q in range(sequences):
                gconv[q, pl.ds(length, 8), :] = jnp.zeros((8, half), f32)

        @pl.loop(0, heads)
        def _(n):
            lanes = head_lanes(n)
            for q in range(sequences):
                total = cw_ref[pl.ds(0, 1), lanes] * gconv[q, pl.ds(0, length), lanes]
                for k in range(1, 4):
                    total = total + cw_ref[pl.ds(k, 1), lanes] * gconv[q, pl.ds(k, length), lanes]
                adj[pl.ds(q * length, length), lanes] = total

        near_first(3, 1)
        near_last(3, 1)

        def own_rows(i):
            return x_all[pl.ds(pl.multiple_of(tokens + i * 16, 16), 16), pl.ds(0, half)].astype(f32)

        @pl.loop(0, tokens // 16)
        def _(i):
            r = pairs(i)
            product_ = adj[r, :] * (own_rows(i) * scales[0, r, :1])
            vec_ref[pl.ds(0, 1), :] += jnp.sum(product_, axis=0, keepdims=True)
            part[2, r, :] = jnp.broadcast_to(jnp.sum(product_ * gain_ref[...], axis=1, keepdims=True), (16, LANES))

        part_copy(2).start()
        vectors_start(0)
        matrices_plane()
        part_copy(2).wait_recv()

        @pl.loop(0, tokens // 16)
        def _(i):
            r = pairs(i)
            scale = scales[0, r, :1]
            hat = own_rows(i) * scale
            mean = ((part[2, r, :] + part_in[2, r, :]) * (1.0 / model))[:, :1]
            fin[r, :] = gres[r, :] + scale * (adj[r, :] * gain_ref[...] - hat * mean)

        near = pltpu.make_async_copy(fin, ingrad_ref.at[:, mine], keep.at[3])
        near.start()
        away = remote(fin, ingrad_ref.at[:, mine], fin_s.at[0], fin_r.at[0], s, 1 - h)
        away.start()
        near_first(3, 0)
        matrices_across()
        near_last(3, 0)
        vectors_sum(0)
        vectors_start(1)
        far_issue(2, *far_slots[2])
        near_send(3, 0, near_slots[3, 0][0])
        far_finish(2, *far_slots[2])
        matrices_spread()

        res = pltpu.make_async_copy(res_keep, rg, keep.at[4])
        res.start()
        res.wait()

        def absorb(src):
            fetch(src)

            @pl.loop(0, tokens // 64)
            def _(i):
                r = pl.ds(pl.multiple_of(i * 64, 64), 64)
                rg[r, :] += ld[r, :].astype(f32)

        sib_copy(1, 3).wait_recv()
        absorb(sib_ref.at[1, 3])
        for k in (1, 2):
            peer_copy(1, k).wait_recv()
            absorb(peer_ref.at[1, k])

        @pl.loop(0, tokens // 64)
        def _(i):
            r = pl.ds(pl.multiple_of(i * 64, 64), 64)
            own = g_all[pl.ds(pl.multiple_of(3 * tokens + i * 64, 64), 64), pl.ds(half, half)]
            ld[r, :] = (rg[r, :] + own.astype(f32)).astype(bf)

        near_out = pltpu.make_async_copy(ld, out_ref.at[:, mine], keep.at[4])
        near_out.start()
        away_out = remote(ld, out_ref.at[:, mine], fin_s.at[1], fin_r.at[1], s, 1 - h)
        away_out.start()
        vectors_sum(1)
        far_issue(3, *far_slots[3])
        far_finish(3, *far_slots[3])
        matrices_end()
        near.wait()
        near_out.wait()
        away.wait()
        away_out.wait()

    act = pltpu.VMEM((tokens, half), f32)
    padded = pltpu.VMEM((sequences, length + 8, half), f32)
    pl.run_scoped(
        recur_backward, act, act, act, act, act, padded, padded, pltpu.VMEM((2, block, block), f32),
    )

    for c in range(chunks):
        s1_drain(c)

        def sent(width, c=c):
            for zh_ in range(far):
                for zl_ in range(2):
                    r1_copy(c, zh_, zl_, width).wait_send()
            r2_copy(c, 1, width).wait_send()
            for d in (1, 2, 3):
                c3_copy(c, d, width, False, far_slots[c][0]).wait_send()
            c3_own(c, width, far_slots[c][0]).wait()
        by_width(c, wide(zl), sent)
        for d in (1, 2, 3):
            by_width(c, wide(peer(d)[2]), lambda width, d=d, c=c: c3_copy(c, d, width, True, far_slots[c][0]).wait_recv())
    for k in range(4):
        sib_copy(1, k).wait_send()
    for which in range(2):
        for k in range(3):
            peer_copy(which, k).wait_send()
    for i in range(3):
        part_copy(i).wait_send()
    pl.when(s + 1 < seq_count)(halo_copy(0).wait_send)
    pl.when(s > 0)(halo_copy(1).wait_send)

    ends_drain(0)
    ends_drain(1)


def block_pass(seq_count, sequences, x, cotangent, norm_gain, conv_weight, conv_bias, recur_weight, recur_bias,
               input_weight, input_bias, decay_param, mlp_gain, w_gate, w_up, w_down):
    tokens, width = x.shape
    half = width // 2
    length = tokens // sequences
    rows, units = w_gate.shape
    pair, far = 2 * rows, seq_count // 8
    chunks = -(-units // (4 * CHUNK))
    span = chunks * CHUNK
    matrix = (2 * recur_weight.shape[0] * recur_weight.shape[1], recur_weight.shape[2])
    planes = seq_count // 4
    bf, f32 = jnp.bfloat16, jnp.float32
    any_space = pl.BlockSpec(memory_space=pl.ANY)
    vmem = pl.BlockSpec(memory_space=pltpu.VMEM)
    outs = [
        ((tokens, width), bf), ((tokens, width), f32), ((3, rows, units), bf), ((16, half), f32), (matrix, bf),
        ((chunks, 3, width, CHUNK), bf), ((chunks, 3, 2 * far * pair, CHUNK), bf), ((chunks, 3, 2 * far * pair, CHUNK), bf),
        ((chunks, far - 1, 3, 2 * pair, CHUNK), bf),
        ((2, 4, tokens, half), bf), ((2, 3, tokens, half), bf),
        ((tokens, half), bf), ((tokens, half), f32), ((tokens, half), f32), ((tokens, half), bf),
        ((sequences, length + 8, half), f32), ((tokens, half), f32), ((tokens, half), f32),
        ((3 * matrix[0] // 4, matrix[1]), bf), ((matrix[0] // 4 // planes * (planes - 1), matrix[1]), bf),
    ]
    sem = pltpu.SemaphoreType.DMA
    scratch = [
        pltpu.VMEM((4 * tokens, width), bf), pltpu.VMEM((4 * tokens, width), bf), pltpu.VMEM((3, width, span), bf),
        pltpu.VMEM((tokens, half), bf), pltpu.VMEM((2, 2, sequences, 8, half), f32),
        pltpu.VMEM((2, 4 + planes, 2 * sequences, half), f32), pltpu.VMEM((sequences, half), f32),
        pltpu.VMEM((sequences, half), f32), pltpu.VMEM((3, tokens, LANES), f32), pltpu.VMEM((3, tokens, LANES), f32),
        pltpu.VMEM((2, tokens, LANES), f32), pltpu.VMEM((2 + planes, 16, half), f32),
    ]
    for shape in (
        (2, 3), (2, 4), (chunks, 3, 3), (chunks, far - 1, 2), (chunks, far, 2), (chunks, far, 2),
        (chunks, far - 1), (chunks, 3), (2, 4), (2, 3), (2,), (2, 2 + planes), (3,), (2,),
        (3,), (planes - 1,), (planes - 1,), (3,), (3,), (planes - 1,),
    ):
        scratch += [sem(shape), sem(shape)]
    scratch += [sem((chunks, far, 4)), sem((6 + sequences,)), sem((chunks + 1 + far, 3))]
    first = lax.axis_index("head") * half
    norm_half = lax.dynamic_slice_in_dim(norm_gain, first, half, 0)
    mlp_half = lax.dynamic_slice_in_dim(mlp_gain, first, half, 0)
    rate = jax.nn.softplus(-decay_param)
    slope = jax.nn.sigmoid(-decay_param)
    vectors = [norm_half, mlp_half, conv_bias, recur_bias, input_bias, rate, slope, slope]
    params = jnp.concatenate([jnp.stack(vectors), conv_weight, jnp.zeros_like(conv_weight)])
    results = pl.pallas_call(
        functools.partial(block_kernel, seq_count, sequences),
        out_shape=[jax.ShapeDtypeStruct(shape, kind) for shape, kind in outs],
        in_specs=[any_space] * 5 + [vmem] * 3,
        out_specs=[any_space] * 3 + [vmem] + [any_space] * (len(outs) - 4),
        scratch_shapes=scratch,
        compiler_params=pltpu.CompilerParams(
            collective_id=0, has_side_effects=True, vmem_limit_bytes=64 * 2**20 - 2**18
        ),
        cost_estimate=pl.CostEstimate(
            flops=18 * 4 * tokens * width * span, bytes_accessed=150 * 2**20, transcendentals=4 * tokens * span
        ),
        name="block_pass",
    )(x, cotangent, w_gate, w_up, w_down, params, recur_weight, input_weight)
    return results[:5]


def gathered_shards(
    block_input,
    norm_gain,
    conv_weight,
    conv_bias,
    recur_weight,
    recur_bias,
    input_weight,
    input_bias,
    decay_param,
    mlp_gain,
    w_gate,
    w_up,
    w_down,
    out_grad,
):
    sequences, span_len, model_width = block_input.shape
    lru_width = conv_bias.shape[0]
    heads_here = recur_weight.shape[0]
    block_width = recur_weight.shape[1]
    token_rows = sequences * span_len
    head_at = lax.axis_index("head")
    stream = block_input.astype(jnp.float32)
    first_scale, first_hat = norm_rows(stream)
    xn_first = (first_hat * norm_gain).astype(jnp.bfloat16)
    own_input = lax.dynamic_slice_in_dim(xn_first, head_at * lru_width, lru_width, 2)
    edge_rows = from_behind(own_input[:, span_len - 3 :, :], "seq", 1)
    padded = jnp.concatenate([edge_rows, own_input], axis=1).astype(jnp.float32)
    conv_sum = conv_bias + conv_weight[0] * padded[:, 3 : 3 + span_len]
    for offset in range(1, 4):
        conv_sum = conv_sum + conv_weight[offset] * padded[:, 3 - offset : 3 - offset + span_len]
    conv_out = conv_sum.astype(jnp.bfloat16)
    conv_blocks = conv_out.reshape(token_rows, heads_here, block_width)
    recur_pre = (
        jnp.einsum(
            "tnh,nhk->tnk", conv_blocks, recur_weight, preferred_element_type=jnp.float32
        ).reshape(sequences, span_len, lru_width)
        + recur_bias
    )
    input_pre = (
        jnp.einsum(
            "tnh,nhk->tnk", conv_blocks, input_weight, preferred_element_type=jnp.float32
        ).reshape(sequences, span_len, lru_width)
        + input_bias
    )
    recur_gate = jax.nn.sigmoid(recur_pre)
    input_gate = jax.nn.sigmoid(input_pre)
    rate = jax.nn.softplus(-decay_param)
    log_decay = -8.0 * rate * recur_gate
    decay = jnp.exp(log_decay)
    multiplier = jnp.sqrt(-jnp.expm1(2.0 * log_decay))
    conv_float = conv_out.astype(jnp.float32)
    pushed = multiplier * input_gate * conv_float
    decay_prod, local_state = lax.associative_scan(link_forward, (decay, pushed), axis=1)
    ones_edge = jnp.ones((sequences, lru_width), jnp.float32)
    zeros_edge = jnp.zeros((sequences, lru_width), jnp.float32)
    entering = prefix(
        (decay_prod[:, -1], local_state[:, -1]), "seq", link_forward, (ones_edge, zeros_edge), False
    )
    state = local_state + decay_prod * entering[1][:, None, :]
    state_full = lax.all_gather(state.astype(jnp.bfloat16), "head", axis=2, tiled=True)
    residual = stream + state_full.astype(jnp.float32)
    second_scale, second_hat = norm_rows(residual)
    xn_second = (second_hat * mlp_gain).astype(jnp.bfloat16).reshape(token_rows, model_width)
    hidden_width = w_gate.shape[1]
    pieces = (
        lax.all_gather(w_gate, "seq", axis=0, tiled=True),
        lax.all_gather(w_up, "seq", axis=0, tiled=True),
    )
    columns = xn_second
    gate = jnp.dot(columns, pieces[0], preferred_element_type=jnp.float32)
    up_value = jnp.dot(columns, pieces[1], preferred_element_type=jnp.float32)
    activated, gelu_back = jax.vjp(jax.nn.gelu, gate)
    hidden = (activated * up_value).astype(jnp.bfloat16)
    partial_mix = contract_last(hidden, lax.all_gather(w_down, "seq", axis=0, tiled=True))
    mixed = lax.psum(partial_mix, "head")
    block_output = (
        (residual.reshape(token_rows, model_width) + mixed)
        .astype(jnp.bfloat16)
        .reshape(block_input.shape)
    )
    cotangent = out_grad.reshape(token_rows, model_width)
    columns = cotangent
    grad_hidden = jnp.dot(
        columns,
        lax.all_gather(w_down, "seq", axis=0, tiled=True),
        preferred_element_type=jnp.float32,
    )
    grad_gate = gelu_back(grad_hidden * up_value)[0].astype(jnp.bfloat16)
    grad_up = (grad_hidden * activated).astype(jnp.bfloat16)
    pieces = (
        lax.all_gather(w_gate, "seq", axis=0, tiled=True),
        lax.all_gather(w_up, "seq", axis=0, tiled=True),
    )
    block_value = contract_last(grad_gate, pieces[0]) + contract_last(grad_up, pieces[1])
    grad_xn_second = lax.psum(block_value, "head").reshape(block_input.shape)
    stacked = jnp.concatenate([grad_gate, grad_up], axis=1)
    local_rows = w_gate.shape[0]
    seq_count = lax.axis_size("seq")
    turns = math.gcd(local_rows, 8)
    per_turn = local_rows // turns
    input_view = xn_second.reshape(token_rows, seq_count, local_rows)
    grad_view = cotangent.reshape(token_rows, seq_count, local_rows)

    def grad_turn(turn, collected):
        first_row = turn * per_turn
        input_cols = lax.dynamic_slice_in_dim(input_view, first_row, per_turn, 2).reshape(
            token_rows, seq_count * per_turn
        )
        grad_cols = lax.dynamic_slice_in_dim(grad_view, first_row, per_turn, 2).reshape(
            token_rows, seq_count * per_turn
        )
        term = jnp.concatenate(
            [contract_first(input_cols, stacked), contract_first(grad_cols, hidden)], axis=1
        )
        share = lax.psum_scatter(term, "seq", scatter_dimension=0, tiled=True)
        return lax.dynamic_update_slice_in_dim(collected, share, first_row, 0)

    weight_grads = lax.fori_loop(
        0, turns, grad_turn, jnp.zeros((local_rows, 3 * hidden_width), jnp.float32)
    )
    w_gate_grad = weight_grads[:, :hidden_width]
    w_up_grad = weight_grads[:, hidden_width : 2 * hidden_width]
    w_down_grad = weight_grads[:, 2 * hidden_width :]
    weighted_second = grad_xn_second * mlp_gain
    mlp_gain_local = jnp.sum(grad_xn_second * second_hat, axis=(0, 1))
    grad_residual = out_grad.astype(jnp.float32) + second_scale * (
        weighted_second
        - second_hat * jnp.mean(weighted_second * second_hat, axis=-1, keepdims=True)
    )
    grad_state = lax.dynamic_slice_in_dim(grad_residual, head_at * lru_width, lru_width, 2)
    next_decay = jnp.concatenate([decay[:, 1:], jnp.ones_like(decay[:, :1])], axis=1)
    flipped = lax.associative_scan(
        link_forward, (jnp.flip(next_decay, 1), jnp.flip(grad_state, 1)), axis=1
    )
    after_prod = jnp.flip(flipped[0], 1)
    local_adjoint = jnp.flip(flipped[1], 1)
    leaving = (decay_prod[:, -1], decay[:, 0] * local_adjoint[:, 0])
    arriving = prefix(leaving, "seq", link_backward, (ones_edge, zeros_edge), True)
    adjoint = local_adjoint + after_prod * arriving[1][:, None, :]
    previous = jnp.concatenate([entering[1][:, None, :], state[:, :-1]], axis=1)
    grad_mult = adjoint * input_gate * conv_float
    grad_log = adjoint * previous * decay - grad_mult * decay * decay / multiplier
    grad_recur_pre = (grad_log * (-8.0 * rate) * recur_gate * (1.0 - recur_gate)).astype(
        jnp.bfloat16
    )
    grad_input_pre = (adjoint * multiplier * conv_float * input_gate * (1.0 - input_gate)).astype(
        jnp.bfloat16
    )
    decay_local = jnp.sum(grad_log * 8.0 * recur_gate, axis=(0, 1)) * jax.nn.sigmoid(-decay_param)
    recur_blocks = grad_recur_pre.reshape(token_rows, heads_here, block_width)
    input_blocks = grad_input_pre.reshape(token_rows, heads_here, block_width)
    back_gates = jnp.einsum(
        "tnk,nhk->tnh", recur_blocks, recur_weight, preferred_element_type=jnp.float32
    )
    back_gates = back_gates + jnp.einsum(
        "tnk,nhk->tnh", input_blocks, input_weight, preferred_element_type=jnp.float32
    )
    grad_conv = (
        adjoint * multiplier * input_gate + back_gates.reshape(sequences, span_len, lru_width)
    ).astype(jnp.bfloat16)
    recur_weight_local = jnp.einsum(
        "tnh,tnk->nhk", conv_blocks, recur_blocks, preferred_element_type=jnp.float32
    )
    input_weight_local = jnp.einsum(
        "tnh,tnk->nhk", conv_blocks, input_blocks, preferred_element_type=jnp.float32
    )
    recur_bias_local = jnp.sum(grad_recur_pre.astype(jnp.float32), axis=(0, 1))
    input_bias_local = jnp.sum(grad_input_pre.astype(jnp.float32), axis=(0, 1))
    later_rows = from_behind(grad_conv[:, :3, :], "seq", -1)
    grad_padded = jnp.concatenate([grad_conv, later_rows], axis=1).astype(jnp.float32)
    grad_conv_float = grad_conv.astype(jnp.float32)
    grad_own_input = conv_weight[0] * grad_padded[:, 0:span_len]
    for offset in range(1, 4):
        grad_own_input = (
            grad_own_input + conv_weight[offset] * grad_padded[:, offset : offset + span_len]
        )
    conv_weight_local = jnp.stack(
        [
            jnp.sum(grad_conv_float * padded[:, 3 - offset : 3 - offset + span_len], axis=(0, 1))
            for offset in range(4)
        ]
    )
    conv_bias_local = jnp.sum(grad_conv_float, axis=(0, 1))
    grad_xn_first = lax.all_gather(
        grad_own_input.astype(jnp.bfloat16), "head", axis=2, tiled=True
    ).astype(grad_own_input.dtype)
    weighted_first = grad_xn_first * norm_gain
    norm_gain_local = jnp.sum(grad_xn_first * first_hat, axis=(0, 1))
    input_grad = grad_residual + first_scale * (
        weighted_first - first_hat * jnp.mean(weighted_first * first_hat, axis=-1, keepdims=True)
    )
    summed = lax.psum(
        (
            norm_gain_local,
            conv_weight_local,
            conv_bias_local,
            recur_weight_local,
            recur_bias_local,
            input_weight_local,
            input_bias_local,
            decay_local,
            mlp_gain_local,
        ),
        "seq",
    )
    return (
        block_output,
        input_grad,
        summed[0],
        summed[1],
        summed[2],
        summed[3],
        summed[4],
        summed[5],
        summed[6],
        summed[7],
        summed[8],
        w_gate_grad,
        w_up_grad,
        w_down_grad,
    )


def shards(
    block_input,
    norm_gain,
    conv_weight,
    conv_bias,
    recur_weight,
    recur_bias,
    input_weight,
    input_bias,
    decay_param,
    mlp_gain,
    w_gate,
    w_up,
    w_down,
    out_grad,
):
    seq_count = lax.axis_size("seq")
    sequences, span_len, width = block_input.shape
    if seq_count != 16 or w_gate.shape[0] % 32:
        return gathered_shards(
            block_input, norm_gain, conv_weight, conv_bias, recur_weight, recur_bias, input_weight, input_bias,
            decay_param, mlp_gain, w_gate, w_up, w_down, out_grad,
        )
    rows = sequences * span_len
    stream = block_input.reshape(rows, width)
    cotangent = out_grad.reshape(rows, width)
    block_output, input_grad, weight_grads, vectors, matrices = block_pass(
        seq_count, sequences, stream, cotangent, norm_gain, conv_weight, conv_bias, recur_weight, recur_bias,
        input_weight, input_bias, decay_param, mlp_gain, w_gate, w_up, w_down,
    )
    matrices = matrices.astype(jnp.float32).reshape(2, *recur_weight.shape)
    gains = lax.all_gather(jnp.stack([vectors[0], vectors[9]]), "head", axis=1, tiled=True)
    return (
        block_output.reshape(block_input.shape),
        input_grad.reshape(block_input.shape),
        gains[0],
        vectors[1:5],
        vectors[5],
        matrices[0],
        vectors[6],
        matrices[1],
        vectors[7],
        vectors[8],
        gains[1],
        weight_grads[0].astype(jnp.float32),
        weight_grads[1].astype(jnp.float32),
        weight_grads[2].astype(jnp.float32),
    )


def solution(mesh):
    placed = (
        P(None, "seq", None),
        P(),
        P(None, "head"),
        P("head"),
        P("head", None, None),
        P("head"),
        P("head", None, None),
        P("head"),
        P("head"),
        P(),
        P("seq", "head"),
        P("seq", "head"),
        P("seq", "head"),
        P(None, "seq", None),
    )
    return jax.shard_map(
        shards,
        mesh=mesh,
        in_specs=placed,
        out_specs=(
            P(None, "seq", None),
            P(None, "seq", None),
            P(),
            P(None, "head"),
            P("head"),
            P("head", None, None),
            P("head"),
            P("head", None, None),
            P("head"),
            P("head"),
            P(),
            P("seq", "head"),
            P("seq", "head"),
            P("seq", "head"),
        ),
        check_vma=False,
    )
```

```python
import functools
import math

import jax
import jax.numpy as jnp
from jax import lax
from jax.experimental import pallas as pl
from jax.experimental.pallas import tpu as pltpu
from jax.sharding import PartitionSpec as P

EPS = 1e-06
MESH = pl.DeviceIdType.MESH
LANES = 128
CHUNK = 256


def from_behind(value, axis, steps):
    count = lax.axis_size(axis)
    initial, last = (max(0, -steps), min(count, count - steps))
    return lax.ppermute(value, axis, [(source, source + steps) for source in range(initial, last)])


def prefix(part, axis, combine, identity, reverse):
    count = lax.axis_size(axis)
    place = lax.axis_index(axis)
    ahead = count - 1 - place if reverse else place
    gathered = jax.tree.map(lambda a: lax.all_gather(a, axis), part)
    state = jax.tree.map(lambda a, e: jnp.zeros_like(a) + jnp.asarray(e, a.dtype), part, identity)

    def one(lap, state):
        source = count - 1 - lap if reverse else lap
        return combine(
            state, jax.tree.map(lambda a: lax.dynamic_index_in_dim(a, source, 0, False), gathered)
        )

    return lax.fori_loop(0, ahead, one, state)


def norm_rows(values):
    scale = lax.rsqrt(jnp.mean(values * values, axis=-1, keepdims=True) + EPS)
    return (scale, values * scale)


def link_forward(earlier, latter):
    return (earlier[0] * latter[0], latter[0] * earlier[1] + latter[1])


def link_backward(earlier, latter):
    return (earlier[0] * latter[0], latter[1] + latter[0] * earlier[1])


def contract_last(left_side, right_side):
    return lax.dot_general(
        left_side, right_side, (((1,), (1,)), ((), ())), preferred_element_type=jnp.float32
    )


def contract_first(left_side, right_side):
    return lax.dot_general(
        left_side, right_side, (((0,), (0,)), ((), ())), preferred_element_type=jnp.float32
    )


def dot_nn(left_side, right_side):
    return jnp.dot(left_side, right_side, preferred_element_type=jnp.float32)


def remote(src, dst, send, recv, seq, head):
    return pltpu.make_async_remote_copy(
        src_ref=src, dst_ref=dst, send_sem=send, recv_sem=recv,
        device_id={"seq": seq, "head": head}, device_id_type=MESH,
    )


def half_window(head, half):
    return pl.ds(pl.multiple_of(head * half, LANES), half)


def greet_all(seq_count, s, h):
    barrier = pltpu.get_barrier_semaphore()

    @pl.loop(1, seq_count)
    def _(q):
        seq = (s + q) % seq_count
        pl.semaphore_signal(barrier, inc=1, device_id={"seq": seq, "head": h}, device_id_type=MESH)

    pl.semaphore_signal(barrier, inc=1, device_id={"seq": s, "head": 1 - h}, device_id_type=MESH)
    pl.semaphore_wait(barrier, seq_count)


def one_minus_square(log_decay):
    twice = 2.0 * log_decay
    series = 1.0 + twice * (1 / 2 + twice * (1 / 6 + twice * (1 / 24 + twice * (1 / 120 + twice * (1 / 720)))))
    return jnp.where(twice > -0.25, -twice * series, 1.0 - jnp.exp(twice))


def shifted(value, step, keep, fill):
    return jnp.where(keep, pltpu.roll(value, step % 8, 0), fill)


def block_kernel(
    seq_count, sequences, x_ref, g_ref, wg_ref, wu_ref, wd_ref,
    prm_ref, rw_ref, iw_ref,
    out_ref, ingrad_ref, dw_ref, vec_ref, mat_ref,
    dh_ref, r1_ref, e_ref, r2_ref, sib_ref, peer_ref, xn_half, rg_keep, ig_keep, conv_keep, ext_keep, state_keep,
    res_keep, ma_ref, mb_ref,
    x_all, g_all, w_all, ld, halos, ends_all, ent, arr, part, part_in, scales, vec_in,
    tok_s, tok_r, fwd_s, fwd_r, s1_s, s1_r, z_s, z_r, y_s, y_r, c1_s, c1_r, c2_s, c2_r, c3_s, c3_r,
    sib_s, sib_r, peer_s, peer_r, halo_s, halo_r, end_s, end_r, part_s, part_r, fin_s, fin_r, ma_s, ma_r, mb_s, mb_r, mc_s, mc_r, md_s, md_r, va_s, va_r, vb_s, vb_r, sums, keep, loc,
):
    far = seq_count // 8
    rows = wg_ref.shape[0]
    pair = 2 * rows
    tokens, half = x_ref.shape[0], x_ref.shape[1] // 2
    span = w_all.shape[2]
    chunks = span // CHUNK
    tiles = wg_ref.shape[1] // LANES
    base, extra = tiles // 4, tiles % 4
    s = lax.axis_index("seq")
    h = lax.axis_index("head")
    x = s % 2
    y = (s // 2) % 2
    zl = (s // 4) % 2
    zh = s // 8
    a = zl * 2 + x
    weights = (wg_ref, wu_ref, wd_ref)

    def seq_of(zh_, zl_, y_, x_):
        return ((zh_ * 2 + zl_) * 2 + y_) * 2 + x_

    def peer(d):
        zl_, x_ = (zl + d // 2) % 2, (x + d % 2) % 2
        return zl_ * 2 + x_, seq_of(zh, zl_, y, x_), zl_, x_

    def first_tile(a_):
        low = base * a_ + jnp.minimum(a_, extra)
        high = base * a_ + jnp.maximum(a_ - (4 - extra), 0)
        return jnp.where(h == 0, low, high)

    def wide(zl_):
        return zl_ == h

    def block_rows(zh_, zl_, y_):
        return pl.ds(pl.multiple_of(((zh_ * 2 + zl_) * 2 + y_) * pair, 32), pair)

    def cols(c, width=CHUNK):
        return pl.ds(pl.multiple_of(c * CHUNK, CHUNK), width)

    def by_width(c, is_wide, run):
        narrow = (c == chunks - 1) & jnp.logical_not(is_wide)
        pl.when(narrow)(lambda: run(LANES))
        pl.when(jnp.logical_not(narrow))(lambda: run(CHUNK))

    y_seq = seq_of(zh, zl, 1 - y, x)

    def z_seq(q):
        return seq_of((zh + q) % far, zl, y, x)

    model = 2 * half
    length = tokens // sequences
    groups = length // 8
    mine = half_window(h, half)
    block = rw_ref.shape[1]
    heads = half // block
    f32, bf = jnp.float32, jnp.bfloat16
    gain_ref, mgain_ref, cb_ref, rb_ref, ib_ref, rate_ref, sig_ref = [prm_ref.at[pl.ds(i, 1)] for i in range(7)]
    cw_ref = prm_ref.at[pl.ds(8, 4)]
    greet_all(seq_count, s, h)

    def s1_send(c, d, w, width):
        a_, seq, zl_, _ = peer(d)
        col = pl.multiple_of((first_tile(a_) + 2 * c) * LANES, LANES)
        return remote(
            weights[w].at[:, pl.ds(col, width)],
            w_all.at[w, pl.ds(pl.multiple_of(s * rows, 32), rows), cols(c, width)],
            s1_s.at[c, d - 1, w], s1_r.at[c, d - 1, w], seq, h,
        )

    def s1_recv(c, d, w, width):
        _, seq, _, _ = peer(d)
        return remote(
            weights[w].at[:, pl.ds(0, width)],
            w_all.at[w, pl.ds(pl.multiple_of(seq * rows, 32), rows), cols(c, width)],
            s1_s.at[c, d - 1, w], s1_r.at[c, d - 1, w], seq, h,
        )

    def s1_own(c, w, width):
        col = pl.multiple_of((first_tile(a) + 2 * c) * LANES, LANES)
        return pltpu.make_async_copy(
            weights[w].at[:, pl.ds(col, width)],
            w_all.at[w, pl.ds(pl.multiple_of(s * rows, 32), rows), cols(c, width)],
            loc.at[c, w],
        )

    def s1_start(c):
        for d in (1, 2, 3):
            def go(width, d=d):
                for w in range(3):
                    s1_send(c, d, w, width).start()
            by_width(c, wide(peer(d)[2]), go)

        def own(width):
            for w in range(3):
                s1_own(c, w, width).start()
        by_width(c, wide(zl), own)

    def s1_wait(c):
        def got(width):
            for w in range(3):
                s1_own(c, w, width).wait()
                for d in (1, 2, 3):
                    s1_recv(c, d, w, width).wait_recv()
        by_width(c, wide(zl), got)

    def s1_drain(c):
        for d in (1, 2, 3):
            def go(width, d=d):
                for w in range(3):
                    s1_send(c, d, w, width).wait_send()
            by_width(c, wide(peer(d)[2]), go)

    def z_copy(c, q, zl_, width, incoming):
        zh_ = (zh - q + far) % far if incoming else zh
        part = w_all.at[:, block_rows(zh_, zl_, y), cols(c, width)]
        return remote(part, part, z_s.at[c, q - 1, zl_], z_r.at[c, q - 1, zl_], z_seq(q), h)

    def y_copy(c, q, zl_, width, incoming):
        part = w_all.at[:, block_rows((zh - q + far) % far, zl_, 1 - y if incoming else y), cols(c, width)]
        return remote(part, part, y_s.at[c, q, zl_], y_r.at[c, q, zl_], y_seq, h)

    def z_start(c, halves=(0, 1)):
        def go(width):
            for zl_ in halves:
                for q in range(1, far):
                    z_copy(c, q, zl_, width, False).start()
                y_copy(c, 0, zl_, width, False).start()
        by_width(c, wide(zl), go)

    def z_forward(c):
        def go(width):
            for q in range(1, far):
                for zl_ in range(2):
                    z_copy(c, q, zl_, width, True).wait_recv()
                    y_copy(c, q, zl_, width, False).start()
        by_width(c, wide(zl), go)

    def y_wait(c):
        def go(width):
            for q in range(far):
                for zl_ in range(2):
                    y_copy(c, q, zl_, width, True).wait_recv()
        by_width(c, wide(zl), go)

    def zy_drain(c):
        def go(width):
            for zl_ in range(2):
                for q in range(1, far):
                    z_copy(c, q, zl_, width, False).wait_send()
                for q in range(far):
                    y_copy(c, q, zl_, width, False).wait_send()
        by_width(c, wide(zl), go)

    half_cols = pl.ds(pl.multiple_of(h * half, LANES), half)

    def tok_rows(a_):
        return pl.ds(pl.multiple_of(a_ * tokens, 32), tokens)

    def tok_copy(k, d, incoming):
        src = xn_half if k == 0 else g_ref.at[:, half_cols]
        dst = (x_all, g_all)[k]
        here = a
        if d == 3:
            here = peer(2)[0]
            src = dst.at[tok_rows(here), half_cols]
        return remote(
            src, dst.at[tok_rows(peer(d)[0] if incoming else here), half_cols],
            tok_s.at[k, d - 1], tok_r.at[k, d - 1], peer(1 if d == 3 else d)[1], h,
        )

    def fwd_copy(k, d, incoming):
        dst = (x_all, g_all)[k]
        side = pl.ds(pl.multiple_of((1 - h if incoming else h) * half, LANES), half)
        part = dst.at[tok_rows(peer(d)[0]), side]
        return remote(part, part, fwd_s.at[k, d], fwd_r.at[k, d], s, 1 - h)

    own_x = pltpu.make_async_copy(xn_half, x_all.at[tok_rows(a), half_cols], loc.at[chunks, 0])
    own_g = pltpu.make_async_copy(g_ref, g_all.at[tok_rows(a), :], loc.at[chunks, 1])

    def tok_start(k):
        tok_copy(k, 2, False).start()
        tok_copy(k, 1, False).start()

    def tok_turn(k):
        tok_copy(k, 2, True).wait_recv()
        tok_copy(k, 3, False).start()
        fwd_copy(k, 2, False).start()

    def tok_last(k):
        for d in (1, 3):
            tok_copy(k, d, True).wait_recv()
            fwd_copy(k, d, False).start()

    def tok_wait(k):
        for d in ((1, 2, 3) if k else (0, 1, 2, 3)):
            fwd_copy(k, d, True).wait_recv()

    def r1_copy(c, zh_, zl_, width):
        lanes = pl.ds(0, width)
        return remote(
            dh_ref.at[c, :, block_rows(zh_, zl_, 1 - y), lanes],
            r1_ref.at[c, :, pl.ds(pl.multiple_of((zh_ * 2 + zl_) * pair, 32), pair), lanes],
            c1_s.at[c, zh_, zl_], c1_r.at[c, zh_, zl_], y_seq, h,
        )

    def r1_start(c, steps_away):
        def go(width):
            for q in steps_away:
                for zl_ in range(2):
                    r1_copy(c, (zh + q) % far, zl_, width).start()
        by_width(c, wide(zl), go)

    def plane_rows(zh_):
        return pl.ds(pl.multiple_of(zh_ * 2 * pair, 32), 2 * pair)

    def r2_copy(c, q, width, src=None):
        lanes = pl.ds(0, width)
        if src is None:
            src = e_ref.at[c, :, plane_rows((zh + q) % far), lanes]
        else:
            src = src.at[:, :, lanes]
        return remote(src, r2_ref.at[c, q - 1, :, :, lanes], c2_s.at[c, q - 1], c2_r.at[c, q - 1], z_seq(q), h)

    def r2_start(c, q, src=None):
        by_width(c, wide(zl), lambda width: r2_copy(c, q, width, src).start())

    def add_into(first, second):
        @pl.loop(0, 3)
        def _(w):
            @pl.loop(0, 2)
            def _(b):
                r = pl.ds(pl.multiple_of(b * pair, 32), pair)
                first[w, r, :] = first[w, r, :] + second[w, r, :]

    def near_loads(c, q, first, second):
        zh_ = (zh + q) % far
        loads = [
            pltpu.make_async_copy(
                dh_ref.at[c, :, block_rows(zh_, zl_, y), :], first.at[:, pl.ds(zl_ * pair, pair)], sums.at[c, q, zl_]
            )
            for zl_ in range(2)
        ]
        return loads + [pltpu.make_async_copy(r1_ref.at[c, :, plane_rows(zh_)], second, sums.at[c, q, 2])]

    def near_store(c, q, first):
        return pltpu.make_async_copy(first, e_ref.at[c, :, plane_rows((zh + q) % far)], sums.at[c, q, 3])

    def near_issue(c, q, first, second):
        def got(width):
            for zl_ in range(2):
                r1_copy(c, (zh + q) % far, zl_, width).wait_recv()
        by_width(c, wide(zl), got)
        for load in near_loads(c, q, first, second):
            load.start()

    def near_finish(c, q, first, second, direct):
        for load in near_loads(c, q, first, second):
            load.wait()
        add_into(first, second)
        if direct and q:
            r2_start(c, q, first)
        else:
            near_store(c, q, first).start()

    def near_send(c, q, first):
        near_store(c, q, first).wait()
        if q:
            r2_start(c, q)

    def far_loads(c, first, second):
        return [
            pltpu.make_async_copy(e_ref.at[c, :, plane_rows(zh)], first, sums.at[c, 0, 0]),
            pltpu.make_async_copy(r2_ref.at[c, 0], second, sums.at[c, 0, 1]),
        ]

    def far_issue(c, first, second):
        by_width(c, wide(zl), lambda width: r2_copy(c, 1, width).wait_recv())
        for load in far_loads(c, first, second):
            load.start()

    def far_finish(c, first, second):
        for load in far_loads(c, first, second):
            load.wait()
        add_into(first, second)

        def go(width):
            for d in (1, 2, 3):
                c3_copy(c, d, width, False, first).start()
            c3_own(c, width, first).start()
        by_width(c, wide(zl), go)

    def c3_copy(c, d, width, incoming, src):
        a_, seq, zl_, x_ = peer(d)
        col = pl.multiple_of((first_tile(a_ if incoming else a) + 2 * c) * LANES, LANES)
        return remote(
            src.at[:, pl.ds(pl.multiple_of((zl_ * 2 + x_) * rows, 32), rows), pl.ds(0, width)],
            dw_ref.at[:, :, pl.ds(col, width)],
            c3_s.at[c, d - 1], c3_r.at[c, d - 1], seq, h,
        )

    def c3_own(c, width, src):
        col = pl.multiple_of((first_tile(a) + 2 * c) * LANES, LANES)
        return pltpu.make_async_copy(
            src.at[:, pl.ds(pl.multiple_of(a * rows, 32), rows), pl.ds(0, width)],
            dw_ref.at[:, :, pl.ds(col, width)], loc.at[c, 0],
        )

    def forward_chunk(c, hid, gg, gu):
        @pl.loop(0, 4)
        def _(i):
            r = tok_rows(i)
            xb = x_all[r, :]
            gate = dot_nn(xb, w_all[0, :, cols(c)])
            up = dot_nn(xb, w_all[1, :, cols(c)])
            gh = dot_nn(g_all[r, :], w_all[2, :, cols(c)])
            k0, k1 = 0.7978845608028654, 0.044715
            th = jnp.tanh(k0 * (gate + k1 * gate * gate * gate))
            cdf = 0.5 * (1.0 + th)
            act = gate * cdf
            slope = cdf + 0.5 * gate * (1.0 - th * th) * k0 * (1.0 + 3.0 * k1 * gate * gate)
            hid[r, cols(c)] = (act * up).astype(jnp.bfloat16)
            gu[r, cols(c)] = (gh * act).astype(jnp.bfloat16)
            gg[r, cols(c)] = (gh * up * slope).astype(jnp.bfloat16)

    def weight_chunk(c, hid, gg, gu, dv):
        for w, (left, right) in enumerate(((x_all, gg), (x_all, gu), (g_all, hid))):
            @pl.loop(0, x_all.shape[1] // 512)
            def _(j):
                r = pl.ds(pl.multiple_of(j * 512, 512), 512)
                dv[w, r, :] = contract_first(left[:, r], right[:, cols(c)]).astype(jnp.bfloat16)
            pltpu.make_async_copy(dv.at[w], dh_ref.at[c, w], loc.at[chunks, w]).start()
        for w in range(3):
            pltpu.make_async_copy(dv.at[w], dh_ref.at[c, w], loc.at[chunks, w]).wait()

    def product(which, r, d_rows, hid, gg, gu):
        if which == 0:
            return contract_last(gg[r, :], w_all[0, d_rows, :]) + contract_last(gu[r, :], w_all[1, d_rows, :])
        return contract_last(hid[r, :], w_all[2, d_rows, :])

    def pairs(i):
        return pl.ds(pl.multiple_of(i * 16, 16), 16)

    def head_lanes(n):
        return pl.ds(pl.multiple_of(n * block, block), block)

    def near_copy(side, k, incoming):
        source = (place - k + 4) % 4 if incoming else place
        part_ends = ends_all.at[side, source]
        return remote(part_ends, part_ends, end_s.at[side, k - 1], end_r.at[side, k - 1], mate(k), h)

    def far_copy(side, j, incoming):
        step = -j if (side == 0) == incoming else j
        source = plane + step if incoming else plane
        target = plane if incoming else plane + step
        bound = jnp.clip(source, 0, planes - 1), jnp.clip(target, 0, planes - 1)
        part_ends = ends_all.at[side, 4 + bound[0]]
        return remote(
            part_ends, part_ends, end_s.at[side, 2 + j], end_r.at[side, 2 + j], bound[1] * 4 + place, h
        )

    def far_exists(side, incoming, j):
        if (side == 0) == incoming:
            return plane >= j
        return plane + j < planes

    def ends_near(side):
        for k in (1, 2, 3):
            near_copy(side, k, False).start()

    def follow(total, got):
        return total[0] * got[:sequences], got[:sequences] * total[1] + got[sequences:]

    def ends_far(side):
        for k in (1, 2, 3):
            near_copy(side, k, True).wait_recv()
        order = range(4) if side == 0 else range(3, -1, -1)
        total = jnp.ones((sequences, half), f32), jnp.zeros((sequences, half), f32)
        for p in order:
            total = follow(total, ends_all[side, p])
        ends_all[side, 4 + plane, pl.ds(0, sequences), :] = total[0]
        ends_all[side, 4 + plane, pl.ds(sequences, sequences), :] = total[1]
        for j in range(1, planes):
            pl.when(far_exists(side, False, j))(far_copy(side, j, False).start)

    def ends_fold(side, out):
        out[...] = jnp.zeros_like(out)
        for j in range(planes - 1, 0, -1):
            @pl.when(far_exists(side, True, j))
            def _(j=j):
                far_copy(side, j, True).wait_recv()
                got = ends_all[side, 4 + (jnp.maximum(plane - j, 0) if side == 0 else jnp.minimum(plane + j, planes - 1))]
                out[...] = got[:sequences] * out[...] + got[sequences:]
        for p in range(4) if side == 0 else range(3, -1, -1):
            @pl.when(p < place if side == 0 else p > place)
            def _(p=p):
                got = ends_all[side, p]
                out[...] = got[:sequences] * out[...] + got[sequences:]

    def ends_drain(side):
        for k in (1, 2, 3):
            near_copy(side, k, False).wait_send()
        for j in range(1, planes):
            pl.when(far_exists(side, False, j))(far_copy(side, j, False).wait_send)

    def part_copy(i):
        return remote(part.at[i], part_in.at[i], part_s.at[i], part_r.at[i], s, 1 - h)

    def halo_copy(side):
        target = jnp.minimum(s + 1, seq_count - 1) if side == 0 else jnp.maximum(s - 1, 0)
        return remote(halos.at[side, 0], halos.at[side, 1], halo_s.at[side], halo_r.at[side], target, h)

    row_ids = lax.broadcasted_iota(jnp.int32, (8, half), 0)

    place, plane, planes = s % 4, s // 4, seq_count // 4
    quarter = 2 * heads * block // 4
    piece = quarter // planes
    mat = w_all.at[0, pl.ds(0, 4 * quarter), pl.ds(2 * CHUNK, block)]
    got_a = w_all.at[1, pl.ds(0, 3 * quarter), pl.ds(2 * CHUNK, block)]
    got_b = w_all.at[2, pl.ds(quarter, (planes - 1) * piece), pl.ds(2 * CHUNK, block)]
    own_sum = w_all.at[2, pl.ds(0, quarter), pl.ds(2 * CHUNK, block)]

    def mate(i):
        return plane * 4 + (place + i) % 4

    def layer(j):
        return (plane + j) % planes * 4 + place

    def rows_at(start, count):
        return pl.ds(pl.multiple_of(start, 32), count)

    def mat_a(i):
        return remote(
            mat.at[rows_at((place + i) % 4 * quarter, quarter)], ma_ref.at[pl.ds((i - 1) * quarter, quarter)],
            ma_s.at[i - 1], ma_r.at[i - 1], mate(i), h,
        )

    def mat_b(j):
        return remote(
            own_sum.at[rows_at((plane + j) % planes * piece, piece)], mb_ref.at[pl.ds((j - 1) * piece, piece)],
            mb_s.at[j - 1], mb_r.at[j - 1], layer(j), h,
        )

    def mat_c(j, incoming):
        source = (plane - j + planes) % planes if incoming else plane
        part_rows = mat_ref.at[rows_at(place * quarter + source * piece, piece)]
        return remote(part_rows, part_rows, mc_s.at[j - 1], mc_r.at[j - 1], layer(j), h)

    def mat_d(i, incoming):
        source = (place - i + 4) % 4 if incoming else place
        part_rows = mat_ref.at[rows_at(source * quarter, quarter)]
        return remote(part_rows, part_rows, md_s.at[i - 1], md_r.at[i - 1], mate(i), h)

    def take(src, dst, i):
        load = pltpu.make_async_copy(src, dst, keep.at[i])
        load.start()
        load.wait()

    def matrices_start():
        for i in (1, 2, 3):
            mat_a(i).start()

    def matrices_plane():
        for i in (1, 2, 3):
            mat_a(i).wait_recv()
        take(ma_ref, got_a, 8)

        @pl.loop(0, quarter // 32)
        def _(i):
            total = mat[rows_at(place * quarter + i * 32, 32), :].astype(f32)
            for k in range(3):
                total = total + got_a[rows_at(k * quarter + i * 32, 32), :].astype(f32)
            own_sum[rows_at(i * 32, 32), :] = total.astype(bf)
        for j in range(1, planes):
            mat_b(j).start()

    def matrices_across():
        for j in range(1, planes):
            mat_b(j).wait_recv()
        take(mb_ref, got_b, 8)

        @pl.loop(0, piece // 32)
        def _(i):
            r = rows_at(plane * piece + i * 32, 32)
            total = own_sum[r, :].astype(f32)
            for k in range(planes - 1):
                total = total + got_b[rows_at(k * piece + i * 32, 32), :].astype(f32)
            own_sum[r, :] = total.astype(bf)
        take(own_sum.at[rows_at(plane * piece, piece)], mat_ref.at[rows_at(place * quarter + plane * piece, piece)], 8)
        for j in range(1, planes):
            mat_c(j, False).start()

    def matrices_spread():
        for j in range(1, planes):
            mat_c(j, True).wait_recv()
        for i in (1, 2, 3):
            mat_d(i, False).start()

    def matrices_end():
        for i in (1, 2, 3):
            mat_d(i, True).wait_recv()
            mat_d(i, False).wait_send()
            mat_a(i).wait_send()
        for j in range(1, planes):
            mat_b(j).wait_send()
            mat_c(j, False).wait_send()

    def vec_copy(level, k):
        if level == 0:
            return remote(vec_ref, vec_in.at[k - 1], va_s.at[k - 1], va_r.at[k - 1], mate(k), h)
        return remote(vec_ref, vec_in.at[2 + k], vb_s.at[k - 1], vb_r.at[k - 1], layer(k), h)

    def vectors_start(level):
        for k in range(1, (4, planes)[level]):
            vec_copy(level, k).start()

    def vectors_sum(level):
        count = (4, planes)[level]
        for k in range(1, count):
            vec_copy(level, k).wait()
        total = vec_ref[...]
        for k in range(1, count):
            total = total + vec_in[(0, 3)[level] + k - 1]
        vec_ref[...] = total

    own_g.start()

    @pl.when(jnp.logical_not(wide(zl)))
    def _():
        w_all[:, :, pl.ds(span - LANES, LANES)] = jnp.zeros((3, w_all.shape[1], LANES), bf)

    def recur_forward(xin, rg, ig, conv, ext, prod, run):
        load = pltpu.make_async_copy(x_ref, xin, loc.at[chunks, 0])
        load.start()
        load.wait()

        def normed(r, count):
            full = xin[pl.ds(r, count), :].astype(f32)
            scale = lax.rsqrt(jnp.sum(full * full, axis=1, keepdims=True) * (1.0 / model) + EPS)
            scales[0, pl.ds(r, count), :] = jnp.broadcast_to(scale, (count, LANES))
            own = xin[pl.ds(r, count), mine].astype(f32)
            return ((own * scale) * gain_ref[...]).astype(bf).astype(f32)

        for q in range(sequences):
            halos[0, 0, q] = normed(q * length + length - 16, 16)[8:]
        pl.when(s + 1 < seq_count)(halo_copy(0).start)
        s1_start(0)
        s1_start(1)
        for q in range(sequences):
            @pl.loop(0, length // 16)
            def _(i, q=q):
                r = pl.multiple_of(i * 16, 16)
                ext[q, pl.ds(8 + r, 16), :] = normed(pl.multiple_of(q * length + r, 16), 16)

        @pl.when(s > 0)
        def _():
            halo_copy(0).wait_recv()
            for q in range(sequences):
                ext[q, pl.ds(0, 8), :] = halos[0, 1, q]

        @pl.when(s == 0)
        def _():
            for q in range(sequences):
                ext[q, pl.ds(0, 8), :] = jnp.zeros((8, half), f32)

        saves = [pltpu.make_async_copy(ext, ext_keep, keep.at[0])]
        saves[0].start()
        @pl.loop(0, heads)
        def _(n):
            lanes = head_lanes(n)
            for q in range(sequences):
                total = cb_ref[:, lanes]
                for k in range(4):
                    total = total + cw_ref[pl.ds(k, 1), lanes] * ext[q, pl.ds(8 - k, length), lanes]
                conv[pl.ds(q * length, length), lanes] = total.astype(bf)
            low = conv[:, lanes]
            rg[:, lanes] = jax.nn.sigmoid(dot_nn(low, rw_ref[n]) + rb_ref[:, lanes])
            ig[:, lanes] = jax.nn.sigmoid(dot_nn(low, iw_ref[n]) + ib_ref[:, lanes])

            @pl.loop(0, tokens // 64)
            def _(i):
                r = pl.ds(pl.multiple_of(i * 64, 64), 64)
                log_decay = -8.0 * rate_ref[:, lanes] * rg[r, lanes]
                prod[r, lanes] = jnp.exp(log_decay)
                mult = jnp.sqrt(one_minus_square(log_decay))
                run[r, lanes] = mult * ig[r, lanes] * conv[r, lanes].astype(f32)

        for i, (src, dst) in enumerate(((rg, rg_keep), (ig, ig_keep), (conv, conv_keep))):
            saves.append(pltpu.make_async_copy(src, dst, keep.at[1 + i]))
            saves[-1].start()

        def scan_group(g, carry):
            out = []
            for q in range(sequences):
                r = pl.ds(pl.multiple_of(q * length + g * 8, 8), 8)
                a_, b_ = prod[r, :], run[r, :]
                for k in (1, 2, 4):
                    inside = row_ids >= k
                    b_ = b_ + a_ * shifted(b_, k, inside, 0.0)
                    a_ = a_ * shifted(a_, k, inside, 1.0)
                b_ = b_ + a_ * carry[2 * q]
                a_ = a_ * carry[2 * q + 1]
                prod[r, :] = a_
                run[r, :] = b_
                out += [b_[7:8], a_[7:8]]
            return tuple(out)

        first = []
        for q in range(sequences):
            first += [jnp.zeros((1, half), f32), jnp.ones((1, half), f32)]
        last = lax.fori_loop(0, groups, scan_group, tuple(first))
        for q in range(sequences):
            ends_all[0, place, pl.ds(q, 1), :] = last[2 * q + 1]
            ends_all[0, place, pl.ds(sequences + q, 1), :] = last[2 * q]
        ends_near(0)
        ends_far(0)
        s1_wait(0)
        z_start(0)
        tok_start(1)
        own_g.wait()
        ends_fold(0, ent)

        for q in range(sequences):
            @pl.loop(0, length // 16)
            def _(i, q=q):
                r = pl.ds(pl.multiple_of(q * length + i * 16, 16), 16)
                state = run[r, :] + prod[r, :] * ent[pl.ds(q, 1), :]
                run[r, :] = state
                residual = xin[r, mine].astype(f32) + state.astype(bf).astype(f32)
                prod[r, :] = residual
                part[0, r, :] = jnp.broadcast_to(jnp.sum(residual * residual, axis=1, keepdims=True), (16, LANES))

        part_copy(0).start()
        for i, (src, dst) in enumerate(((run, state_keep), (prod, res_keep))):
            saves.append(pltpu.make_async_copy(src, dst, keep.at[4 + i]))
            saves[-1].start()
        part_copy(0).wait_recv()

        @pl.loop(0, tokens // 16)
        def _(i):
            r = pairs(i)
            scale = lax.rsqrt((part[0, r, :] + part_in[0, r, :]) * (1.0 / model) + EPS)
            scales[1, r, :] = scale
            ld[r, :] = ((prod[r, :] * scale[:, :1]) * mgain_ref[...]).astype(bf)

        saves.append(pltpu.make_async_copy(ld, xn_half, keep.at[6]))
        saves[-1].start()
        for save in saves:
            save.wait()

    pl.run_scoped(
        recur_forward,
        pltpu.VMEM((tokens, model), bf), pltpu.VMEM((tokens, half), f32), pltpu.VMEM((tokens, half), f32),
        pltpu.VMEM((tokens, half), bf), pltpu.VMEM((sequences, length + 8, half), f32),
        pltpu.VMEM((tokens, half), f32), pltpu.VMEM((tokens, half), f32),
    )
    tok_start(0)
    own_x.start()
    s1_start(2)
    s1_wait(1)
    z_start(1)
    own_x.wait()
    fwd_copy(0, 0, False).start()
    tok_turn(1)
    s1_start(3)
    z_forward(0)
    s1_wait(2)
    z_start(2)
    tok_last(1)
    tok_turn(0)
    z_forward(1)
    s1_wait(3)
    z_start(3)
    tok_last(0)
    tok_wait(1)
    tok_wait(0)

    stage = (x_all, g_all)
    steps = half // 256

    def slot(k):
        return pl.ds(pl.multiple_of(k * tokens, 32), tokens)

    def sib_copy(which, k):
        return remote(
            stage[which].at[slot(k), pl.ds(0, half)], sib_ref.at[which, k], sib_s.at[which, k], sib_r.at[which, k],
            s, 1 - h,
        )

    def peer_copy(which, k):
        zl_step, x_step = k // 2, 1 - k // 2
        seq = seq_of(zh, (zl + zl_step) % 2, y, (x + x_step) % 2)
        return remote(
            stage[which].at[slot(k), pl.ds(half, half)], peer_ref.at[which, k], peer_s.at[which, k], peer_r.at[which, k],
            seq, h,
        )

    def fetch(src):
        load = pltpu.make_async_copy(src, ld, loc.at[chunks, 0])
        load.start()
        load.wait()

    def add_slot(which, k, src):
        fetch(src)

        @pl.loop(0, tokens // 64)
        def _(i):
            r = pl.ds(pl.multiple_of(k * tokens + i * 64, 64), 64)
            lanes = pl.ds(half, half)
            stage[which][r, lanes] = stage[which][r, lanes] + ld[pl.ds(pl.multiple_of(i * 64, 64), 64), :]

    def combine(which, k):
        sib_copy(which, k).wait_recv()
        add_slot(which, k, sib_ref.at[which, k])
        if k == 2:
            peer_copy(which, 0).wait_recv()
            add_slot(which, k, peer_ref.at[which, 0])
        peer_copy(which, k).start()

    def compute_sums(which, k, hid, gg, gu):
        zl_step, x_step = 1 - k % 2, 1 - k // 2
        r = tok_rows(((zl + zl_step) % 2) * 2 + (x + x_step) % 2)

        def one(side, base_col):
            @pl.loop(0, steps)
            def _(j):
                dr = pl.ds(pl.multiple_of(side * half + j * 256, 256), 256)
                value = product(which, r, dr, hid, gg, gu)
                stage[which][slot(k), pl.ds(pl.multiple_of(base_col + j * 256, 256), 256)] = value.astype(bf)

        one(1 - h, 0)
        sib_copy(which, k).start()
        one(h, half)

    def feed_forward(hid, gg, gu, dv, sum_bufs):
        bufs = [(sum_bufs.at[0], sum_bufs.at[1]), (sum_bufs.at[2], sum_bufs.at[3])]

        @pl.loop(0, chunks)
        def _(c):
            y_wait(c)
            forward_chunk(c, hid, gg, gu)
            weight_chunk(c, hid, gg, gu, dv)
            away, near = range(1, far), (0,)


            @pl.when(c == 0)
            def _():
                z_forward(2)
                r1_start(0, away)

            @pl.when(c == 1)
            def _():
                z_forward(3)
                r1_start(0, near)

            pl.when((c >= 1) & (c < chunks - 1))(lambda: r1_start(c, (*away, *near)))
            pl.when(c == chunks - 1)(lambda: r1_start(c, away))

        for k in (0, 1, 2, 3):
            for d in (1, 2, 3) if k == 0 else ():
                for i in (0, 1):
                    tok_copy(i, d, False).wait_send()
                    fwd_copy(i, d, False).wait_send()
            if k == 0:
                fwd_copy(0, 0, False).wait_send()
            if k == 2:
                near_issue(0, 1, *bufs[0])
            if k == 3:
                near_finish(0, 1, *bufs[0], False)
            compute_sums(0, k, hid, gg, gu)
            if k in (1, 2):
                combine(0, k - 1)
        near_send(0, 1, bufs[0][0])
        near_issue(0, 0, *bufs[1])
        compute_sums(1, 0, hid, gg, gu)
        near_finish(0, 0, *bufs[1], False)
        compute_sums(1, 1, hid, gg, gu)
        combine(0, 2)
        near_issue(1, 1, *bufs[0])
        compute_sums(1, 2, hid, gg, gu)
        near_finish(1, 1, *bufs[0], False)
        near_send(0, 0, bufs[1][0])
        compute_sums(1, 3, hid, gg, gu)
        near_send(1, 1, bufs[0][0])

    wide_buf = pltpu.VMEM((4 * tokens, span), bf)
    pl.run_scoped(
        feed_forward, wide_buf, wide_buf, wide_buf, pltpu.VMEM((3, model, CHUNK), bf),
        pltpu.VMEM((4, 3, 2 * pair, CHUNK), bf),
    )
    pl.loop(0, chunks)(zy_drain)
    held = 2 * pair

    def hold(row, col):
        return w_all.at[:, pl.ds(row * held, held), pl.ds(col * CHUNK, CHUNK)]

    near_slots = {
        (1, 0): (hold(0, 3), hold(1, 3)), (2, 1): (hold(0, 0), hold(1, 0)), (2, 0): (hold(2, 0), hold(3, 0)),
        (3, 1): (hold(0, 1), hold(1, 1)), (3, 0): (hold(2, 1), hold(3, 1)),
    }
    far_slots = [
        (hold(2, 3), hold(3, 3)), (hold(1, 3), hold(1, 0)), (hold(3, 0), hold(1, 1)), (hold(3, 1), hold(3, 3)),
    ]

    def near_first(c, q):
        near_issue(c, q, *near_slots[c, q])

    def near_last(c, q):
        near_finish(c, q, *near_slots[c, q], True)

    def recur_backward(fin, adj, gres, rg, ig, gconv, ext, wsum):
        spare = [x_all.at[slot(k), pl.ds(0, half)] for k in range(4)]
        for k in range(4):
            sib_copy(0, k).wait_send()
        conv, own_x_half, own_g_half = spare[0], spare[1], spare[2]
        loads = [
            pltpu.make_async_copy(conv_keep, conv, keep.at[0]),
            pltpu.make_async_copy(x_ref.at[:, mine], own_x_half, keep.at[1]),
            pltpu.make_async_copy(g_ref.at[:, mine], own_g_half, keep.at[2]),
            pltpu.make_async_copy(rg_keep, rg, keep.at[3]),
            pltpu.make_async_copy(ig_keep, ig, keep.at[4]),
            pltpu.make_async_copy(res_keep, adj, keep.at[5]),
        ]
        for q in range(sequences):
            loads.append(pltpu.make_async_copy(
                state_keep.at[pl.ds(q * length, length)], ext.at[q, pl.ds(8, length)], keep.at[6 + q]
            ))
        for load in loads:
            load.start()

        def widen(first):
            @pl.loop(0, tokens // 64)
            def _(i):
                r = pl.ds(pl.multiple_of(i * 64, 64), 64)
                if first:
                    own = x_all[pl.ds(pl.multiple_of(3 * tokens + i * 64, 64), 64), pl.ds(half, half)]
                    fin[r, :] = own.astype(f32) + ld[r, :].astype(f32)
                else:
                    fin[r, :] += ld[r, :].astype(f32)

        sib_copy(0, 3).wait_recv()
        fetch(sib_ref.at[0, 3])
        widen(True)
        peer_copy(0, 1).wait_recv()
        fetch(peer_ref.at[0, 1])
        widen(False)
        vec_ref[...] = jnp.zeros_like(vec_ref)
        for load in loads:
            load.wait()
        for q in range(sequences):
            ext[q, pl.ds(0, 8), :] = jnp.broadcast_to(ent[pl.ds(q, 1), :], (8, half))

            @pl.loop(0, length // 16)
            def _(i, q=q):
                r = pl.ds(pl.multiple_of(q * length + i * 16, 16), 16)
                gconv[q, pairs(i), :] = jnp.exp(-8.0 * rate_ref[...] * rg[r, :])
        near_first(1, 0)
        peer_copy(0, 2).wait_recv()
        fetch(peer_ref.at[0, 2])
        widen(False)
        near_last(1, 0)
        combine(1, 0)

        @pl.loop(0, tokens // 16)
        def _(i):
            r = pairs(i)
            hat = adj[r, :] * scales[1, r, :1]
            product_ = fin[r, :] * hat
            vec_ref[pl.ds(9, 1), :] += jnp.sum(product_, axis=0, keepdims=True)
            part[1, r, :] = jnp.broadcast_to(jnp.sum(product_ * mgain_ref[...], axis=1, keepdims=True), (16, LANES))

        part_copy(1).start()
        near_send(1, 0, near_slots[1, 0][0])
        far_issue(0, *far_slots[0])
        part_copy(1).wait_recv()

        @pl.loop(0, tokens // 16)
        def _(i):
            r = pairs(i)
            scale = scales[1, r, :1]
            hat = adj[r, :] * scale
            mean = ((part[1, r, :] + part_in[1, r, :]) * (1.0 / model))[:, :1]
            own = x_all[pl.ds(pl.multiple_of(2 * tokens + i * 16, 16), 16), pl.ds(0, half)].astype(f32)
            gres[r, :] = own + scale * (fin[r, :] * mgain_ref[...] - hat * mean)

        far_finish(0, *far_slots[0])

        def scan_group(i, carry):
            g = groups - 1 - i
            out = []
            for q in range(sequences):
                t = pl.multiple_of(g * 8, 8)
                r = pl.ds(pl.multiple_of(q * length + t, 8), 8)
                here = gconv[q, pl.ds(t, 8), :]
                a_, b_ = shifted(here, -1, row_ids < 7, carry[3 * q + 2]), gres[r, :]
                for k in (1, 2, 4):
                    inside = row_ids < 8 - k
                    b_ = b_ + a_ * shifted(b_, -k, inside, 0.0)
                    a_ = a_ * shifted(a_, -k, inside, 1.0)
                b_ = b_ + a_ * carry[3 * q]
                a_ = a_ * carry[3 * q + 1]
                fin[r, :] = a_
                adj[r, :] = b_
                out += [b_[:1], a_[:1], here[:1]]
            return tuple(out)

        first = []
        for q in range(sequences):
            one = jnp.ones((1, half), f32)
            first += [jnp.zeros((1, half), f32), one, one]
        last = lax.fori_loop(0, groups, scan_group, tuple(first))
        for q in range(sequences):
            ends_all[1, place, pl.ds(q, 1), :] = last[3 * q + 1] * last[3 * q + 2]
            ends_all[1, place, pl.ds(sequences + q, 1), :] = last[3 * q] * last[3 * q + 2]
        ends_near(1)
        ends_far(1)
        r1_start(chunks - 1, (0,))
        near_first(2, 1)
        combine(1, 1)
        ends_fold(1, arr)

        for q in range(sequences):
            @pl.loop(0, length // 16)
            def _(i, q=q):
                r = pl.ds(pl.multiple_of(q * length + i * 16, 16), 16)
                adj[r, :] += fin[r, :] * arr[pl.ds(q, 1), :]

        near_last(2, 1)
        near_first(2, 0)
        combine(1, 2)

        @pl.loop(0, heads)
        def _(n):
            lanes = head_lanes(n)
            rate = rate_ref[:, lanes]
            sums = [jnp.zeros((1, block), f32)] * 3
            for q in range(sequences):
                for i in range(2):
                    count = length // 2
                    t = i * count
                    r = pl.ds(q * length + t, count)
                    rg_, ig_ = rg[r, lanes], ig[r, lanes]
                    low = x_all[r, lanes]
                    conv_ = low.astype(f32)
                    a_ = adj[r, lanes]
                    log_decay = -8.0 * rate * rg_
                    decay = jnp.exp(log_decay)
                    mult = jnp.sqrt(one_minus_square(log_decay))
                    previous = ext[q, pl.ds(7 + t, count), lanes]
                    grad_mult = a_ * ig_ * conv_
                    grad_log = a_ * previous * decay - grad_mult * decay * decay / mult
                    pre_r = (grad_log * (-8.0 * rate) * rg_ * (1.0 - rg_)).astype(bf)
                    pre_i = (a_ * mult * conv_ * ig_ * (1.0 - ig_)).astype(bf)
                    sums[0] = sums[0] + jnp.sum(grad_log * rg_, axis=0, keepdims=True)
                    sums[1] = sums[1] + jnp.sum(pre_r.astype(f32), axis=0, keepdims=True)
                    sums[2] = sums[2] + jnp.sum(pre_i.astype(f32), axis=0, keepdims=True)
                    back = contract_last(pre_r, rw_ref[n]) + contract_last(pre_i, iw_ref[n])
                    gconv[q, pl.ds(t, count), lanes] = (a_ * mult * ig_ + back).astype(bf).astype(f32)
                    if q == 0 and i == 0:
                        wsum[0] = contract_first(low, pre_r)
                        wsum[1] = contract_first(low, pre_i)
                    else:
                        wsum[0] += contract_first(low, pre_r)
                        wsum[1] += contract_first(low, pre_i)
            for k in range(2):
                mat[rows_at((k * heads + n) * block, block), :] = wsum[k].astype(bf)
            vec_ref[pl.ds(8, 1), lanes] = sums[0] * 8.0 * sig_ref[:, lanes]
            vec_ref[pl.ds(6, 1), lanes] = sums[1]
            vec_ref[pl.ds(7, 1), lanes] = sums[2]

        near_last(2, 0)
        for q in range(sequences):
            halos[1, 0, q] = gconv[q, pl.ds(0, 8), :]
        pl.when(s > 0)(halo_copy(1).start)
        matrices_start()
        far_issue(1, *far_slots[1])
        near_send(2, 0, near_slots[2, 0][0])
        again = pltpu.make_async_copy(ext_keep, ext, keep.at[2])
        again.start()
        again.wait()

        @pl.loop(0, heads)
        def _(n):
            lanes = head_lanes(n)
            for k in range(5):
                total = jnp.zeros((1, block), f32)
                for q in range(sequences):
                    value = gconv[q, pl.ds(0, length), lanes]
                    if k < 4:
                        value = value * ext[q, pl.ds(8 - k, length), lanes]
                    total = total + jnp.sum(value, axis=0, keepdims=True)
                vec_ref[pl.ds(1 + k, 1), lanes] = total

        far_finish(1, *far_slots[1])
        near_first(3, 1)

        @pl.when(s + 1 < seq_count)
        def _():
            halo_copy(1).wait_recv()
            for q in range(sequences):
                gconv[q, pl.ds(length, 8), :] = halos[1, 1, q]

        @pl.when(s + 1 == seq_count)
        def _():
            for q in range(sequences):
                gconv[q, pl.ds(length, 8), :] = jnp.zeros((8, half), f32)

        @pl.loop(0, heads)
        def _(n):
            lanes = head_lanes(n)
            for q in range(sequences):
                total = cw_ref[pl.ds(0, 1), lanes] * gconv[q, pl.ds(0, length), lanes]
                for k in range(1, 4):
                    total = total + cw_ref[pl.ds(k, 1), lanes] * gconv[q, pl.ds(k, length), lanes]
                adj[pl.ds(q * length, length), lanes] = total

        near_last(3, 1)

        def own_rows(i):
            return x_all[pl.ds(pl.multiple_of(tokens + i * 16, 16), 16), pl.ds(0, half)].astype(f32)

        @pl.loop(0, tokens // 16)
        def _(i):
            r = pairs(i)
            product_ = adj[r, :] * (own_rows(i) * scales[0, r, :1])
            vec_ref[pl.ds(0, 1), :] += jnp.sum(product_, axis=0, keepdims=True)
            part[2, r, :] = jnp.broadcast_to(jnp.sum(product_ * gain_ref[...], axis=1, keepdims=True), (16, LANES))

        part_copy(2).start()
        vectors_start(0)
        matrices_plane()
        part_copy(2).wait_recv()

        @pl.loop(0, tokens // 16)
        def _(i):
            r = pairs(i)
            scale = scales[0, r, :1]
            hat = own_rows(i) * scale
            mean = ((part[2, r, :] + part_in[2, r, :]) * (1.0 / model))[:, :1]
            fin[r, :] = gres[r, :] + scale * (adj[r, :] * gain_ref[...] - hat * mean)

        near = pltpu.make_async_copy(fin, ingrad_ref.at[:, mine], keep.at[3])
        near.start()
        away = remote(fin, ingrad_ref.at[:, mine], fin_s.at[0], fin_r.at[0], s, 1 - h)
        away.start()
        near_first(3, 0)
        near_last(3, 0)
        far_issue(2, *far_slots[2])
        matrices_across()
        far_finish(2, *far_slots[2])
        vectors_sum(0)
        vectors_start(1)
        near_send(3, 0, near_slots[3, 0][0])
        matrices_spread()

        res = pltpu.make_async_copy(res_keep, rg, keep.at[4])
        res.start()
        res.wait()

        def absorb(src):
            fetch(src)

            @pl.loop(0, tokens // 64)
            def _(i):
                r = pl.ds(pl.multiple_of(i * 64, 64), 64)
                rg[r, :] += ld[r, :].astype(f32)

        sib_copy(1, 3).wait_recv()
        absorb(sib_ref.at[1, 3])
        for k in (1, 2):
            peer_copy(1, k).wait_recv()
            absorb(peer_ref.at[1, k])

        @pl.loop(0, tokens // 64)
        def _(i):
            r = pl.ds(pl.multiple_of(i * 64, 64), 64)
            own = g_all[pl.ds(pl.multiple_of(3 * tokens + i * 64, 64), 64), pl.ds(half, half)]
            ld[r, :] = (rg[r, :] + own.astype(f32)).astype(bf)

        near_out = pltpu.make_async_copy(ld, out_ref.at[:, mine], keep.at[4])
        near_out.start()
        away_out = remote(ld, out_ref.at[:, mine], fin_s.at[1], fin_r.at[1], s, 1 - h)
        away_out.start()
        vectors_sum(1)
        far_issue(3, *far_slots[3])
        far_finish(3, *far_slots[3])
        matrices_end()
        near.wait()
        near_out.wait()
        away.wait()
        away_out.wait()

    act = pltpu.VMEM((tokens, half), f32)
    padded = pltpu.VMEM((sequences, length + 8, half), f32)
    pl.run_scoped(
        recur_backward, act, act, act, act, act, padded, padded, pltpu.VMEM((2, block, block), f32),
    )

    for c in range(chunks):
        s1_drain(c)

        def sent(width, c=c):
            for zh_ in range(far):
                for zl_ in range(2):
                    r1_copy(c, zh_, zl_, width).wait_send()
            r2_copy(c, 1, width).wait_send()
            for d in (1, 2, 3):
                c3_copy(c, d, width, False, far_slots[c][0]).wait_send()
            c3_own(c, width, far_slots[c][0]).wait()
        by_width(c, wide(zl), sent)
        for d in (1, 2, 3):
            by_width(c, wide(peer(d)[2]), lambda width, d=d, c=c: c3_copy(c, d, width, True, far_slots[c][0]).wait_recv())
    for k in range(4):
        sib_copy(1, k).wait_send()
    for which in range(2):
        for k in range(3):
            peer_copy(which, k).wait_send()
    for i in range(3):
        part_copy(i).wait_send()
    pl.when(s + 1 < seq_count)(halo_copy(0).wait_send)
    pl.when(s > 0)(halo_copy(1).wait_send)

    ends_drain(0)
    ends_drain(1)


def block_pass(seq_count, sequences, x, cotangent, norm_gain, conv_weight, conv_bias, recur_weight, recur_bias,
               input_weight, input_bias, decay_param, mlp_gain, w_gate, w_up, w_down):
    tokens, width = x.shape
    half = width // 2
    length = tokens // sequences
    rows, units = w_gate.shape
    pair, far = 2 * rows, seq_count // 8
    chunks = -(-units // (4 * CHUNK))
    span = chunks * CHUNK
    matrix = (2 * recur_weight.shape[0] * recur_weight.shape[1], recur_weight.shape[2])
    planes = seq_count // 4
    bf, f32 = jnp.bfloat16, jnp.float32
    any_space = pl.BlockSpec(memory_space=pl.ANY)
    vmem = pl.BlockSpec(memory_space=pltpu.VMEM)
    outs = [
        ((tokens, width), bf), ((tokens, width), f32), ((3, rows, units), bf), ((16, half), f32), (matrix, bf),
        ((chunks, 3, width, CHUNK), bf), ((chunks, 3, 2 * far * pair, CHUNK), bf), ((chunks, 3, 2 * far * pair, CHUNK), bf),
        ((chunks, far - 1, 3, 2 * pair, CHUNK), bf),
        ((2, 4, tokens, half), bf), ((2, 3, tokens, half), bf),
        ((tokens, half), bf), ((tokens, half), f32), ((tokens, half), f32), ((tokens, half), bf),
        ((sequences, length + 8, half), f32), ((tokens, half), f32), ((tokens, half), f32),
        ((3 * matrix[0] // 4, matrix[1]), bf), ((matrix[0] // 4 // planes * (planes - 1), matrix[1]), bf),
    ]
    sem = pltpu.SemaphoreType.DMA
    scratch = [
        pltpu.VMEM((4 * tokens, width), bf), pltpu.VMEM((4 * tokens, width), bf), pltpu.VMEM((3, width, span), bf),
        pltpu.VMEM((tokens, half), bf), pltpu.VMEM((2, 2, sequences, 8, half), f32),
        pltpu.VMEM((2, 4 + planes, 2 * sequences, half), f32), pltpu.VMEM((sequences, half), f32),
        pltpu.VMEM((sequences, half), f32), pltpu.VMEM((3, tokens, LANES), f32), pltpu.VMEM((3, tokens, LANES), f32),
        pltpu.VMEM((2, tokens, LANES), f32), pltpu.VMEM((2 + planes, 16, half), f32),
    ]
    for shape in (
        (2, 3), (2, 4), (chunks, 3, 3), (chunks, far - 1, 2), (chunks, far, 2), (chunks, far, 2),
        (chunks, far - 1), (chunks, 3), (2, 4), (2, 3), (2,), (2, 2 + planes), (3,), (2,),
        (3,), (planes - 1,), (planes - 1,), (3,), (3,), (planes - 1,),
    ):
        scratch += [sem(shape), sem(shape)]
    scratch += [sem((chunks, far, 4)), sem((6 + sequences,)), sem((chunks + 1 + far, 3))]
    first = lax.axis_index("head") * half
    norm_half = lax.dynamic_slice_in_dim(norm_gain, first, half, 0)
    mlp_half = lax.dynamic_slice_in_dim(mlp_gain, first, half, 0)
    rate = jax.nn.softplus(-decay_param)
    slope = jax.nn.sigmoid(-decay_param)
    vectors = [norm_half, mlp_half, conv_bias, recur_bias, input_bias, rate, slope, slope]
    params = jnp.concatenate([jnp.stack(vectors), conv_weight, jnp.zeros_like(conv_weight)])
    results = pl.pallas_call(
        functools.partial(block_kernel, seq_count, sequences),
        out_shape=[jax.ShapeDtypeStruct(shape, kind) for shape, kind in outs],
        in_specs=[any_space] * 5 + [vmem] * 3,
        out_specs=[any_space] * 3 + [vmem] + [any_space] * (len(outs) - 4),
        scratch_shapes=scratch,
        compiler_params=pltpu.CompilerParams(
            collective_id=0, has_side_effects=True, vmem_limit_bytes=64 * 2**20 - 2**18
        ),
        cost_estimate=pl.CostEstimate(
            flops=18 * 4 * tokens * width * span, bytes_accessed=150 * 2**20, transcendentals=4 * tokens * span
        ),
        name="block_pass",
    )(x, cotangent, w_gate, w_up, w_down, params, recur_weight, input_weight)
    return results[:5]


def gathered_shards(
    block_input,
    norm_gain,
    conv_weight,
    conv_bias,
    recur_weight,
    recur_bias,
    input_weight,
    input_bias,
    decay_param,
    mlp_gain,
    w_gate,
    w_up,
    w_down,
    out_grad,
):
    sequences, span_len, model_width = block_input.shape
    lru_width = conv_bias.shape[0]
    heads_here = recur_weight.shape[0]
    block_width = recur_weight.shape[1]
    token_rows = sequences * span_len
    head_at = lax.axis_index("head")
    stream = block_input.astype(jnp.float32)
    first_scale, first_hat = norm_rows(stream)
    xn_first = (first_hat * norm_gain).astype(jnp.bfloat16)
    own_input = lax.dynamic_slice_in_dim(xn_first, head_at * lru_width, lru_width, 2)
    edge_rows = from_behind(own_input[:, span_len - 3 :, :], "seq", 1)
    padded = jnp.concatenate([edge_rows, own_input], axis=1).astype(jnp.float32)
    conv_sum = conv_bias + conv_weight[0] * padded[:, 3 : 3 + span_len]
    for offset in range(1, 4):
        conv_sum = conv_sum + conv_weight[offset] * padded[:, 3 - offset : 3 - offset + span_len]
    conv_out = conv_sum.astype(jnp.bfloat16)
    conv_blocks = conv_out.reshape(token_rows, heads_here, block_width)
    recur_pre = (
        jnp.einsum(
            "tnh,nhk->tnk", conv_blocks, recur_weight, preferred_element_type=jnp.float32
        ).reshape(sequences, span_len, lru_width)
        + recur_bias
    )
    input_pre = (
        jnp.einsum(
            "tnh,nhk->tnk", conv_blocks, input_weight, preferred_element_type=jnp.float32
        ).reshape(sequences, span_len, lru_width)
        + input_bias
    )
    recur_gate = jax.nn.sigmoid(recur_pre)
    input_gate = jax.nn.sigmoid(input_pre)
    rate = jax.nn.softplus(-decay_param)
    log_decay = -8.0 * rate * recur_gate
    decay = jnp.exp(log_decay)
    multiplier = jnp.sqrt(-jnp.expm1(2.0 * log_decay))
    conv_float = conv_out.astype(jnp.float32)
    pushed = multiplier * input_gate * conv_float
    decay_prod, local_state = lax.associative_scan(link_forward, (decay, pushed), axis=1)
    ones_edge = jnp.ones((sequences, lru_width), jnp.float32)
    zeros_edge = jnp.zeros((sequences, lru_width), jnp.float32)
    entering = prefix(
        (decay_prod[:, -1], local_state[:, -1]), "seq", link_forward, (ones_edge, zeros_edge), False
    )
    state = local_state + decay_prod * entering[1][:, None, :]
    state_full = lax.all_gather(state.astype(jnp.bfloat16), "head", axis=2, tiled=True)
    residual = stream + state_full.astype(jnp.float32)
    second_scale, second_hat = norm_rows(residual)
    xn_second = (second_hat * mlp_gain).astype(jnp.bfloat16).reshape(token_rows, model_width)
    hidden_width = w_gate.shape[1]
    pieces = (
        lax.all_gather(w_gate, "seq", axis=0, tiled=True),
        lax.all_gather(w_up, "seq", axis=0, tiled=True),
    )
    columns = xn_second
    gate = jnp.dot(columns, pieces[0], preferred_element_type=jnp.float32)
    up_value = jnp.dot(columns, pieces[1], preferred_element_type=jnp.float32)
    activated, gelu_back = jax.vjp(jax.nn.gelu, gate)
    hidden = (activated * up_value).astype(jnp.bfloat16)
    partial_mix = contract_last(hidden, lax.all_gather(w_down, "seq", axis=0, tiled=True))
    mixed = lax.psum(partial_mix, "head")
    block_output = (
        (residual.reshape(token_rows, model_width) + mixed)
        .astype(jnp.bfloat16)
        .reshape(block_input.shape)
    )
    cotangent = out_grad.reshape(token_rows, model_width)
    columns = cotangent
    grad_hidden = jnp.dot(
        columns,
        lax.all_gather(w_down, "seq", axis=0, tiled=True),
        preferred_element_type=jnp.float32,
    )
    grad_gate = gelu_back(grad_hidden * up_value)[0].astype(jnp.bfloat16)
    grad_up = (grad_hidden * activated).astype(jnp.bfloat16)
    pieces = (
        lax.all_gather(w_gate, "seq", axis=0, tiled=True),
        lax.all_gather(w_up, "seq", axis=0, tiled=True),
    )
    block_value = contract_last(grad_gate, pieces[0]) + contract_last(grad_up, pieces[1])
    grad_xn_second = lax.psum(block_value, "head").reshape(block_input.shape)
    stacked = jnp.concatenate([grad_gate, grad_up], axis=1)
    local_rows = w_gate.shape[0]
    seq_count = lax.axis_size("seq")
    turns = math.gcd(local_rows, 8)
    per_turn = local_rows // turns
    input_view = xn_second.reshape(token_rows, seq_count, local_rows)
    grad_view = cotangent.reshape(token_rows, seq_count, local_rows)

    def grad_turn(turn, collected):
        first_row = turn * per_turn
        input_cols = lax.dynamic_slice_in_dim(input_view, first_row, per_turn, 2).reshape(
            token_rows, seq_count * per_turn
        )
        grad_cols = lax.dynamic_slice_in_dim(grad_view, first_row, per_turn, 2).reshape(
            token_rows, seq_count * per_turn
        )
        term = jnp.concatenate(
            [contract_first(input_cols, stacked), contract_first(grad_cols, hidden)], axis=1
        )
        share = lax.psum_scatter(term, "seq", scatter_dimension=0, tiled=True)
        return lax.dynamic_update_slice_in_dim(collected, share, first_row, 0)

    weight_grads = lax.fori_loop(
        0, turns, grad_turn, jnp.zeros((local_rows, 3 * hidden_width), jnp.float32)
    )
    w_gate_grad = weight_grads[:, :hidden_width]
    w_up_grad = weight_grads[:, hidden_width : 2 * hidden_width]
    w_down_grad = weight_grads[:, 2 * hidden_width :]
    weighted_second = grad_xn_second * mlp_gain
    mlp_gain_local = jnp.sum(grad_xn_second * second_hat, axis=(0, 1))
    grad_residual = out_grad.astype(jnp.float32) + second_scale * (
        weighted_second
        - second_hat * jnp.mean(weighted_second * second_hat, axis=-1, keepdims=True)
    )
    grad_state = lax.dynamic_slice_in_dim(grad_residual, head_at * lru_width, lru_width, 2)
    next_decay = jnp.concatenate([decay[:, 1:], jnp.ones_like(decay[:, :1])], axis=1)
    flipped = lax.associative_scan(
        link_forward, (jnp.flip(next_decay, 1), jnp.flip(grad_state, 1)), axis=1
    )
    after_prod = jnp.flip(flipped[0], 1)
    local_adjoint = jnp.flip(flipped[1], 1)
    leaving = (decay_prod[:, -1], decay[:, 0] * local_adjoint[:, 0])
    arriving = prefix(leaving, "seq", link_backward, (ones_edge, zeros_edge), True)
    adjoint = local_adjoint + after_prod * arriving[1][:, None, :]
    previous = jnp.concatenate([entering[1][:, None, :], state[:, :-1]], axis=1)
    grad_mult = adjoint * input_gate * conv_float
    grad_log = adjoint * previous * decay - grad_mult * decay * decay / multiplier
    grad_recur_pre = (grad_log * (-8.0 * rate) * recur_gate * (1.0 - recur_gate)).astype(
        jnp.bfloat16
    )
    grad_input_pre = (adjoint * multiplier * conv_float * input_gate * (1.0 - input_gate)).astype(
        jnp.bfloat16
    )
    decay_local = jnp.sum(grad_log * 8.0 * recur_gate, axis=(0, 1)) * jax.nn.sigmoid(-decay_param)
    recur_blocks = grad_recur_pre.reshape(token_rows, heads_here, block_width)
    input_blocks = grad_input_pre.reshape(token_rows, heads_here, block_width)
    back_gates = jnp.einsum(
        "tnk,nhk->tnh", recur_blocks, recur_weight, preferred_element_type=jnp.float32
    )
    back_gates = back_gates + jnp.einsum(
        "tnk,nhk->tnh", input_blocks, input_weight, preferred_element_type=jnp.float32
    )
    grad_conv = (
        adjoint * multiplier * input_gate + back_gates.reshape(sequences, span_len, lru_width)
    ).astype(jnp.bfloat16)
    recur_weight_local = jnp.einsum(
        "tnh,tnk->nhk", conv_blocks, recur_blocks, preferred_element_type=jnp.float32
    )
    input_weight_local = jnp.einsum(
        "tnh,tnk->nhk", conv_blocks, input_blocks, preferred_element_type=jnp.float32
    )
    recur_bias_local = jnp.sum(grad_recur_pre.astype(jnp.float32), axis=(0, 1))
    input_bias_local = jnp.sum(grad_input_pre.astype(jnp.float32), axis=(0, 1))
    later_rows = from_behind(grad_conv[:, :3, :], "seq", -1)
    grad_padded = jnp.concatenate([grad_conv, later_rows], axis=1).astype(jnp.float32)
    grad_conv_float = grad_conv.astype(jnp.float32)
    grad_own_input = conv_weight[0] * grad_padded[:, 0:span_len]
    for offset in range(1, 4):
        grad_own_input = (
            grad_own_input + conv_weight[offset] * grad_padded[:, offset : offset + span_len]
        )
    conv_weight_local = jnp.stack(
        [
            jnp.sum(grad_conv_float * padded[:, 3 - offset : 3 - offset + span_len], axis=(0, 1))
            for offset in range(4)
        ]
    )
    conv_bias_local = jnp.sum(grad_conv_float, axis=(0, 1))
    grad_xn_first = lax.all_gather(
        grad_own_input.astype(jnp.bfloat16), "head", axis=2, tiled=True
    ).astype(grad_own_input.dtype)
    weighted_first = grad_xn_first * norm_gain
    norm_gain_local = jnp.sum(grad_xn_first * first_hat, axis=(0, 1))
    input_grad = grad_residual + first_scale * (
        weighted_first - first_hat * jnp.mean(weighted_first * first_hat, axis=-1, keepdims=True)
    )
    summed = lax.psum(
        (
            norm_gain_local,
            conv_weight_local,
            conv_bias_local,
            recur_weight_local,
            recur_bias_local,
            input_weight_local,
            input_bias_local,
            decay_local,
            mlp_gain_local,
        ),
        "seq",
    )
    return (
        block_output,
        input_grad,
        summed[0],
        summed[1],
        summed[2],
        summed[3],
        summed[4],
        summed[5],
        summed[6],
        summed[7],
        summed[8],
        w_gate_grad,
        w_up_grad,
        w_down_grad,
    )


def shards(
    block_input,
    norm_gain,
    conv_weight,
    conv_bias,
    recur_weight,
    recur_bias,
    input_weight,
    input_bias,
    decay_param,
    mlp_gain,
    w_gate,
    w_up,
    w_down,
    out_grad,
):
    seq_count = lax.axis_size("seq")
    sequences, span_len, width = block_input.shape
    if seq_count != 16 or w_gate.shape[0] % 32:
        return gathered_shards(
            block_input, norm_gain, conv_weight, conv_bias, recur_weight, recur_bias, input_weight, input_bias,
            decay_param, mlp_gain, w_gate, w_up, w_down, out_grad,
        )
    rows = sequences * span_len
    stream = block_input.reshape(rows, width)
    cotangent = out_grad.reshape(rows, width)
    block_output, input_grad, weight_grads, vectors, matrices = block_pass(
        seq_count, sequences, stream, cotangent, norm_gain, conv_weight, conv_bias, recur_weight, recur_bias,
        input_weight, input_bias, decay_param, mlp_gain, w_gate, w_up, w_down,
    )
    matrices = matrices.astype(jnp.float32).reshape(2, *recur_weight.shape)
    gains = lax.all_gather(jnp.stack([vectors[0], vectors[9]]), "head", axis=1, tiled=True)
    return (
        block_output.reshape(block_input.shape),
        input_grad.reshape(block_input.shape),
        gains[0],
        vectors[1:5],
        vectors[5],
        matrices[0],
        vectors[6],
        matrices[1],
        vectors[7],
        vectors[8],
        gains[1],
        weight_grads[0].astype(jnp.float32),
        weight_grads[1].astype(jnp.float32),
        weight_grads[2].astype(jnp.float32),
    )


def solution(mesh):
    placed = (
        P(None, "seq", None),
        P(),
        P(None, "head"),
        P("head"),
        P("head", None, None),
        P("head"),
        P("head", None, None),
        P("head"),
        P("head"),
        P(),
        P("seq", "head"),
        P("seq", "head"),
        P("seq", "head"),
        P(None, "seq", None),
    )
    return jax.shard_map(
        shards,
        mesh=mesh,
        in_specs=placed,
        out_specs=(
            P(None, "seq", None),
            P(None, "seq", None),
            P(),
            P(None, "head"),
            P("head"),
            P("head", None, None),
            P("head"),
            P("head", None, None),
            P("head"),
            P("head"),
            P(),
            P("seq", "head"),
            P("seq", "head"),
            P("seq", "head"),
        ),
        check_vma=False,
    )
```
